32 devices in a mesh: group: 1, chan: 32 (over z, y, x, core).
Axes of the slice: x: 2, y: 2, z: 4, core: 2. Of those that a mesh axis runs over, the one named last changes fastest.
Arguments:
- records: bfloat16 [8, 128, 16384], P('group', None, 'chan'), may hold values from -6 to 6
- valid_flags: int32 [8, 128], P('group', 'chan'), may hold values 0 or 1
- source_ids: int32 [64], P('group'), may hold values from 0 to 127, as said below
Outputs:
- correlations: float32 [64, 128, 1001], P('group', 'chan')
The draws below stay inside these ranges and needn't reach their ends.
Inputs may be any that keep to these rules, and one draw needn't show every extreme that they name: `source_ids`: 64 distinct channel indices.
All inputs are finite; a program needn't handle non-finite values. No bound on the sum of `valid_flags` on one device may be relied on, other than what follows from the above.
Results may differ from the reference program's by a relative error of at most 0.00035.
The reference program's roundings to bfloat16 on the way count: a program that leaves them out, or rounds other values in their place, can miss the bound.
Values may be sent and summed in bfloat16 or wider, within the bound.
No kernel may reach another device: no remote copies, remote signals or barrier semaphores. Data moves between devices by JAX's collectives and lax.ppermute only.
A program may use at most 64 MiB of HBM per device.

```python
import math
import jax
import jax.numpy as jnp
from jax import lax

SEGS = 8
WINDOW_TICKS = 16384
BAND = 600
SOURCES = 64
HALF_LAG = 500
CHANNELS = 128


noise_scale = 0.3


envelope_scale = 1.4


def draw_source_ids(key, part):
    inner = jax.random.permutation(key, CHANNELS - 2)[:SOURCES - 2].astype(jnp.int32) + 1
    ends = jnp.array([0, CHANNELS - 1], dtype=jnp.int32)
    joined = jnp.concatenate([ends, inner])
    order = jax.random.permutation(jax.random.fold_in(key, 7), SOURCES)
    return joined[order].astype(jnp.int32)


def segment_records(seg_key):
    cable_locations = jnp.arange(WINDOW_TICKS, dtype=jnp.int32)
    noise_key = jax.random.fold_in(seg_key, 1)
    coarse_key = jax.random.fold_in(seg_key, 2)
    phase_key = jax.random.fold_in(seg_key, 3)
    sensor_interval = 8 + 3 * BAND // 4
    sinusoid_tones = []
    for partition_quotient in (2, 4, 8):
        sinusoid_tones.append(WINDOW_TICKS // partition_quotient - sensor_interval)
        sinusoid_tones.append(WINDOW_TICKS // partition_quotient + sensor_interval)
    sensor_total = len(sinusoid_tones)
    background = jax.random.normal(noise_key, (CHANNELS, WINDOW_TICKS), jnp.float32) * noise_scale
    coarse = jax.random.normal(coarse_key, (sensor_total, CHANNELS, BAND + 1), jnp.float32) * envelope_scale
    record_gain = jnp.ones((CHANNELS, 1), jnp.float32)
    phases = jax.random.uniform(phase_key, (sensor_total, CHANNELS), jnp.float32, -math.pi, math.pi)
    scaled = cable_locations * BAND
    lower_index = (scaled // WINDOW_TICKS).astype(jnp.int32)
    upper_index = (lower_index + 1).astype(jnp.int32)
    fraction = (scaled % WINDOW_TICKS).astype(jnp.float32) / WINDOW_TICKS
    combined = background
    for element_ordinal in range(sensor_total):
        lower_value = jnp.take(coarse[element_ordinal], lower_index, axis=1)
        upper_value = jnp.take(coarse[element_ordinal], upper_index, axis=1)
        envelope = lower_value + (upper_value - lower_value) * fraction[None, :]
        cycle_revolutions = (cable_locations * sinusoid_tones[element_ordinal] % WINDOW_TICKS).astype(jnp.float32) * (2.0 * math.pi / WINDOW_TICKS)
        combined = combined + envelope * jnp.cos(cycle_revolutions[None, :] + phases[element_ordinal][:, None])
    return combined * record_gain


def draw_records(key, part):
    alive = (jax.random.randint(jax.random.fold_in(key, 11), (SEGS, CHANNELS), 0, 4) != 0).astype(jnp.float32)
    seg_keys = jax.random.split(jax.random.fold_in(key, 13), SEGS)
    whole = lax.map(segment_records, seg_keys)
    clipped = jnp.clip(whole, -6.0, 6.0) * alive[:, :, None]
    return clipped.astype(jnp.bfloat16)


def set_ends(drawn, rng, smallest, top_value):
    longest = drawn.shape.index(max(drawn.shape))
    spots = []
    for shift in (0, 1):
        where = [jax.random.randint(jax.random.fold_in(rng, axis), (), 0, length) for axis, length in enumerate(drawn.shape)]
        where[longest] = (where[longest] + shift) % drawn.shape[longest]
        spots.append(tuple(where))
    return drawn.at[spots[0]].set(smallest).at[spots[1]].set(top_value)


def setup_inputs(seed: int = 0, part: int = 0) -> dict:
    keys = jax.random.split(jax.random.key(seed), 4)
    part_splits = jax.random.split(jax.random.fold_in(keys[3], part), 4)
    records = draw_records(jax.random.fold_in(jax.random.fold_in(keys[3], part), 71), part)
    valid_flags = set_ends((jax.random.randint(part_splits[1], (SEGS, CHANNELS), 0, 4) < 3).astype(jnp.int32), jax.random.fold_in(part_splits[1], 1), 0, 1)
    source_ids = draw_source_ids(jax.random.fold_in(jax.random.fold_in(keys[3], part), 71), part)
    return dict(records=records, valid_flags=valid_flags, source_ids=source_ids)


lowest_bin = 8
floor_share = 0.05
epsilon = 1e-06

def forward_table(offset, length, samples):
    position = offset + jnp.arange(length, dtype=jnp.int32)
    bins = lowest_bin + jnp.arange(BAND, dtype=jnp.int32)
    phase = position[:, None] * bins[None, :] % samples
    angle = phase.astype(jnp.float32) * (2.0 * math.pi / samples)
    return jnp.concatenate([jnp.cos(angle), -jnp.sin(angle)], axis=1).astype(jnp.bfloat16)

def inverse_table(samples):
    shifts = jnp.arange(2 * HALF_LAG + 1, dtype=jnp.int32) - HALF_LAG
    bins = lowest_bin + jnp.arange(BAND, dtype=jnp.int32)
    phase = bins[:, None] * shifts[None, :] % samples
    angle = phase.astype(jnp.float32) * (2.0 * math.pi / samples)
    factor = 1.0 / math.sqrt(BAND)
    return (jnp.concatenate([jnp.cos(angle), -jnp.sin(angle)], axis=0) * factor).astype(jnp.bfloat16)

def whiten(spectra):
    real_part = spectra[..., :BAND]
    imag_part = spectra[..., BAND:]
    power = real_part * real_part + imag_part * imag_part
    level = lax.optimization_barrier(jnp.mean(power, axis=-1, keepdims=True))
    factor = lax.rsqrt(power + floor_share * level + epsilon)
    return jnp.concatenate([real_part * factor, imag_part * factor], axis=-1).astype(jnp.bfloat16)

def cross_stack(panel, source_weights, receivers, weights):
    highest = lax.Precision.HIGHEST
    src_real = panel[..., :BAND]
    src_imag = panel[..., BAND:]
    rec_real = receivers[..., :BAND]
    rec_imag = receivers[..., BAND:]
    cross_real = jnp.einsum('gsf,gcf->scf', src_real, rec_real, precision=highest) + jnp.einsum('gsf,gcf->scf', src_imag, rec_imag, precision=highest)
    cross_imag = jnp.einsum('gsf,gcf->scf', src_imag, rec_real, precision=highest) - jnp.einsum('gsf,gcf->scf', src_real, rec_imag, precision=highest)
    counts = jnp.einsum('gs,gc->sc', source_weights, weights, precision=highest)
    divisor = jnp.maximum(counts, 1.0)[:, :, None]
    return (jnp.concatenate([cross_real, cross_imag], axis=-1) / divisor).astype(jnp.bfloat16)

def reference(records, valid_flags, source_ids):
    samples = records.shape[2]
    table = forward_table(0, samples, samples)
    spectra = lax.map(lambda segment: jnp.dot(segment, table, preferred_element_type=jnp.float32), records)
    white = whiten(spectra)
    weights = valid_flags.astype(jnp.float32)
    receivers = white.astype(jnp.float32) * weights[:, :, None]
    panel = receivers[:, source_ids, :]
    source_weights = weights[:, source_ids]
    stacked = cross_stack(panel, source_weights, receivers, weights)
    result = jnp.dot(stacked.reshape(-1, 2 * BAND), inverse_table(samples), preferred_element_type=jnp.float32)
    return result.reshape(SOURCES, -1, 2 * HALF_LAG + 1)
```

```python
import functools
import math

import jax
import jax.numpy as jnp
import ml_dtypes
import numpy as np
from jax import lax
from jax.experimental import pallas as pl
from jax.experimental.pallas import tpu as pltpu
from jax.sharding import PartitionSpec as P

BAND = 600
SOURCES = 64
HALF_LAG = 500

lowest_bin = 8
floor_share = 0.05
epsilon = 1e-06

PART = 640
WIDTH = 2 * PART
LAGS = 2 * HALF_LAG + 1
FLAG_TILE = BAND // 128 * 128
FLAG_LANE = BAND - FLAG_TILE


def angles(phase, samples):
    step = np.float32(2.0 * math.pi / samples)
    return (phase.astype(np.float32) * step).astype(np.float64)


def cos_sin(samples):
    angle = angles(np.arange(samples), samples)
    return np.cos(angle).astype(np.float32), (-np.sin(angle)).astype(np.float32)


def lane_tiles(table):
    tiled = table.reshape(*table.shape[:-1], -1, 128)
    return np.ascontiguousarray(np.moveaxis(tiled, -2, -3))


@functools.lru_cache(maxsize=None)
def forward_table(samples):
    cosine, sine = (part.astype(ml_dtypes.bfloat16) for part in cos_sin(samples))
    bins = lowest_bin + np.arange(BAND)
    phase = np.arange(samples)[:, None] * bins[None, :] % samples
    table = np.zeros((samples, WIDTH), ml_dtypes.bfloat16)
    table[:, :BAND] = cosine[phase]
    table[:, PART : PART + BAND] = sine[phase]
    return lane_tiles(table.reshape(2, samples // 2, WIDTH))


@functools.lru_cache(maxsize=None)
def inverse_table(samples):
    factor = np.float32(1.0 / math.sqrt(BAND))
    cosine, sine = ((part * factor).astype(ml_dtypes.bfloat16) for part in cos_sin(samples))
    bins = lowest_bin + np.arange(BAND)
    shifts = np.arange(LAGS) - HALF_LAG
    phase = bins[:, None] * shifts[None, :] % samples
    table = np.zeros((WIDTH, -(-LAGS // 128) * 128), ml_dtypes.bfloat16)
    table[:BAND, :LAGS] = cosine[phase]
    table[PART : PART + BAND, :LAGS] = sine[phase]
    return lane_tiles(table)


def transform_kernel(half_ref, records_ref, table_ref, own_ref, other_ref, total_ref):
    step = pl.program_id(0)
    pieces, _, span = records_ref.shape

    @pl.when(step == 0)
    def _():
        total_ref[...] = jnp.zeros_like(total_ref)

    total = total_ref[...]
    for piece in range(pieces):
        rows = slice(piece * span, (piece + 1) * span)
        tiles = [table_ref[0, tile, rows, :] for tile in range(WIDTH // 128)]
        total += jnp.dot(
            records_ref[piece],
            jnp.concatenate(tiles, axis=1),
            preferred_element_type=jnp.float32,
        )
    total_ref[...] = total

    @pl.when(step == pl.num_programs(0) - 1)
    def _():
        rows = own_ref.shape[0]
        first = half_ref[0] == 0
        low, high = total_ref[:rows], total_ref[rows:]
        own_ref[...] = jnp.where(first, low, high)
        other_ref[...] = jnp.where(first, high, low)


def transform(half, records, table):
    senders, rows, span = records.shape
    depth = table.shape[2]
    block = max(span, min(1024, depth))
    pieces = block // span
    spec = pl.BlockSpec((rows // 2, WIDTH), lambda k, half: (0, 0))
    shape = jax.ShapeDtypeStruct((rows // 2, WIDTH), jnp.float32)
    return pl.pallas_call(
        transform_kernel,
        grid_spec=pltpu.PrefetchScalarGridSpec(
            num_scalar_prefetch=1,
            grid=(depth // block,),
            in_specs=[
                pl.BlockSpec((pieces, rows, span), lambda k, half: (k, 0, 0)),
                pl.BlockSpec((1, WIDTH // 128, block, 128), lambda k, half: (half[0], 0, k, 0)),
            ],
            out_specs=[spec, spec],
            scratch_shapes=[pltpu.VMEM((rows, WIDTH), jnp.float32)],
        ),
        out_shape=[shape, shape],
        compiler_params=pltpu.CompilerParams(vmem_limit_bytes=24 * 2**20),
        cost_estimate=pl.CostEstimate(
            flops=2 * rows * depth * WIDTH,
            bytes_accessed=2 * depth * WIDTH,
            transcendentals=0,
        ),
        name="transform",
    )(half, records, table)


def whiten_kernel(own_ref, received_ref, flags_ref, white_ref):
    real_part = own_ref[:, :PART] + received_ref[:, :PART]
    imag_part = own_ref[:, PART:] + received_ref[:, PART:]
    power = real_part * real_part + imag_part * imag_part
    level = jnp.sum(power, axis=1, keepdims=True) * (1.0 / BAND)
    factor = lax.rsqrt(power + floor_share * level + epsilon)
    white_ref[:, :PART] = (real_part * factor).astype(jnp.bfloat16)
    white_ref[:, PART:] = (imag_part * factor).astype(jnp.bfloat16)
    rows = own_ref.shape[0]
    lane = lax.broadcasted_iota(jnp.int32, (rows, 128), 1)
    held = (lane >= FLAG_LANE) & (lane < FLAG_LANE + flags_ref.shape[1])
    tile = (real_part * factor)[:, FLAG_TILE : FLAG_TILE + 128]
    flags = jnp.concatenate(
        [
            jnp.zeros((1, FLAG_LANE), jnp.float32),
            flags_ref[...],
            jnp.zeros((1, 128 - FLAG_LANE - flags_ref.shape[1]), jnp.float32),
        ],
        axis=1,
    )
    white_ref[:, FLAG_TILE : FLAG_TILE + 128] = jnp.where(held, flags, tile).astype(jnp.bfloat16)


def whiten(own, received, flags):
    return pl.pallas_call(
        whiten_kernel,
        out_shape=jax.ShapeDtypeStruct(own.shape, jnp.bfloat16),
        compiler_params=pltpu.CompilerParams(vmem_limit_bytes=16 * 2**20),
        name="whiten",
    )(own, received, flags)


def correlate_kernel(segments, channels, place_ref, flags_ref, ids_ref, inverse_ref, *rest):
    blocks, (out_ref, held_ref, panel_ref, receivers_ref, stacked_ref, sems) = rest[:-6], rest[-6:]
    far, near = held_ref.shape[0], held_ref.shape[1]
    rows = held_ref.shape[3]
    copies = []
    for index, block in enumerate(blocks):
        copies.append(
            pltpu.make_async_copy(block, held_ref.at[:, index // 2, index % 2], sems.at[index])
        )
        copies[-1].start()
    devices = far * near * 2
    half = devices // 2
    ch_local = channels // devices
    place = place_ref[0]
    ids = ids_ref[...]
    sources = ids.shape[0]
    for copy in copies:
        copy.wait()

    tails = held_ref[:, :, :, :, FLAG_TILE : FLAG_TILE + 128].reshape(devices * rows, 128)
    column = lax.broadcasted_iota(jnp.int32, (sources, devices * rows), 1)
    choice = (column == ((ids // ch_local) ^ place) * rows).astype(jnp.bfloat16)
    tail = jnp.dot(choice, tails, preferred_element_type=jnp.float32)
    lane = lax.broadcasted_iota(jnp.int32, (sources, 128), 1)

    channel = lax.broadcasted_iota(jnp.int32, (sources, channels), 1)
    pick_sources = (channel == ids).astype(jnp.bfloat16)
    line = lax.broadcasted_iota(jnp.int32, (16, channels), 0)
    channel = lax.broadcasted_iota(jnp.int32, (16, channels), 1)
    pick_own = ((channel == place * ch_local + line) & (line < ch_local)).astype(jnp.bfloat16)
    pick = jnp.concatenate([pick_sources, pick_own], axis=0)

    counts = [jnp.zeros((sources, 1), jnp.float32) for _ in range(ch_local)]
    for g in range(segments):
        parts = []
        for first in range(0, channels, rows):
            block = (g * channels + first) // rows
            index = place ^ (block % 2 * half + block // 2)
            parts.append(held_ref[index // (2 * near), index // 2 % near, index % 2])
        segment = jnp.concatenate(parts, axis=0)
        picked = jnp.dot(pick, segment, preferred_element_type=jnp.float32)
        mine = lane == FLAG_LANE + g * ch_local + ids % ch_local
        weight = jnp.sum(jnp.where(mine, tail, 0.0), axis=1, keepdims=True)
        panel_ref[g] = picked[:sources] * weight
        receivers_ref[g] = picked[sources:]
        for c in range(ch_local):
            counts[c] += weight * flags_ref[g, c]

    inverse = jnp.concatenate([inverse_ref[tile] for tile in range(inverse_ref.shape[0])], axis=1)
    for c in range(ch_local):
        share = 1.0 / jnp.maximum(counts[c], 1.0)
        for start in range(0, PART, 128):
            re = slice(start, start + 128)
            im = slice(PART + start, PART + start + 128)
            real_sum = jnp.zeros((sources, 128), jnp.float32)
            imag_sum = jnp.zeros((sources, 128), jnp.float32)
            for g in range(segments):
                rec_real = receivers_ref[g, c : c + 1, re] * flags_ref[g, c]
                rec_imag = receivers_ref[g, c : c + 1, im] * flags_ref[g, c]
                src_real, src_imag = panel_ref[g, :, re], panel_ref[g, :, im]
                real_sum += src_real * rec_real + src_imag * rec_imag
                imag_sum += src_imag * rec_real - src_real * rec_imag
            stacked_ref[:, re] = (real_sum * share).astype(jnp.bfloat16)
            stacked_ref[:, im] = (imag_sum * share).astype(jnp.bfloat16)
        lags = jnp.dot(stacked_ref[...], inverse, preferred_element_type=jnp.float32)
        out_ref[:, c, :] = lags[:, :LAGS]


def correlate(place, weights, source_ids, inverse, blocks, segments, channels):
    far, rows, _ = blocks[0].shape
    near = len(blocks) // 2
    devices = far * near * 2
    ch_local = channels // devices
    sources = source_ids.shape[0]
    smem = pl.BlockSpec(memory_space=pltpu.SMEM)
    vmem = pl.BlockSpec(memory_space=pltpu.VMEM)
    anywhere = pl.BlockSpec(memory_space=pl.ANY)
    return pl.pallas_call(
        functools.partial(correlate_kernel, segments, channels),
        in_specs=[smem, smem, vmem, vmem] + [anywhere] * len(blocks),
        out_specs=vmem,
        out_shape=jax.ShapeDtypeStruct((sources, ch_local, LAGS), jnp.float32),
        scratch_shapes=[
            pltpu.VMEM((far, near, 2, rows, WIDTH), jnp.bfloat16),
            pltpu.VMEM((segments, sources, WIDTH), jnp.float32),
            pltpu.VMEM((segments, 16, WIDTH), jnp.float32),
            pltpu.VMEM((sources, WIDTH), jnp.bfloat16),
            pltpu.SemaphoreType.DMA((len(blocks),)),
        ],
        compiler_params=pltpu.CompilerParams(vmem_limit_bytes=40 * 2**20),
        name="correlate",
    )(place, weights, source_ids.reshape(sources, 1), inverse, *blocks)


def per_device(records, valid_flags, source_ids):
    segments, channels, span = records.shape
    devices = lax.axis_size("chan")
    half = devices // 2
    samples = span * devices
    place = lax.axis_index("chan")
    weights = valid_flags.astype(jnp.float32)

    grouped = records.reshape(half, segments * channels // half, span)
    groups = [list(range(half)), list(range(half, devices))]
    regrouped = lax.all_to_all(
        grouped, "chan", split_axis=0, concat_axis=0, axis_index_groups=groups, tiled=True
    )
    own, other = transform((place // half).reshape(1), regrouped, forward_table(samples))

    def exchange(block, bit):
        return lax.ppermute(block, "chan", [(i, i ^ bit) for i in range(devices)])

    white = whiten(own, exchange(other, half), weights.reshape(1, -1))

    far = devices // 8
    line = jnp.stack([white] + [exchange(white, 8 * k) for k in range(1, far)])
    plane = [line] + [exchange(line, 2 * k) for k in range(1, 4)]
    blocks = [b for block in plane for b in (block, exchange(block, 1))]
    return correlate(
        place.reshape(1), weights, source_ids, inverse_table(samples), blocks, segments, channels
    )


def solution(mesh):
    return jax.shard_map(
        per_device,
        mesh=mesh,
        in_specs=(P("group", None, "chan"), P("group", "chan"), P("group")),
        out_specs=P("group", "chan", None),
        check_vma=False,
    )
```

```python
import functools
import math

import jax
import jax.numpy as jnp
import ml_dtypes
import numpy as np
from jax import lax
from jax.experimental import pallas as pl
from jax.experimental.pallas import tpu as pltpu
from jax.sharding import PartitionSpec as P

BAND = 600
SOURCES = 64
HALF_LAG = 500

lowest_bin = 8
floor_share = 0.05
epsilon = 1e-06

PART = 640
WIDTH = 2 * PART
LAGS = 2 * HALF_LAG + 1
SHARES = 4
BATCHES = 4
FLAG_TILE = BAND // 128 * 128
FLAG_LANE = BAND - FLAG_TILE


def angles(phase, samples):
    step = np.float32(2.0 * math.pi / samples)
    return (phase.astype(np.float32) * step).astype(np.float64)


def cos_sin(samples):
    angle = angles(np.arange(samples), samples)
    return np.cos(angle).astype(np.float32), (-np.sin(angle)).astype(np.float32)


def lane_tiles(table):
    tiled = table.reshape(*table.shape[:-1], -1, 128)
    return np.ascontiguousarray(np.moveaxis(tiled, -2, -3))


@functools.lru_cache(maxsize=None)
def forward_table(samples):
    cosine, sine = (part.astype(ml_dtypes.bfloat16) for part in cos_sin(samples))
    bins = lowest_bin + np.arange(BAND)
    phase = np.arange(samples)[:, None] * bins[None, :] % samples
    table = np.zeros((samples, WIDTH), ml_dtypes.bfloat16)
    table[:, :BAND] = cosine[phase]
    table[:, PART : PART + BAND] = sine[phase]
    return lane_tiles(table)


@functools.lru_cache(maxsize=None)
def inverse_table(samples):
    factor = np.float32(1.0 / math.sqrt(BAND))
    cosine, sine = ((part * factor).astype(ml_dtypes.bfloat16) for part in cos_sin(samples))
    bins = lowest_bin + np.arange(BAND)
    shifts = np.arange(LAGS) - HALF_LAG
    phase = bins[:, None] * shifts[None, :] % samples
    table = np.zeros((WIDTH, -(-LAGS // 128) * 128), ml_dtypes.bfloat16)
    table[:BAND, :LAGS] = cosine[phase]
    table[PART : PART + BAND, :LAGS] = sine[phase]
    return lane_tiles(table)


def spread_kernel(place_ref, records_ref, *rest):
    outs, sems = rest[:-1], rest[-1]
    copies = [
        pltpu.make_async_copy(records_ref.at[place_ref[0] ^ step], out, sems.at[step])
        for step, out in enumerate(outs)
    ]
    for copy in copies:
        copy.start()
    for copy in copies:
        copy.wait()


def spread(member, grouped):
    members, rows, span = grouped.shape
    return pl.pallas_call(
        spread_kernel,
        in_specs=[
            pl.BlockSpec(memory_space=pltpu.SMEM),
            pl.BlockSpec(memory_space=pltpu.HBM),
        ],
        out_specs=[pl.BlockSpec(memory_space=pltpu.VMEM)] * members,
        out_shape=[jax.ShapeDtypeStruct((rows, span), jnp.bfloat16)] * members,
        scratch_shapes=[pltpu.SemaphoreType.DMA((members,))],
        compiler_params=pltpu.CompilerParams(vmem_limit_bytes=16 * 2**20),
        name="spread",
    )(member.reshape(1), grouped)


def transform_kernel(count, started, order_ref, table_ref, *rest):
    records, rest = rest[:count], rest[count:]
    if started:
        before_ref, rest = rest[0], rest[1:]
    outs, (tiles_ref, sems) = rest[:-2], rest[-2:]
    span = records[0].shape[1]
    copies = []
    for index in range(count):
        rows = pl.ds(pl.multiple_of(order_ref[index] * span, span), span)
        copies.append(
            pltpu.make_async_copy(table_ref.at[:, rows, :], tiles_ref.at[index], sems.at[index])
        )
        copies[-1].start()
    total = before_ref[...] if started else None
    for index in range(count):
        copies[index].wait()
        tiles = [tiles_ref[index, tile] for tile in range(WIDTH // 128)]
        product = jnp.dot(
            records[index][...],
            jnp.concatenate(tiles, axis=1),
            preferred_element_type=jnp.float32,
        )
        total = product if total is None else total + product
    if len(outs) == 1:
        outs[0][...] = total
    else:
        rows = outs[0].shape[0]
        first = order_ref[count]
        for step, out in enumerate(outs):
            chosen = total[:rows]
            for owner in range(1, len(outs)):
                mine = (first ^ step) == owner
                chosen = jnp.where(mine, total[owner * rows : (owner + 1) * rows], chosen)
            out[...] = chosen


def transform(order, table, records, before, owners):
    count = len(records)
    rows, span = records[0].shape
    vmem = pl.BlockSpec(memory_space=pltpu.VMEM)
    shape = jax.ShapeDtypeStruct((rows // owners, WIDTH), jnp.float32)
    started = before is not None
    return pl.pallas_call(
        functools.partial(transform_kernel, count, started),
        in_specs=[
            pl.BlockSpec(memory_space=pltpu.SMEM),
            pl.BlockSpec(memory_space=pltpu.HBM),
        ]
        + [vmem] * (count + started),
        out_specs=[vmem] * owners,
        out_shape=[shape] * owners,
        scratch_shapes=[
            pltpu.VMEM((count, WIDTH // 128, span, 128), jnp.bfloat16),
            pltpu.SemaphoreType.DMA((count,)),
        ],
        compiler_params=pltpu.CompilerParams(vmem_limit_bytes=24 * 2**20),
        cost_estimate=pl.CostEstimate(
            flops=2 * rows * count * span * WIDTH,
            bytes_accessed=2 * count * span * WIDTH,
            transcendentals=0,
        ),
        name="transform",
    )(order, table, *records, *([before] if started else []))


def whiten_kernel(flags_ref, *rest):
    parts, white_ref = rest[:-1], rest[-1]
    total = parts[0][...]
    for part in parts[1:]:
        total += part[...]
    real_part, imag_part = total[:, :PART], total[:, PART:]
    power = real_part * real_part + imag_part * imag_part
    level = jnp.sum(power, axis=1, keepdims=True) * (1.0 / BAND)
    factor = lax.rsqrt(power + floor_share * level + epsilon)
    white_ref[:, :PART] = (real_part * factor).astype(jnp.bfloat16)
    white_ref[:, PART:] = (imag_part * factor).astype(jnp.bfloat16)
    rows = total.shape[0]
    lane = lax.broadcasted_iota(jnp.int32, (rows, 128), 1)
    held = (lane >= FLAG_LANE) & (lane < FLAG_LANE + flags_ref.shape[1])
    tile = (real_part * factor)[:, FLAG_TILE : FLAG_TILE + 128]
    flags = jnp.concatenate(
        [
            jnp.zeros((1, FLAG_LANE), jnp.float32),
            flags_ref[...],
            jnp.zeros((1, 128 - FLAG_LANE - flags_ref.shape[1]), jnp.float32),
        ],
        axis=1,
    )
    white_ref[:, FLAG_TILE : FLAG_TILE + 128] = jnp.where(held, flags, tile).astype(jnp.bfloat16)


def whiten(flags, parts):
    return pl.pallas_call(
        whiten_kernel,
        out_shape=jax.ShapeDtypeStruct(parts[0].shape, jnp.bfloat16),
        compiler_params=pltpu.CompilerParams(vmem_limit_bytes=16 * 2**20),
        name="whiten",
    )(flags, *parts)


def correlate_kernel(segments, channels, shares, place_ref, flags_ref, ids_ref, table_ref, *rest):
    blocks, rest = rest[:-7], rest[-7:]
    out_ref, held_ref, inverse_ref, panel_ref, receivers_ref, stacked_ref, sems = rest
    far, near = held_ref.shape[0], held_ref.shape[1]
    rows = held_ref.shape[3]
    copies = []
    for index, block in enumerate(blocks):
        copies.append(
            pltpu.make_async_copy(block, held_ref.at[:, index // 2, index % 2], sems.at[index])
        )
        copies[-1].start()
    fetch = pltpu.make_async_copy(table_ref, inverse_ref, sems.at[len(blocks)])
    fetch.start()
    devices = far * near * 2
    members = devices // shares
    ch_local = channels // devices
    place = place_ref[0]
    ids = ids_ref[...]
    sources = ids.shape[0]
    for copy in copies:
        copy.wait()

    tails = held_ref[:, :, :, :, FLAG_TILE : FLAG_TILE + 128].reshape(devices * rows, 128)
    column = lax.broadcasted_iota(jnp.int32, (sources, devices * rows), 1)
    choice = (column == ((ids // ch_local) ^ place) * rows).astype(jnp.bfloat16)
    tail = jnp.dot(choice, tails, preferred_element_type=jnp.float32)
    lane = lax.broadcasted_iota(jnp.int32, (sources, 128), 1)

    channel = lax.broadcasted_iota(jnp.int32, (sources, channels), 1)
    pick_sources = (channel == ids).astype(jnp.bfloat16)
    line = lax.broadcasted_iota(jnp.int32, (16, channels), 0)
    channel = lax.broadcasted_iota(jnp.int32, (16, channels), 1)
    pick_own = ((channel == place * ch_local + line) & (line < ch_local)).astype(jnp.bfloat16)
    pick = jnp.concatenate([pick_sources, pick_own], axis=0)

    counts = [jnp.zeros((sources, 1), jnp.float32) for _ in range(ch_local)]
    for g in range(segments):
        parts = []
        for first in range(0, channels, rows):
            block = (g * channels + first) // rows
            index = place ^ (block % shares * members + block // shares)
            parts.append(held_ref[index // (2 * near), index // 2 % near, index % 2])
        segment = jnp.concatenate(parts, axis=0)
        picked = jnp.dot(pick, segment, preferred_element_type=jnp.float32)
        mine = lane == FLAG_LANE + g * ch_local + ids % ch_local
        weight = jnp.sum(jnp.where(mine, tail, 0.0), axis=1, keepdims=True)
        panel_ref[g] = picked[:sources] * weight
        receivers_ref[g] = picked[sources:]
        for c in range(ch_local):
            counts[c] += weight * flags_ref[g, c]

    fetch.wait()
    inverse = jnp.concatenate([inverse_ref[tile] for tile in range(inverse_ref.shape[0])], axis=1)
    for c in range(ch_local):
        share = 1.0 / jnp.maximum(counts[c], 1.0)
        for start in range(0, PART, 128):
            re = slice(start, start + 128)
            im = slice(PART + start, PART + start + 128)
            real_sum = jnp.zeros((sources, 128), jnp.float32)
            imag_sum = jnp.zeros((sources, 128), jnp.float32)
            for g in range(segments):
                rec_real = receivers_ref[g, c : c + 1, re] * flags_ref[g, c]
                rec_imag = receivers_ref[g, c : c + 1, im] * flags_ref[g, c]
                src_real, src_imag = panel_ref[g, :, re], panel_ref[g, :, im]
                real_sum += src_real * rec_real + src_imag * rec_imag
                imag_sum += src_imag * rec_real - src_real * rec_imag
            stacked_ref[:, re] = (real_sum * share).astype(jnp.bfloat16)
            stacked_ref[:, im] = (imag_sum * share).astype(jnp.bfloat16)
        lags = jnp.dot(stacked_ref[...], inverse, preferred_element_type=jnp.float32)
        out_ref[:, c, :] = lags[:, :LAGS]


def correlate(place, weights, source_ids, inverse, blocks, segments, channels, shares):
    far, rows, _ = blocks[0].shape
    near = len(blocks) // 2
    devices = far * near * 2
    ch_local = channels // devices
    sources = source_ids.shape[0]
    smem = pl.BlockSpec(memory_space=pltpu.SMEM)
    vmem = pl.BlockSpec(memory_space=pltpu.VMEM)
    anywhere = pl.BlockSpec(memory_space=pl.ANY)
    return pl.pallas_call(
        functools.partial(correlate_kernel, segments, channels, shares),
        in_specs=[smem, smem, vmem, pl.BlockSpec(memory_space=pltpu.HBM)] + [anywhere] * len(blocks),
        out_specs=vmem,
        out_shape=jax.ShapeDtypeStruct((sources, ch_local, LAGS), jnp.float32),
        scratch_shapes=[
            pltpu.VMEM((far, near, 2, rows, WIDTH), jnp.bfloat16),
            pltpu.VMEM(inverse.shape, jnp.bfloat16),
            pltpu.VMEM((segments, sources, WIDTH), jnp.float32),
            pltpu.VMEM((segments, 16, WIDTH), jnp.float32),
            pltpu.VMEM((sources, WIDTH), jnp.bfloat16),
            pltpu.SemaphoreType.DMA((len(blocks) + 1,)),
        ],
        compiler_params=pltpu.CompilerParams(vmem_limit_bytes=40 * 2**20),
        name="correlate",
    )(place, weights, source_ids.reshape(sources, 1), inverse, *blocks)


def per_device(records, valid_flags, source_ids):
    segments, channels, span = records.shape
    devices = lax.axis_size("chan")
    members = devices // SHARES
    samples = span * devices
    place = lax.axis_index("chan")
    weights = valid_flags.astype(jnp.float32)

    def exchange(block, bits):
        return lax.ppermute(block, "chan", [(i, i ^ bits) for i in range(devices)])

    grouped = records.reshape(members, segments * channels // members, span)
    sent = spread(place % members, grouped)
    steps = sorted(range(members), key=lambda step: (step.bit_count(), step))
    arrived = {step: exchange(sent[step], step) if step else sent[0] for step in steps}
    table = forward_table(samples)
    parts = None
    batch = -(-members // BATCHES)
    for first in range(0, members, batch):
        now = steps[first : first + batch]
        order = jnp.stack([place ^ step for step in now] + [place // members])
        last = first + batch >= members
        parts = transform(
            order,
            table,
            [arrived[step] for step in now],
            parts[0] if parts else None,
            SHARES if last else 1,
        )
    received = [exchange(parts[k], k * members) for k in range(1, SHARES)]
    white = whiten(weights.reshape(1, -1), [parts[0]] + received)

    far = devices // 8
    line = jnp.stack([white] + [exchange(white, 8 * k) for k in range(1, far)])
    plane = [line] + [exchange(line, 2 * k) for k in range(1, 4)]
    blocks = [b for block in plane for b in (block, exchange(block, 1))]
    return correlate(
        place.reshape(1),
        weights,
        source_ids,
        inverse_table(samples),
        blocks,
        segments,
        channels,
        SHARES,
    )


def solution(mesh):
    return jax.shard_map(
        per_device,
        mesh=mesh,
        in_specs=(P("group", None, "chan"), P("group", "chan"), P("group")),
        out_specs=P("group", "chan", None),
        check_vma=False,
    )
```

```python
import functools
import math

import jax
import jax.numpy as jnp
import ml_dtypes
import numpy as np
from jax import lax
from jax.experimental import pallas as pl
from jax.experimental.pallas import tpu as pltpu
from jax.sharding import PartitionSpec as P

BAND = 600
SOURCES = 64
HALF_LAG = 500

lowest_bin = 8
floor_share = 0.05
epsilon = 1e-06

PART = 640
WIDTH = 2 * PART
LAGS = 2 * HALF_LAG + 1
SHARES = 2
FLAG_TILE = BAND // 128 * 128
FLAG_LANE = BAND - FLAG_TILE


def angles(phase, samples):
    step = np.float32(2.0 * math.pi / samples)
    return (phase.astype(np.float32) * step).astype(np.float64)


def cos_sin(samples):
    angle = angles(np.arange(samples), samples)
    return np.cos(angle).astype(np.float32), (-np.sin(angle)).astype(np.float32)


def lane_tiles(table):
    tiled = table.reshape(*table.shape[:-1], -1, 128)
    return np.ascontiguousarray(np.moveaxis(tiled, -2, -3))


@functools.lru_cache(maxsize=None)
def forward_table(samples):
    cosine, sine = (part.astype(ml_dtypes.bfloat16) for part in cos_sin(samples))
    bins = lowest_bin + np.arange(BAND)
    phase = np.arange(samples)[:, None] * bins[None, :] % samples
    table = np.zeros((samples, WIDTH), ml_dtypes.bfloat16)
    table[:, :BAND] = cosine[phase]
    table[:, PART : PART + BAND] = sine[phase]
    return lane_tiles(table.T)


@functools.lru_cache(maxsize=None)
def inverse_table(samples):
    factor = np.float32(1.0 / math.sqrt(BAND))
    cosine, sine = ((part * factor).astype(ml_dtypes.bfloat16) for part in cos_sin(samples))
    bins = lowest_bin + np.arange(BAND)
    shifts = np.arange(LAGS) - HALF_LAG
    phase = bins[:, None] * shifts[None, :] % samples
    table = np.zeros((WIDTH, -(-LAGS // 128) * 128), ml_dtypes.bfloat16)
    table[:BAND, :LAGS] = cosine[phase]
    table[PART : PART + BAND, :LAGS] = sine[phase]
    return lane_tiles(table)


def transform_kernel(half_ref, records_ref, table_ref, out_ref, total_ref):
    step = pl.program_id(0)

    @pl.when(step == 0)
    def _():
        total_ref[...] = jnp.zeros_like(total_ref)

    tiles = jnp.concatenate([table_ref[tile] for tile in range(table_ref.shape[0])], axis=1)
    records = jnp.concatenate([records_ref[i] for i in range(records_ref.shape[0])], axis=1)
    total_ref[...] += lax.dot_general(
        tiles, records, (((1,), (1,)), ((), ())), preferred_element_type=jnp.float32
    )

    @pl.when(step == pl.num_programs(0) - 1)
    def _():
        out_ref[...] = total_ref[...].T


def transform(half, records, table):
    senders, rows, span = records.shape
    depth = senders * span
    block = max(span, min(1024, depth))
    steps = depth // block
    return pl.pallas_call(
        transform_kernel,
        grid_spec=pltpu.PrefetchScalarGridSpec(
            num_scalar_prefetch=1,
            grid=(steps,),
            in_specs=[
                pl.BlockSpec((block // span, rows, span), lambda k, half: (k, 0, 0)),
                pl.BlockSpec((block // 128, WIDTH, 128), lambda k, half: (half[0] * steps + k, 0, 0)),
            ],
            out_specs=pl.BlockSpec((rows, WIDTH), lambda k, half: (0, 0)),
            scratch_shapes=[pltpu.VMEM((WIDTH, rows), jnp.float32)],
        ),
        out_shape=jax.ShapeDtypeStruct((rows, WIDTH), jnp.float32),
        compiler_params=pltpu.CompilerParams(vmem_limit_bytes=24 * 2**20),
        cost_estimate=pl.CostEstimate(
            flops=2 * rows * depth * WIDTH,
            bytes_accessed=2 * depth * WIDTH,
            transcendentals=0,
        ),
        name="transform",
    )(half, records, table)


def whiten_kernel(flags_ref, *rest):
    parts, white_ref = rest[:-1], rest[-1]
    total = parts[0][...]
    for part in parts[1:]:
        total += part[...]
    real_part, imag_part = total[:, :PART], total[:, PART:]
    power = real_part * real_part + imag_part * imag_part
    level = jnp.sum(power, axis=1, keepdims=True) * (1.0 / BAND)
    factor = lax.rsqrt(power + floor_share * level + epsilon)
    white_ref[:, :PART] = (real_part * factor).astype(jnp.bfloat16)
    white_ref[:, PART:] = (imag_part * factor).astype(jnp.bfloat16)
    rows = total.shape[0]
    lane = lax.broadcasted_iota(jnp.int32, (rows, 128), 1)
    held = (lane >= FLAG_LANE) & (lane < FLAG_LANE + flags_ref.shape[1])
    tile = (real_part * factor)[:, FLAG_TILE : FLAG_TILE + 128]
    flags = jnp.concatenate(
        [
            jnp.zeros((1, FLAG_LANE), jnp.float32),
            flags_ref[...],
            jnp.zeros((1, 128 - FLAG_LANE - flags_ref.shape[1]), jnp.float32),
        ],
        axis=1,
    )
    white_ref[:, FLAG_TILE : FLAG_TILE + 128] = jnp.where(held, flags, tile).astype(jnp.bfloat16)


def whiten(flags, parts):
    return pl.pallas_call(
        whiten_kernel,
        out_shape=jax.ShapeDtypeStruct(parts[0].shape, jnp.bfloat16),
        compiler_params=pltpu.CompilerParams(vmem_limit_bytes=16 * 2**20),
        name="whiten",
    )(flags, *parts)


def correlate_kernel(segments, channels, shares, place_ref, flags_ref, ids_ref, table_ref, *rest):
    blocks, rest = rest[:-7], rest[-7:]
    out_ref, held_ref, inverse_ref, panel_ref, receivers_ref, stacked_ref, sems = rest
    far, near = held_ref.shape[0], held_ref.shape[1]
    rows = held_ref.shape[3]
    copies = []
    for index, block in enumerate(blocks):
        copies.append(
            pltpu.make_async_copy(block, held_ref.at[:, index // 2, index % 2], sems.at[index])
        )
        copies[-1].start()
    fetch = pltpu.make_async_copy(table_ref, inverse_ref, sems.at[len(blocks)])
    fetch.start()
    devices = far * near * 2
    members = devices // shares
    ch_local = channels // devices
    place = place_ref[0]
    ids = ids_ref[...]
    sources = ids.shape[0]
    for copy in copies:
        copy.wait()

    tails = held_ref[:, :, :, :, FLAG_TILE : FLAG_TILE + 128].reshape(devices * rows, 128)
    column = lax.broadcasted_iota(jnp.int32, (sources, devices * rows), 1)
    choice = (column == ((ids // ch_local) ^ place) * rows).astype(jnp.bfloat16)
    tail = jnp.dot(choice, tails, preferred_element_type=jnp.float32)
    lane = lax.broadcasted_iota(jnp.int32, (sources, 128), 1)

    channel = lax.broadcasted_iota(jnp.int32, (sources, channels), 1)
    pick_sources = (channel == ids).astype(jnp.bfloat16)
    line = lax.broadcasted_iota(jnp.int32, (16, channels), 0)
    channel = lax.broadcasted_iota(jnp.int32, (16, channels), 1)
    pick_own = ((channel == place * ch_local + line) & (line < ch_local)).astype(jnp.bfloat16)
    pick = jnp.concatenate([pick_sources, pick_own], axis=0)

    counts = [jnp.zeros((sources, 1), jnp.float32) for _ in range(ch_local)]
    for g in range(segments):
        parts = []
        for first in range(0, channels, rows):
            block = (g * channels + first) // rows
            index = place ^ (block % shares * members + block // shares)
            parts.append(held_ref[index // (2 * near), index // 2 % near, index % 2])
        segment = jnp.concatenate(parts, axis=0)
        picked = jnp.dot(pick, segment, preferred_element_type=jnp.float32)
        mine = lane == FLAG_LANE + g * ch_local + ids % ch_local
        weight = jnp.sum(jnp.where(mine, tail, 0.0), axis=1, keepdims=True)
        panel_ref[g] = picked[:sources] * weight
        receivers_ref[g] = picked[sources:]
        for c in range(ch_local):
            counts[c] += weight * flags_ref[g, c]

    for c in range(ch_local):
        share = 1.0 / jnp.maximum(counts[c], 1.0)
        lines = slice(c * sources, (c + 1) * sources)
        for start in range(0, PART, 128):
            re = slice(start, start + 128)
            im = slice(PART + start, PART + start + 128)
            real_sum = jnp.zeros((sources, 128), jnp.float32)
            imag_sum = jnp.zeros((sources, 128), jnp.float32)
            for g in range(segments):
                rec_real = receivers_ref[g, c : c + 1, re] * flags_ref[g, c]
                rec_imag = receivers_ref[g, c : c + 1, im] * flags_ref[g, c]
                src_real, src_imag = panel_ref[g, :, re], panel_ref[g, :, im]
                real_sum += src_real * rec_real + src_imag * rec_imag
                imag_sum += src_imag * rec_real - src_real * rec_imag
            stacked_ref[lines, re] = (real_sum * share).astype(jnp.bfloat16)
            stacked_ref[lines, im] = (imag_sum * share).astype(jnp.bfloat16)
    fetch.wait()
    inverse = jnp.concatenate([inverse_ref[tile] for tile in range(inverse_ref.shape[0])], axis=1)
    lags = jnp.dot(stacked_ref[...], inverse, preferred_element_type=jnp.float32)
    for c in range(ch_local):
        out_ref[:, c, :] = lags[c * sources : (c + 1) * sources, :LAGS]


def correlate(place, weights, source_ids, inverse, blocks, segments, channels, shares):
    far, rows, _ = blocks[0].shape
    near = len(blocks) // 2
    devices = far * near * 2
    ch_local = channels // devices
    sources = source_ids.shape[0]
    smem = pl.BlockSpec(memory_space=pltpu.SMEM)
    vmem = pl.BlockSpec(memory_space=pltpu.VMEM)
    anywhere = pl.BlockSpec(memory_space=pl.ANY)
    return pl.pallas_call(
        functools.partial(correlate_kernel, segments, channels, shares),
        in_specs=[smem, smem, vmem, pl.BlockSpec(memory_space=pltpu.HBM)] + [anywhere] * len(blocks),
        out_specs=vmem,
        out_shape=jax.ShapeDtypeStruct((sources, ch_local, LAGS), jnp.float32),
        scratch_shapes=[
            pltpu.VMEM((far, near, 2, rows, WIDTH), jnp.bfloat16),
            pltpu.VMEM(inverse.shape, jnp.bfloat16),
            pltpu.VMEM((segments, sources, WIDTH), jnp.float32),
            pltpu.VMEM((segments, 16, WIDTH), jnp.float32),
            pltpu.VMEM((ch_local * sources, WIDTH), jnp.bfloat16),
            pltpu.SemaphoreType.DMA((len(blocks) + 1,)),
        ],
        compiler_params=pltpu.CompilerParams(vmem_limit_bytes=40 * 2**20),
        name="correlate",
    )(place, weights, source_ids.reshape(sources, 1), inverse, *blocks)


def per_device(records, valid_flags, source_ids):
    segments, channels, span = records.shape
    devices = lax.axis_size("chan")
    members = devices // SHARES
    samples = span * devices
    place = lax.axis_index("chan")
    weights = valid_flags.astype(jnp.float32)

    def exchange(block, bits):
        return lax.ppermute(block, "chan", [(i, i ^ bits) for i in range(devices)])

    half = place // members
    groups = [list(range(members)), list(range(members, devices))]
    rows = segments * channels // devices
    grouped = records.reshape(members, SHARES, rows, span)
    table = forward_table(samples)

    def partial(owner):
        chosen = lax.dynamic_index_in_dim(grouped, owner, 1, keepdims=False)
        regrouped = lax.all_to_all(
            chosen, "chan", split_axis=0, concat_axis=0, axis_index_groups=groups, tiled=True
        )
        return transform(half.reshape(1), regrouped, table)

    received = exchange(partial(1 - half), members)
    white = whiten(weights.reshape(1, -1), [partial(half), received])

    far = devices // 8
    line = jnp.stack([white] + [exchange(white, 8 * k) for k in range(1, far)])
    plane = [line] + [exchange(line, 2 * k) for k in range(1, 4)]
    blocks = [b for block in plane for b in (block, exchange(block, 1))]
    return correlate(
        place.reshape(1),
        weights,
        source_ids,
        inverse_table(samples),
        blocks,
        segments,
        channels,
        SHARES,
    )


def solution(mesh):
    return jax.shard_map(
        per_device,
        mesh=mesh,
        in_specs=(P("group", None, "chan"), P("group", "chan"), P("group")),
        out_specs=P("group", "chan", None),
        check_vma=False,
    )
```

```python
import functools
import math

import jax
import jax.numpy as jnp
import ml_dtypes
import numpy as np
from jax import lax
from jax.experimental import pallas as pl
from jax.experimental.pallas import tpu as pltpu
from jax.sharding import PartitionSpec as P

BAND = 600
SOURCES = 64
HALF_LAG = 500

lowest_bin = 8
floor_share = 0.05
epsilon = 1e-06

PART = 640
WIDTH = 2 * PART
LAGS = 2 * HALF_LAG + 1
LAG_TILES = -(-LAGS // 128)
BLOCK = 512
SHARES = 2
FIRST_TILES = 6
FLAG_TILE = BAND // 128 * 128
FLAG_LANE = BAND - FLAG_TILE


def angles(phase, samples):
    step = np.float32(2.0 * math.pi / samples)
    return (phase.astype(np.float32) * step).astype(np.float64)


def cos_sin(samples):
    angle = angles(np.arange(samples), samples)
    return np.cos(angle).astype(np.float32), (-np.sin(angle)).astype(np.float32)


def lane_tiles(table):
    tiled = table.reshape(*table.shape[:-1], -1, 128)
    return np.ascontiguousarray(np.moveaxis(tiled, -2, -3))


@functools.lru_cache(maxsize=None)
def tables(samples):
    bins = lowest_bin + np.arange(BAND)
    cosine, sine = cos_sin(samples)
    phase = np.arange(samples)[:, None] * bins[None, :] % samples
    forward = np.zeros((samples, WIDTH), ml_dtypes.bfloat16)
    forward[:, :BAND] = cosine.astype(ml_dtypes.bfloat16)[phase]
    forward[:, PART : PART + BAND] = sine.astype(ml_dtypes.bfloat16)[phase]
    factor = np.float32(1.0 / math.sqrt(BAND))
    phase = bins[:, None] * (np.arange(LAGS) - HALF_LAG)[None, :] % samples
    inverse = np.zeros((WIDTH, LAG_TILES * 128), ml_dtypes.bfloat16)
    inverse[:BAND, :LAGS] = (cosine * factor).astype(ml_dtypes.bfloat16)[phase]
    inverse[PART : PART + BAND, :LAGS] = (sine * factor).astype(ml_dtypes.bfloat16)[phase]
    parts = [lane_tiles(forward.reshape(-1, BLOCK, WIDTH)), lane_tiles(inverse)]
    return np.concatenate([part.reshape(-1, 128) for part in parts])


def transform_kernel(first, share_ref, records_ref, table_ref, *rest):
    own_ref, other_ref, tiles_ref, sems = rest
    senders, rows, span = records_ref.shape
    blocks, lines, _ = tiles_ref.shape
    columns = lines // BLOCK
    copies = []
    for index in range(blocks):
        block = share_ref[0] * blocks + index
        start = (block * (WIDTH // 128) + first) * BLOCK
        source = table_ref.at[pl.ds(pl.multiple_of(start, BLOCK), lines)]
        copies.append(pltpu.make_async_copy(source, tiles_ref.at[index], sems.at[index]))
        copies[-1].start()
    total = jnp.zeros((rows, columns * 128), jnp.float32)
    pieces = BLOCK // span
    for index in range(blocks):
        copies[index].wait()
        tiles = [tiles_ref[index, tile * BLOCK : (tile + 1) * BLOCK] for tile in range(columns)]
        records = [records_ref[index * pieces + piece] for piece in range(pieces)]
        total += jnp.dot(
            jnp.concatenate(records, axis=1),
            jnp.concatenate(tiles, axis=1),
            preferred_element_type=jnp.float32,
        )
    low, high = total[: rows // 2], total[rows // 2 :]
    mine = share_ref[0] == 0
    own_ref[...] = jnp.where(mine, low, high)
    other_ref[...] = jnp.where(mine, high, low)


def transform(share, records, table, first, last):
    senders, rows, span = records.shape
    columns = last - first
    depth = senders * span
    blocks = depth // BLOCK
    vmem = pl.BlockSpec(memory_space=pltpu.VMEM)
    shape = jax.ShapeDtypeStruct((rows // 2, columns * 128), jnp.float32)
    return pl.pallas_call(
        functools.partial(transform_kernel, first),
        in_specs=[
            pl.BlockSpec(memory_space=pltpu.SMEM),
            vmem,
            pl.BlockSpec(memory_space=pltpu.HBM),
        ],
        out_specs=[vmem, vmem],
        out_shape=[shape, shape],
        scratch_shapes=[
            pltpu.VMEM((blocks, columns * BLOCK, 128), jnp.bfloat16),
            pltpu.SemaphoreType.DMA((blocks,)),
        ],
        compiler_params=pltpu.CompilerParams(vmem_limit_bytes=32 * 2**20),
        cost_estimate=pl.CostEstimate(
            flops=2 * rows * depth * columns * 128,
            bytes_accessed=2 * depth * columns * 128,
            transcendentals=0,
        ),
        name="transform",
    )(share, records, table)


def whiten_kernel(flags_ref, *rest):
    parts, white_ref = rest[:-1], rest[-1]
    sums = [mine[...] + other[...] for mine, other in zip(parts[::2], parts[1::2])]
    total = jnp.concatenate(sums, axis=1)
    real_part, imag_part = total[:, :PART], total[:, PART:]
    power = real_part * real_part + imag_part * imag_part
    level = jnp.sum(power, axis=1, keepdims=True) * (1.0 / BAND)
    factor = lax.rsqrt(power + floor_share * level + epsilon)
    white_ref[:, :PART] = (real_part * factor).astype(jnp.bfloat16)
    white_ref[:, PART:] = (imag_part * factor).astype(jnp.bfloat16)
    rows = total.shape[0]
    lane = lax.broadcasted_iota(jnp.int32, (rows, 128), 1)
    held = (lane >= FLAG_LANE) & (lane < FLAG_LANE + flags_ref.shape[1])
    tile = (real_part * factor)[:, FLAG_TILE : FLAG_TILE + 128]
    flags = jnp.concatenate(
        [
            jnp.zeros((1, FLAG_LANE), jnp.float32),
            flags_ref[...],
            jnp.zeros((1, 128 - FLAG_LANE - flags_ref.shape[1]), jnp.float32),
        ],
        axis=1,
    )
    white_ref[:, FLAG_TILE : FLAG_TILE + 128] = jnp.where(held, flags, tile).astype(jnp.bfloat16)


def whiten(flags, parts):
    return pl.pallas_call(
        whiten_kernel,
        out_shape=jax.ShapeDtypeStruct((parts[0].shape[0], WIDTH), jnp.bfloat16),
        compiler_params=pltpu.CompilerParams(vmem_limit_bytes=16 * 2**20),
        name="whiten",
    )(flags, *parts)


def correlate_kernel(segments, channels, shares, place_ref, flags_ref, ids_ref, table_ref, *rest):
    blocks, rest = rest[:-7], rest[-7:]
    out_ref, held_ref, inverse_ref, panel_ref, receivers_ref, stacked_ref, sem = rest
    lines = inverse_ref.shape[0]
    fetch = pltpu.make_async_copy(
        table_ref.at[pl.ds(table_ref.shape[0] - lines, lines)], inverse_ref, sem
    )
    fetch.start()
    devices, rows, _ = held_ref.shape
    members = devices // shares
    ch_local = channels // devices
    place = place_ref[0]
    ids = ids_ref[...]
    sources = ids.shape[0]

    def position(device):
        return device % members * shares + device // members

    for index, block in enumerate(blocks):
        for line in range(block.shape[0]):
            held_ref[position(place ^ (line * len(blocks) + index))] = block[line]

    tails = held_ref[:, :, FLAG_TILE : FLAG_TILE + 128].reshape(devices * rows, 128)
    column = lax.broadcasted_iota(jnp.int32, (sources, devices * rows), 1)
    choice = (column == position(ids // ch_local) * rows).astype(jnp.bfloat16)
    tail = jnp.dot(choice, tails, preferred_element_type=jnp.float32)
    lane = lax.broadcasted_iota(jnp.int32, (sources, 128), 1)

    channel = lax.broadcasted_iota(jnp.int32, (sources, channels), 1)
    pick_sources = (channel == ids).astype(jnp.bfloat16)
    line = lax.broadcasted_iota(jnp.int32, (16, channels), 0)
    channel = lax.broadcasted_iota(jnp.int32, (16, channels), 1)
    pick_own = ((channel == place * ch_local + line) & (line < ch_local)).astype(jnp.bfloat16)
    pick = jnp.concatenate([pick_sources, pick_own], axis=0)

    counts = [jnp.zeros((sources, 1), jnp.float32) for _ in range(ch_local)]
    for g in range(segments):
        blocks_per = channels // rows
        segment = held_ref[g * blocks_per : (g + 1) * blocks_per].reshape(channels, WIDTH)
        picked = jnp.dot(pick, segment, preferred_element_type=jnp.float32)
        mine = lane == FLAG_LANE + g * ch_local + ids % ch_local
        weight = jnp.sum(jnp.where(mine, tail, 0.0), axis=1, keepdims=True)
        panel_ref[g] = picked[:sources] * weight
        receivers_ref[g] = picked[sources:]
        for c in range(ch_local):
            counts[c] += weight * flags_ref[g, c]

    for c in range(ch_local):
        share = 1.0 / jnp.maximum(counts[c], 1.0)
        lines = slice(c * sources, (c + 1) * sources)
        for start in range(0, PART, 128):
            re = slice(start, start + 128)
            im = slice(PART + start, PART + start + 128)
            real_sum = jnp.zeros((sources, 128), jnp.float32)
            imag_sum = jnp.zeros((sources, 128), jnp.float32)
            for g in range(segments):
                rec_real = receivers_ref[g, c : c + 1, re] * flags_ref[g, c]
                rec_imag = receivers_ref[g, c : c + 1, im] * flags_ref[g, c]
                src_real, src_imag = panel_ref[g, :, re], panel_ref[g, :, im]
                real_sum += src_real * rec_real + src_imag * rec_imag
                imag_sum += src_imag * rec_real - src_real * rec_imag
            stacked_ref[lines, re] = (real_sum * share).astype(jnp.bfloat16)
            stacked_ref[lines, im] = (imag_sum * share).astype(jnp.bfloat16)
    fetch.wait()
    tiles = [inverse_ref[tile * WIDTH : (tile + 1) * WIDTH] for tile in range(LAG_TILES)]
    inverse = jnp.concatenate(tiles, axis=1)
    lags = jnp.dot(stacked_ref[...], inverse, preferred_element_type=jnp.float32)
    for c in range(ch_local):
        out_ref[:, c, :] = lags[c * sources : (c + 1) * sources, :LAGS]


def correlate(place, weights, source_ids, table, blocks, segments, channels, shares):
    far, rows, _ = blocks[0].shape
    devices = far * len(blocks)
    ch_local = channels // devices
    sources = source_ids.shape[0]
    smem = pl.BlockSpec(memory_space=pltpu.SMEM)
    vmem = pl.BlockSpec(memory_space=pltpu.VMEM)
    return pl.pallas_call(
        functools.partial(correlate_kernel, segments, channels, shares),
        in_specs=[smem, smem, vmem, pl.BlockSpec(memory_space=pltpu.HBM)] + [vmem] * len(blocks),
        out_specs=vmem,
        out_shape=jax.ShapeDtypeStruct((sources, ch_local, LAGS), jnp.float32),
        scratch_shapes=[
            pltpu.VMEM((devices, rows, WIDTH), jnp.bfloat16),
            pltpu.VMEM((LAG_TILES * WIDTH, 128), jnp.bfloat16),
            pltpu.VMEM((segments, sources, WIDTH), jnp.float32),
            pltpu.VMEM((segments, 16, WIDTH), jnp.float32),
            pltpu.VMEM((ch_local * sources, WIDTH), jnp.bfloat16),
            pltpu.SemaphoreType.DMA,
        ],
        compiler_params=pltpu.CompilerParams(vmem_limit_bytes=40 * 2**20),
        name="correlate",
    )(place, weights, source_ids.reshape(sources, 1), table, *blocks)


def per_device(records, valid_flags, source_ids):
    segments, channels, span = records.shape
    devices = lax.axis_size("chan")
    members = devices // SHARES
    samples = span * devices
    place = lax.axis_index("chan")
    weights = valid_flags.astype(jnp.float32)

    def exchange(block, bits):
        return lax.ppermute(block, "chan", [(i, i ^ bits) for i in range(devices)])

    share = (place // members).reshape(1)
    groups = [list(range(members)), list(range(members, devices))]
    grouped = records.reshape(members, segments * channels // members, span)
    regrouped = lax.all_to_all(
        grouped, "chan", split_axis=0, concat_axis=0, axis_index_groups=groups, tiled=True
    )
    table = tables(samples)
    parts = []
    for first, last in ((0, FIRST_TILES), (FIRST_TILES, WIDTH // 128)):
        own, other = transform(share, regrouped, table, first, last)
        parts += [own, exchange(other, members)]
    white = whiten(weights.reshape(1, -1), parts)

    far = devices // 8
    line = jnp.stack([white] + [exchange(white, 8 * k) for k in range(1, far)])
    plane = [line] + [exchange(line, 2 * k) for k in range(1, 4)]
    blocks = [b for block in plane for b in (block, exchange(block, 1))]
    return correlate(
        place.reshape(1),
        weights,
        source_ids,
        table,
        blocks,
        segments,
        channels,
        SHARES,
    )


def solution(mesh):
    return jax.shard_map(
        per_device,
        mesh=mesh,
        in_specs=(P("group", None, "chan"), P("group", "chan"), P("group")),
        out_specs=P("group", "chan", None),
        check_vma=False,
    )
```

```python
import functools
import math

import jax
import jax.numpy as jnp
import ml_dtypes
import numpy as np
from jax import lax
from jax.experimental import pallas as pl
from jax.experimental.pallas import tpu as pltpu
from jax.sharding import PartitionSpec as P

BAND = 600
SOURCES = 64
HALF_LAG = 500

lowest_bin = 8
floor_share = 0.05
epsilon = 1e-06

PART = 640
WIDTH = 2 * PART
LAGS = 2 * HALF_LAG + 1
LAG_TILES = -(-LAGS // 128)
SHARES = 2
COLUMN_TILES = WIDTH // 128
FIRST_TILES = 6
FLAG_TILE = BAND // 128 * 128
FLAG_LANE = BAND - FLAG_TILE


def angles(phase, samples):
    step = np.float32(2.0 * math.pi / samples)
    return (phase.astype(np.float32) * step).astype(np.float64)


def cos_sin(samples):
    angle = angles(np.arange(samples), samples)
    return np.cos(angle).astype(np.float32), (-np.sin(angle)).astype(np.float32)


def lane_tiles(table):
    tiled = table.reshape(*table.shape[:-1], -1, 128)
    return np.ascontiguousarray(np.moveaxis(tiled, -2, -3))


@functools.lru_cache(maxsize=None)
def tables(samples, span):
    bins = lowest_bin + np.arange(BAND)
    cosine, sine = cos_sin(samples)
    phase = np.arange(samples)[:, None] * bins[None, :] % samples
    forward = np.zeros((samples, WIDTH), ml_dtypes.bfloat16)
    forward[:, :BAND] = cosine.astype(ml_dtypes.bfloat16)[phase]
    forward[:, PART : PART + BAND] = sine.astype(ml_dtypes.bfloat16)[phase]
    factor = np.float32(1.0 / math.sqrt(BAND))
    phase = bins[:, None] * (np.arange(LAGS) - HALF_LAG)[None, :] % samples
    inverse = np.zeros((WIDTH, LAG_TILES * 128), ml_dtypes.bfloat16)
    inverse[:BAND, :LAGS] = (cosine * factor).astype(ml_dtypes.bfloat16)[phase]
    inverse[PART : PART + BAND, :LAGS] = (sine * factor).astype(ml_dtypes.bfloat16)[phase]
    parts = [lane_tiles(forward.reshape(-1, span, WIDTH)), lane_tiles(inverse)]
    return np.concatenate([part.reshape(-1, 128) for part in parts])


def fetch_kernel(share_ref, table_ref, after_ref, out_ref, sems):
    blocks, lines, _ = out_ref.shape
    batch = blocks // sems.shape[0]
    copies = []
    for index in range(sems.shape[0]):
        for block in range(index * batch, (index + 1) * batch):
            start = (share_ref[0] * blocks + block) * lines
            source = table_ref.at[pl.ds(pl.multiple_of(start, lines), lines)]
            copies.append(pltpu.make_async_copy(source, out_ref.at[block], sems.at[block]))
            copies[-1].start()
    for copy in copies:
        copy.wait()


def fetch(share, table, members, span, after):
    shape = (members, COLUMN_TILES * span, 128)
    return pl.pallas_call(
        fetch_kernel,
        in_specs=[
            pl.BlockSpec(memory_space=pltpu.SMEM),
            pl.BlockSpec(memory_space=pltpu.HBM),
            pl.BlockSpec(memory_space=pl.ANY),
        ],
        out_specs=pl.BlockSpec(memory_space=pltpu.VMEM),
        out_shape=jax.ShapeDtypeStruct(shape, jnp.bfloat16),
        scratch_shapes=[pltpu.SemaphoreType.DMA((members,))],
        compiler_params=pltpu.CompilerParams(vmem_limit_bytes=8 * 2**20),
        cost_estimate=pl.CostEstimate(
            flops=0, bytes_accessed=4 * math.prod(shape), transcendentals=0
        ),
        name="fetch",
    )(share, table, after)


def transform_kernel(steps, first, started, place_ref, table_ref, *rest):
    records, rest = rest[: len(steps)], rest[len(steps) :]
    span = records[0].shape[1]
    members = table_ref.shape[0]
    if started:
        total, outs = rest[0][...], rest[1:]
    else:
        total, outs = None, rest
    columns = outs[0].shape[1] // 128
    for step, block in zip(steps, records):
        member = place_ref[0] % members ^ step
        tiles = [
            table_ref[member, (first + tile) * span : (first + tile + 1) * span]
            for tile in range(columns)
        ]
        product = jnp.dot(
            block[...], jnp.concatenate(tiles, axis=1), preferred_element_type=jnp.float32
        )
        total = product if total is None else total + product
    if len(outs) == 1:
        outs[0][...] = total
    else:
        rows = outs[0].shape[0]
        mine = place_ref[0] < members
        outs[0][...] = jnp.where(mine, total[:rows], total[rows:])
        outs[1][...] = jnp.where(mine, total[rows:], total[:rows])


def transform(place, table, steps, records, first, last, before, split):
    rows, span = records[0].shape
    columns = (last - first) * 128
    vmem = pl.BlockSpec(memory_space=pltpu.VMEM)
    outs = 2 if split else 1
    started = before is not None
    return pl.pallas_call(
        functools.partial(transform_kernel, steps, first, started),
        in_specs=[pl.BlockSpec(memory_space=pltpu.SMEM)] + [vmem] * (1 + len(steps) + started),
        out_specs=[vmem] * outs,
        out_shape=[jax.ShapeDtypeStruct((rows // outs, columns), jnp.float32)] * outs,
        compiler_params=pltpu.CompilerParams(vmem_limit_bytes=8 * 2**20),
        cost_estimate=pl.CostEstimate(
            flops=2 * rows * len(steps) * span * columns,
            bytes_accessed=2 * len(steps) * span * columns,
            transcendentals=0,
        ),
        name="transform",
    )(place, table, *records, *([before] if started else []))


def whiten_kernel(flags_ref, *rest):
    parts, white_ref = rest[:-1], rest[-1]
    sums = [mine[...] + other[...] for mine, other in zip(parts[::2], parts[1::2])]
    total = jnp.concatenate(sums, axis=1)
    real_part, imag_part = total[:, :PART], total[:, PART:]
    power = real_part * real_part + imag_part * imag_part
    level = jnp.sum(power, axis=1, keepdims=True) * (1.0 / BAND)
    factor = lax.rsqrt(power + floor_share * level + epsilon)
    white_ref[:, :PART] = (real_part * factor).astype(jnp.bfloat16)
    white_ref[:, PART:] = (imag_part * factor).astype(jnp.bfloat16)
    rows = total.shape[0]
    lane = lax.broadcasted_iota(jnp.int32, (rows, 128), 1)
    held = (lane >= FLAG_LANE) & (lane < FLAG_LANE + flags_ref.shape[1])
    tile = (real_part * factor)[:, FLAG_TILE : FLAG_TILE + 128]
    flags = jnp.concatenate(
        [
            jnp.zeros((1, FLAG_LANE), jnp.float32),
            flags_ref[...],
            jnp.zeros((1, 128 - FLAG_LANE - flags_ref.shape[1]), jnp.float32),
        ],
        axis=1,
    )
    white_ref[:, FLAG_TILE : FLAG_TILE + 128] = jnp.where(held, flags, tile).astype(jnp.bfloat16)


def whiten(flags, parts):
    return pl.pallas_call(
        whiten_kernel,
        out_shape=jax.ShapeDtypeStruct((parts[0].shape[0], WIDTH), jnp.bfloat16),
        compiler_params=pltpu.CompilerParams(vmem_limit_bytes=16 * 2**20),
        name="whiten",
    )(flags, *parts)


def correlate_kernel(segments, channels, shares, place_ref, flags_ref, ids_ref, table_ref, *rest):
    blocks, rest = rest[:-7], rest[-7:]
    out_ref, held_ref, inverse_ref, panel_ref, receivers_ref, stacked_ref, sem = rest
    lines = inverse_ref.shape[0]
    fetch = pltpu.make_async_copy(
        table_ref.at[pl.ds(table_ref.shape[0] - lines, lines)], inverse_ref, sem
    )
    fetch.start()
    devices, rows, _ = held_ref.shape
    members = devices // shares
    ch_local = channels // devices
    place = place_ref[0]
    ids = ids_ref[...]
    sources = ids.shape[0]

    def position(device):
        return device % members * shares + device // members

    for index, block in enumerate(blocks):
        for line in range(block.shape[0]):
            held_ref[position(place ^ (line * len(blocks) + index))] = block[line]

    tails = held_ref[:, :, FLAG_TILE : FLAG_TILE + 128].reshape(devices * rows, 128)
    column = lax.broadcasted_iota(jnp.int32, (sources, devices * rows), 1)
    choice = (column == position(ids // ch_local) * rows).astype(jnp.bfloat16)
    tail = jnp.dot(choice, tails, preferred_element_type=jnp.float32)
    lane = lax.broadcasted_iota(jnp.int32, (sources, 128), 1)

    channel = lax.broadcasted_iota(jnp.int32, (sources, channels), 1)
    pick_sources = (channel == ids).astype(jnp.bfloat16)
    line = lax.broadcasted_iota(jnp.int32, (16, channels), 0)
    channel = lax.broadcasted_iota(jnp.int32, (16, channels), 1)
    pick_own = ((channel == place * ch_local + line) & (line < ch_local)).astype(jnp.bfloat16)
    pick = jnp.concatenate([pick_sources, pick_own], axis=0)

    counts = [jnp.zeros((sources, 1), jnp.float32) for _ in range(ch_local)]
    for g in range(segments):
        blocks_per = channels // rows
        segment = held_ref[g * blocks_per : (g + 1) * blocks_per].reshape(channels, WIDTH)
        picked = jnp.dot(pick, segment, preferred_element_type=jnp.float32)
        mine = lane == FLAG_LANE + g * ch_local + ids % ch_local
        weight = jnp.sum(jnp.where(mine, tail, 0.0), axis=1, keepdims=True)
        panel_ref[g] = picked[:sources] * weight
        receivers_ref[g] = picked[sources:]
        for c in range(ch_local):
            counts[c] += weight * flags_ref[g, c]

    for c in range(ch_local):
        share = 1.0 / jnp.maximum(counts[c], 1.0)
        lines = slice(c * sources, (c + 1) * sources)
        for start in range(0, PART, 128):
            re = slice(start, start + 128)
            im = slice(PART + start, PART + start + 128)
            real_sum = jnp.zeros((sources, 128), jnp.float32)
            imag_sum = jnp.zeros((sources, 128), jnp.float32)
            for g in range(segments):
                rec_real = receivers_ref[g, c : c + 1, re] * flags_ref[g, c]
                rec_imag = receivers_ref[g, c : c + 1, im] * flags_ref[g, c]
                src_real, src_imag = panel_ref[g, :, re], panel_ref[g, :, im]
                real_sum += src_real * rec_real + src_imag * rec_imag
                imag_sum += src_imag * rec_real - src_real * rec_imag
            stacked_ref[lines, re] = (real_sum * share).astype(jnp.bfloat16)
            stacked_ref[lines, im] = (imag_sum * share).astype(jnp.bfloat16)
    fetch.wait()
    tiles = [inverse_ref[tile * WIDTH : (tile + 1) * WIDTH] for tile in range(LAG_TILES)]
    inverse = jnp.concatenate(tiles, axis=1)
    lags = jnp.dot(stacked_ref[...], inverse, preferred_element_type=jnp.float32)
    for c in range(ch_local):
        out_ref[:, c, :] = lags[c * sources : (c + 1) * sources, :LAGS]


def correlate(place, weights, source_ids, table, blocks, segments, channels, shares):
    far, rows, _ = blocks[0].shape
    devices = far * len(blocks)
    ch_local = channels // devices
    sources = source_ids.shape[0]
    smem = pl.BlockSpec(memory_space=pltpu.SMEM)
    vmem = pl.BlockSpec(memory_space=pltpu.VMEM)
    return pl.pallas_call(
        functools.partial(correlate_kernel, segments, channels, shares),
        in_specs=[smem, smem, vmem, pl.BlockSpec(memory_space=pltpu.HBM)] + [vmem] * len(blocks),
        out_specs=vmem,
        out_shape=jax.ShapeDtypeStruct((sources, ch_local, LAGS), jnp.float32),
        scratch_shapes=[
            pltpu.VMEM((devices, rows, WIDTH), jnp.bfloat16),
            pltpu.VMEM((LAG_TILES * WIDTH, 128), jnp.bfloat16),
            pltpu.VMEM((segments, sources, WIDTH), jnp.float32),
            pltpu.VMEM((segments, 16, WIDTH), jnp.float32),
            pltpu.VMEM((ch_local * sources, WIDTH), jnp.bfloat16),
            pltpu.SemaphoreType.DMA,
        ],
        compiler_params=pltpu.CompilerParams(vmem_limit_bytes=40 * 2**20),
        name="correlate",
    )(place, weights, source_ids.reshape(sources, 1), table, *blocks)


def balanced_steps(members):
    chips = members // 2
    masks = [m for low in range(1, chips // 2) for m in (low, low ^ (chips - 1))] + [chips - 1]
    first = [2 * m for m in masks]
    return [0] + first[5:] + first[:5] + [2 * m + 1 for m in masks] + [1]


def per_device(records, valid_flags, source_ids):
    segments, channels, span = records.shape
    devices = lax.axis_size("chan")
    members = devices // SHARES
    samples = span * devices
    place = lax.axis_index("chan")
    weights = valid_flags.astype(jnp.float32)

    def exchange(block, bits):
        return lax.ppermute(block, "chan", [(i, i ^ bits) for i in range(devices)])

    me = place.reshape(1)
    grouped = records.reshape(members, segments * channels // members, span)
    sent = [
        lax.dynamic_index_in_dim(grouped, place % members ^ step, 0, keepdims=False)
        for step in range(members)
    ]
    arrived = {step: exchange(sent[step], step) if step else sent[0] for step in range(members)}
    table = tables(samples, span)
    near = fetch(me // members, table, members, span, sent[0])
    steps = balanced_steps(members)
    early, late = steps[: members // 2], steps[members // 2 :]
    parts = []
    spans = (0, FIRST_TILES), (FIRST_TILES, COLUMN_TILES)
    begun = [
        transform(me, near, early, [arrived[k] for k in early], first, last, None, False)[0]
        for first, last in spans
    ]
    for (first, last), before in zip(spans, begun):
        own, other = transform(
            me, near, late, [arrived[k] for k in late], first, last, before, True
        )
        parts += [own, exchange(other, members)]
    white = whiten(weights.reshape(1, -1), parts)

    far = devices // 8
    line = jnp.stack([white] + [exchange(white, 8 * k) for k in range(1, far)])
    plane = [line] + [exchange(line, 2 * k) for k in range(1, 4)]
    blocks = [b for block in plane for b in (block, exchange(block, 1))]
    return correlate(
        place.reshape(1),
        weights,
        source_ids,
        table,
        blocks,
        segments,
        channels,
        SHARES,
    )


def solution(mesh):
    return jax.shard_map(
        per_device,
        mesh=mesh,
        in_specs=(P("group", None, "chan"), P("group", "chan"), P("group")),
        out_specs=P("group", "chan", None),
        check_vma=False,
    )
```

```python
import functools
import math

import jax
import jax.numpy as jnp
import ml_dtypes
import numpy as np
from jax import lax
from jax.experimental import pallas as pl
from jax.experimental.pallas import tpu as pltpu
from jax.sharding import PartitionSpec as P

BAND = 600
SOURCES = 64
HALF_LAG = 500

lowest_bin = 8
floor_share = 0.05
epsilon = 1e-06

PART = 640
WIDTH = 2 * PART
LAGS = 2 * HALF_LAG + 1
LAG_TILES = -(-LAGS // 128)
BLOCK = 512
SHARES = 2
FIRST_TILES = 6
LINE_TILES = 7
SPLIT = LINE_TILES * 128
FLAG_TILE = BAND // 128 * 128
FLAG_LANE = BAND - FLAG_TILE


def angles(phase, samples):
    step = np.float32(2.0 * math.pi / samples)
    return (phase.astype(np.float32) * step).astype(np.float64)


def cos_sin(samples):
    angle = angles(np.arange(samples), samples)
    return np.cos(angle).astype(np.float32), (-np.sin(angle)).astype(np.float32)


def lane_tiles(table):
    tiled = table.reshape(*table.shape[:-1], -1, 128)
    return np.ascontiguousarray(np.moveaxis(tiled, -2, -3))


@functools.lru_cache(maxsize=None)
def tables(samples):
    bins = lowest_bin + np.arange(BAND)
    cosine, sine = cos_sin(samples)
    phase = np.arange(samples)[:, None] * bins[None, :] % samples
    forward = np.zeros((samples, WIDTH), ml_dtypes.bfloat16)
    forward[:, :BAND] = cosine.astype(ml_dtypes.bfloat16)[phase]
    forward[:, PART : PART + BAND] = sine.astype(ml_dtypes.bfloat16)[phase]
    factor = np.float32(1.0 / math.sqrt(BAND))
    phase = bins[:, None] * (np.arange(LAGS) - HALF_LAG)[None, :] % samples
    inverse = np.zeros((WIDTH, LAG_TILES * 128), ml_dtypes.bfloat16)
    inverse[:BAND, :LAGS] = (cosine * factor).astype(ml_dtypes.bfloat16)[phase]
    inverse[PART : PART + BAND, :LAGS] = (sine * factor).astype(ml_dtypes.bfloat16)[phase]
    parts = [lane_tiles(forward.reshape(-1, BLOCK, WIDTH)), lane_tiles(inverse)]
    return np.concatenate([part.reshape(-1, 128) for part in parts])


def transform_kernel(first, share_ref, records_ref, table_ref, *rest):
    own_ref, other_ref, tiles_ref, sems = rest
    senders, rows, span = records_ref.shape
    blocks, lines, _ = tiles_ref.shape
    columns = lines // BLOCK
    copies = []
    for index in range(blocks):
        block = share_ref[0] * blocks + index
        start = (block * (WIDTH // 128) + first) * BLOCK
        source = table_ref.at[pl.ds(pl.multiple_of(start, BLOCK), lines)]
        copies.append(pltpu.make_async_copy(source, tiles_ref.at[index], sems.at[index]))
        copies[-1].start()
    total = jnp.zeros((rows, columns * 128), jnp.float32)
    pieces = BLOCK // span
    for index in range(blocks):
        copies[index].wait()
        tiles = [tiles_ref[index, tile * BLOCK : (tile + 1) * BLOCK] for tile in range(columns)]
        records = [records_ref[index * pieces + piece] for piece in range(pieces)]
        total += jnp.dot(
            jnp.concatenate(records, axis=1),
            jnp.concatenate(tiles, axis=1),
            preferred_element_type=jnp.float32,
        )
    low, high = total[: rows // 2], total[rows // 2 :]
    mine = share_ref[0] == 0
    own_ref[...] = jnp.where(mine, low, high)
    other_ref[...] = jnp.where(mine, high, low)


def transform(share, records, table, first, last):
    senders, rows, span = records.shape
    columns = last - first
    depth = senders * span
    blocks = depth // BLOCK
    vmem = pl.BlockSpec(memory_space=pltpu.VMEM)
    shape = jax.ShapeDtypeStruct((rows // 2, columns * 128), jnp.float32)
    return pl.pallas_call(
        functools.partial(transform_kernel, first),
        in_specs=[
            pl.BlockSpec(memory_space=pltpu.SMEM),
            vmem,
            pl.BlockSpec(memory_space=pltpu.HBM),
        ],
        out_specs=[vmem, vmem],
        out_shape=[shape, shape],
        scratch_shapes=[
            pltpu.VMEM((blocks, columns * BLOCK, 128), jnp.bfloat16),
            pltpu.SemaphoreType.DMA((blocks,)),
        ],
        compiler_params=pltpu.CompilerParams(vmem_limit_bytes=32 * 2**20),
        cost_estimate=pl.CostEstimate(
            flops=2 * rows * depth * columns * 128,
            bytes_accessed=2 * depth * columns * 128,
            transcendentals=0,
        ),
        name="transform",
    )(share, records, table)


def whiten_kernel(flags_ref, *rest):
    parts, (first_ref, second_ref) = rest[:-2], rest[-2:]
    sums = [mine[...] + other[...] for mine, other in zip(parts[::2], parts[1::2])]
    total = jnp.concatenate(sums, axis=1)
    real_part, imag_part = total[:, :PART], total[:, PART:]
    power = real_part * real_part + imag_part * imag_part
    level = jnp.sum(power, axis=1, keepdims=True) * (1.0 / BAND)
    factor = lax.rsqrt(power + floor_share * level + epsilon)
    real_part, imag_part = real_part * factor, imag_part * factor
    lane = lax.broadcasted_iota(jnp.int32, (total.shape[0], 128), 1)
    held = (lane >= FLAG_LANE) & (lane < FLAG_LANE + flags_ref.shape[1])
    flags = jnp.concatenate(
        [
            jnp.zeros((1, FLAG_LANE), jnp.float32),
            flags_ref[...],
            jnp.zeros((1, 128 - FLAG_LANE - flags_ref.shape[1]), jnp.float32),
        ],
        axis=1,
    )
    tail = jnp.where(held, flags, real_part[:, FLAG_TILE:])
    white = jnp.concatenate([real_part[:, :FLAG_TILE], tail, imag_part], axis=1)
    white = white.astype(jnp.bfloat16)
    first_ref[...] = white[:, :SPLIT]
    second_ref[...] = white[:, SPLIT:]


def whiten(flags, parts):
    rows = parts[0].shape[0]
    return pl.pallas_call(
        whiten_kernel,
        out_shape=[
            jax.ShapeDtypeStruct((rows, SPLIT), jnp.bfloat16),
            jax.ShapeDtypeStruct((rows, WIDTH - SPLIT), jnp.bfloat16),
        ],
        compiler_params=pltpu.CompilerParams(vmem_limit_bytes=16 * 2**20),
        name="whiten",
    )(flags, *parts)


def correlate_kernel(segments, channels, shares, steps, place_ref, flags_ref, ids_ref, table_ref, *rest):
    blocks, rest = rest[:-7], rest[-7:]
    out_ref, held_ref, inverse_ref, panel_ref, receivers_ref, stacked_ref, sem = rest
    lines = inverse_ref.shape[0]
    fetch = pltpu.make_async_copy(
        table_ref.at[pl.ds(table_ref.shape[0] - lines, lines)], inverse_ref, sem
    )
    fetch.start()
    devices, rows, _ = held_ref.shape
    members = devices // shares
    ch_local = channels // devices
    place = place_ref[0]
    ids = ids_ref[...]
    sources = ids.shape[0]

    def position(device):
        return device % members * shares + device // members

    for (step, stride), block in zip(steps, blocks):
        columns = slice(0, SPLIT) if block.shape[2] == SPLIT else slice(SPLIT, WIDTH)
        for line in range(block.shape[0]):
            held_ref[position(place ^ (line * stride + step)), :, columns] = block[line]

    tails = held_ref[:, :, FLAG_TILE : FLAG_TILE + 128].reshape(devices * rows, 128)
    column = lax.broadcasted_iota(jnp.int32, (sources, devices * rows), 1)
    choice = (column == position(ids // ch_local) * rows).astype(jnp.bfloat16)
    tail = jnp.dot(choice, tails, preferred_element_type=jnp.float32)
    lane = lax.broadcasted_iota(jnp.int32, (sources, 128), 1)

    channel = lax.broadcasted_iota(jnp.int32, (sources, channels), 1)
    pick_sources = (channel == ids).astype(jnp.bfloat16)
    line = lax.broadcasted_iota(jnp.int32, (16, channels), 0)
    channel = lax.broadcasted_iota(jnp.int32, (16, channels), 1)
    pick_own = ((channel == place * ch_local + line) & (line < ch_local)).astype(jnp.bfloat16)
    pick = jnp.concatenate([pick_sources, pick_own], axis=0)

    counts = [jnp.zeros((sources, 1), jnp.float32) for _ in range(ch_local)]
    for g in range(segments):
        blocks_per = channels // rows
        segment = held_ref[g * blocks_per : (g + 1) * blocks_per].reshape(channels, WIDTH)
        picked = jnp.dot(pick, segment, preferred_element_type=jnp.float32)
        mine = lane == FLAG_LANE + g * ch_local + ids % ch_local
        weight = jnp.sum(jnp.where(mine, tail, 0.0), axis=1, keepdims=True)
        panel_ref[g] = picked[:sources] * weight
        receivers_ref[g] = picked[sources:]
        for c in range(ch_local):
            counts[c] += weight * flags_ref[g, c]

    for c in range(ch_local):
        share = 1.0 / jnp.maximum(counts[c], 1.0)
        lines = slice(c * sources, (c + 1) * sources)
        for start in range(0, PART, 128):
            re = slice(start, start + 128)
            im = slice(PART + start, PART + start + 128)
            real_sum = jnp.zeros((sources, 128), jnp.float32)
            imag_sum = jnp.zeros((sources, 128), jnp.float32)
            for g in range(segments):
                rec_real = receivers_ref[g, c : c + 1, re] * flags_ref[g, c]
                rec_imag = receivers_ref[g, c : c + 1, im] * flags_ref[g, c]
                src_real, src_imag = panel_ref[g, :, re], panel_ref[g, :, im]
                real_sum += src_real * rec_real + src_imag * rec_imag
                imag_sum += src_imag * rec_real - src_real * rec_imag
            stacked_ref[lines, re] = (real_sum * share).astype(jnp.bfloat16)
            stacked_ref[lines, im] = (imag_sum * share).astype(jnp.bfloat16)
    fetch.wait()
    tiles = [inverse_ref[tile * WIDTH : (tile + 1) * WIDTH] for tile in range(LAG_TILES)]
    inverse = jnp.concatenate(tiles, axis=1)
    lags = jnp.dot(stacked_ref[...], inverse, preferred_element_type=jnp.float32)
    for c in range(ch_local):
        out_ref[:, c, :] = lags[c * sources : (c + 1) * sources, :LAGS]


def correlate(place, weights, source_ids, table, steps, blocks, segments, channels, devices):
    rows = blocks[0].shape[1]
    ch_local = channels // devices
    sources = source_ids.shape[0]
    smem = pl.BlockSpec(memory_space=pltpu.SMEM)
    vmem = pl.BlockSpec(memory_space=pltpu.VMEM)
    return pl.pallas_call(
        functools.partial(correlate_kernel, segments, channels, SHARES, steps),
        in_specs=[smem, smem, vmem, pl.BlockSpec(memory_space=pltpu.HBM)] + [vmem] * len(blocks),
        out_specs=vmem,
        out_shape=jax.ShapeDtypeStruct((sources, ch_local, LAGS), jnp.float32),
        scratch_shapes=[
            pltpu.VMEM((devices, rows, WIDTH), jnp.bfloat16),
            pltpu.VMEM((LAG_TILES * WIDTH, 128), jnp.bfloat16),
            pltpu.VMEM((segments, sources, WIDTH), jnp.float32),
            pltpu.VMEM((segments, 16, WIDTH), jnp.float32),
            pltpu.VMEM((ch_local * sources, WIDTH), jnp.bfloat16),
            pltpu.SemaphoreType.DMA,
        ],
        compiler_params=pltpu.CompilerParams(vmem_limit_bytes=40 * 2**20),
        name="correlate",
    )(place, weights, source_ids.reshape(sources, 1), table, *blocks)


def per_device(records, valid_flags, source_ids):
    segments, channels, span = records.shape
    devices = lax.axis_size("chan")
    members = devices // SHARES
    samples = span * devices
    place = lax.axis_index("chan")
    weights = valid_flags.astype(jnp.float32)

    def exchange(block, bits):
        return lax.ppermute(block, "chan", [(i, i ^ bits) for i in range(devices)])

    share = (place // members).reshape(1)
    groups = [list(range(members)), list(range(members, devices))]
    grouped = records.reshape(members, segments * channels // members, span)
    regrouped = lax.all_to_all(
        grouped, "chan", split_axis=0, concat_axis=0, axis_index_groups=groups, tiled=True
    )
    table = tables(samples)
    parts = []
    for first, last in ((0, FIRST_TILES), (FIRST_TILES, WIDTH // 128)):
        own, other = transform(share, regrouped, table, first, last)
        parts += [own, exchange(other, members)]
    first, second = whiten(weights.reshape(1, -1), parts)

    far, near = [8 * k for k in range(devices // 8)], [2 * k for k in range(4)]
    line = jnp.stack([exchange(first, step) if step else first for step in far])
    plane = jnp.stack([exchange(second, step) if step else second for step in near])
    steps, blocks = [], []
    for stacked, stride, others in ((line, 8, near), (plane, 2, far)):
        for step in others:
            block = exchange(stacked, step) if step else stacked
            blocks += [block, exchange(block, 1)]
            steps += [(step, stride), (step + 1, stride)]
    return correlate(
        place.reshape(1),
        weights,
        source_ids,
        table,
        steps,
        blocks,
        segments,
        channels,
        devices,
    )


def solution(mesh):
    return jax.shard_map(
        per_device,
        mesh=mesh,
        in_specs=(P("group", None, "chan"), P("group", "chan"), P("group")),
        out_specs=P("group", "chan", None),
        check_vma=False,
    )
```

```python
import functools
import math

import jax
import jax.numpy as jnp
import ml_dtypes
import numpy as np
from jax import lax
from jax.experimental import pallas as pl
from jax.experimental.pallas import tpu as pltpu
from jax.sharding import PartitionSpec as P

BAND = 600
SOURCES = 64
HALF_LAG = 500

lowest_bin = 8
floor_share = 0.05
epsilon = 1e-06

PART = 640
WIDTH = 2 * PART
LAGS = 2 * HALF_LAG + 1
LAG_TILES = -(-LAGS // 128)
BLOCK = 512
SHARES = 2
FIRST_TILES = 6
FLAG_TILE = BAND // 128 * 128
FLAG_LANE = BAND - FLAG_TILE


def angles(phase, samples):
    step = np.float32(2.0 * math.pi / samples)
    return (phase.astype(np.float32) * step).astype(np.float64)


def cos_sin(samples):
    angle = angles(np.arange(samples), samples)
    return np.cos(angle).astype(np.float32), (-np.sin(angle)).astype(np.float32)


def lane_tiles(table):
    tiled = table.reshape(*table.shape[:-1], -1, 128)
    return np.ascontiguousarray(np.moveaxis(tiled, -2, -3))


@functools.lru_cache(maxsize=None)
def tables(samples):
    bins = lowest_bin + np.arange(BAND)
    cosine, sine = cos_sin(samples)
    phase = np.arange(samples)[:, None] * bins[None, :] % samples
    forward = np.zeros((samples, WIDTH), ml_dtypes.bfloat16)
    forward[:, :BAND] = cosine.astype(ml_dtypes.bfloat16)[phase]
    forward[:, PART : PART + BAND] = sine.astype(ml_dtypes.bfloat16)[phase]
    factor = np.float32(1.0 / math.sqrt(BAND))
    phase = bins[:, None] * (np.arange(LAGS) - HALF_LAG)[None, :] % samples
    inverse = np.zeros((WIDTH, LAG_TILES * 128), ml_dtypes.bfloat16)
    inverse[:BAND, :LAGS] = (cosine * factor).astype(ml_dtypes.bfloat16)[phase]
    inverse[PART : PART + BAND, :LAGS] = (sine * factor).astype(ml_dtypes.bfloat16)[phase]
    parts = [lane_tiles(forward.reshape(-1, BLOCK, WIDTH)), lane_tiles(inverse)]
    return np.concatenate([part.reshape(-1, 128) for part in parts])


def transform_kernel(first, share_ref, records_ref, table_ref, *rest):
    own_ref, other_ref, tiles_ref, sems = rest
    senders, rows, span = records_ref.shape
    blocks, lines, _ = tiles_ref.shape
    columns = lines // BLOCK
    copies = []
    for index in range(blocks):
        block = share_ref[0] * blocks + index
        start = (block * (WIDTH // 128) + first) * BLOCK
        source = table_ref.at[pl.ds(pl.multiple_of(start, BLOCK), lines)]
        copies.append(pltpu.make_async_copy(source, tiles_ref.at[index], sems.at[index]))
        copies[-1].start()
    total = jnp.zeros((rows, columns * 128), jnp.float32)
    pieces = BLOCK // span
    for index in range(blocks):
        copies[index].wait()
        tiles = [tiles_ref[index, tile * BLOCK : (tile + 1) * BLOCK] for tile in range(columns)]
        records = [records_ref[index * pieces + piece] for piece in range(pieces)]
        total += jnp.dot(
            jnp.concatenate(records, axis=1),
            jnp.concatenate(tiles, axis=1),
            preferred_element_type=jnp.float32,
        )
    low, high = total[: rows // 2], total[rows // 2 :]
    mine = share_ref[0] == 0
    own_ref[...] = jnp.where(mine, low, high)
    other_ref[...] = jnp.where(mine, high, low)


def transform(share, records, table, first, last):
    senders, rows, span = records.shape
    columns = last - first
    depth = senders * span
    blocks = depth // BLOCK
    vmem = pl.BlockSpec(memory_space=pltpu.VMEM)
    shape = jax.ShapeDtypeStruct((rows // 2, columns * 128), jnp.float32)
    return pl.pallas_call(
        functools.partial(transform_kernel, first),
        in_specs=[
            pl.BlockSpec(memory_space=pltpu.SMEM),
            vmem,
            pl.BlockSpec(memory_space=pltpu.HBM),
        ],
        out_specs=[vmem, vmem],
        out_shape=[shape, shape],
        scratch_shapes=[
            pltpu.VMEM((blocks, columns * BLOCK, 128), jnp.bfloat16),
            pltpu.SemaphoreType.DMA((blocks,)),
        ],
        compiler_params=pltpu.CompilerParams(vmem_limit_bytes=32 * 2**20),
        cost_estimate=pl.CostEstimate(
            flops=2 * rows * depth * columns * 128,
            bytes_accessed=2 * depth * columns * 128,
            transcendentals=0,
        ),
        name="transform",
    )(share, records, table)


def whiten_kernel(flags_ref, *rest):
    parts, white_ref = rest[:-1], rest[-1]
    sums = [mine[...] + other[...] for mine, other in zip(parts[::2], parts[1::2])]
    total = jnp.concatenate(sums, axis=1)
    real_part, imag_part = total[:, :PART], total[:, PART:]
    power = real_part * real_part + imag_part * imag_part
    level = jnp.sum(power, axis=1, keepdims=True) * (1.0 / BAND)
    factor = lax.rsqrt(power + floor_share * level + epsilon)
    white_ref[:, :PART] = (real_part * factor).astype(jnp.bfloat16)
    white_ref[:, PART:] = (imag_part * factor).astype(jnp.bfloat16)
    rows = total.shape[0]
    lane = lax.broadcasted_iota(jnp.int32, (rows, 128), 1)
    held = (lane >= FLAG_LANE) & (lane < FLAG_LANE + flags_ref.shape[1])
    tile = (real_part * factor)[:, FLAG_TILE : FLAG_TILE + 128]
    flags = jnp.concatenate(
        [
            jnp.zeros((1, FLAG_LANE), jnp.float32),
            flags_ref[...],
            jnp.zeros((1, 128 - FLAG_LANE - flags_ref.shape[1]), jnp.float32),
        ],
        axis=1,
    )
    white_ref[:, FLAG_TILE : FLAG_TILE + 128] = jnp.where(held, flags, tile).astype(jnp.bfloat16)


def whiten(flags, parts):
    return pl.pallas_call(
        whiten_kernel,
        out_shape=jax.ShapeDtypeStruct((parts[0].shape[0], WIDTH), jnp.bfloat16),
        compiler_params=pltpu.CompilerParams(vmem_limit_bytes=16 * 2**20),
        name="whiten",
    )(flags, *parts)


def correlate_kernel(segments, channels, shares, place_ref, flags_ref, ids_ref, table_ref, *rest):
    blocks, rest = rest[:-7], rest[-7:]
    out_ref, held_ref, inverse_ref, panel_ref, receivers_ref, stacked_ref, sem = rest
    lines = inverse_ref.shape[0]
    fetch = pltpu.make_async_copy(
        table_ref.at[pl.ds(table_ref.shape[0] - lines, lines)], inverse_ref, sem
    )
    fetch.start()
    devices, rows, _ = held_ref.shape
    members = devices // shares
    ch_local = channels // devices
    place = place_ref[0]
    ids = ids_ref[...]
    sources = ids.shape[0]

    def position(device):
        return device % members * shares + device // members

    for core, block in enumerate(blocks):
        for near in range(block.shape[0]):
            for far in range(block.shape[1]):
                held_ref[position(8 * far + 2 * near + (place % 2 ^ core))] = block[near, far]

    tails = held_ref[:, :, FLAG_TILE : FLAG_TILE + 128].reshape(devices * rows, 128)
    column = lax.broadcasted_iota(jnp.int32, (sources, devices * rows), 1)
    choice = (column == position(ids // ch_local) * rows).astype(jnp.bfloat16)
    tail = jnp.dot(choice, tails, preferred_element_type=jnp.float32)
    lane = lax.broadcasted_iota(jnp.int32, (sources, 128), 1)

    channel = lax.broadcasted_iota(jnp.int32, (sources, channels), 1)
    pick_sources = (channel == ids).astype(jnp.bfloat16)
    line = lax.broadcasted_iota(jnp.int32, (16, channels), 0)
    channel = lax.broadcasted_iota(jnp.int32, (16, channels), 1)
    pick_own = ((channel == place * ch_local + line) & (line < ch_local)).astype(jnp.bfloat16)
    pick = jnp.concatenate([pick_sources, pick_own], axis=0)

    counts = [jnp.zeros((sources, 1), jnp.float32) for _ in range(ch_local)]
    for g in range(segments):
        blocks_per = channels // rows
        segment = held_ref[g * blocks_per : (g + 1) * blocks_per].reshape(channels, WIDTH)
        picked = jnp.dot(pick, segment, preferred_element_type=jnp.float32)
        mine = lane == FLAG_LANE + g * ch_local + ids % ch_local
        weight = jnp.sum(jnp.where(mine, tail, 0.0), axis=1, keepdims=True)
        panel_ref[g] = picked[:sources] * weight
        receivers_ref[g] = picked[sources:]
        for c in range(ch_local):
            counts[c] += weight * flags_ref[g, c]

    for c in range(ch_local):
        share = 1.0 / jnp.maximum(counts[c], 1.0)
        lines = slice(c * sources, (c + 1) * sources)
        for start in range(0, PART, 128):
            re = slice(start, start + 128)
            im = slice(PART + start, PART + start + 128)
            real_sum = jnp.zeros((sources, 128), jnp.float32)
            imag_sum = jnp.zeros((sources, 128), jnp.float32)
            for g in range(segments):
                rec_real = receivers_ref[g, c : c + 1, re] * flags_ref[g, c]
                rec_imag = receivers_ref[g, c : c + 1, im] * flags_ref[g, c]
                src_real, src_imag = panel_ref[g, :, re], panel_ref[g, :, im]
                real_sum += src_real * rec_real + src_imag * rec_imag
                imag_sum += src_imag * rec_real - src_real * rec_imag
            stacked_ref[lines, re] = (real_sum * share).astype(jnp.bfloat16)
            stacked_ref[lines, im] = (imag_sum * share).astype(jnp.bfloat16)
    fetch.wait()
    tiles = [inverse_ref[tile * WIDTH : (tile + 1) * WIDTH] for tile in range(LAG_TILES)]
    inverse = jnp.concatenate(tiles, axis=1)
    lags = jnp.dot(stacked_ref[...], inverse, preferred_element_type=jnp.float32)
    for c in range(ch_local):
        out_ref[:, c, :] = lags[c * sources : (c + 1) * sources, :LAGS]


def correlate(place, weights, source_ids, table, blocks, segments, channels, shares):
    near, far, rows, _ = blocks[0].shape
    devices = far * near * len(blocks)
    ch_local = channels // devices
    sources = source_ids.shape[0]
    smem = pl.BlockSpec(memory_space=pltpu.SMEM)
    vmem = pl.BlockSpec(memory_space=pltpu.VMEM)
    return pl.pallas_call(
        functools.partial(correlate_kernel, segments, channels, shares),
        in_specs=[smem, smem, vmem, pl.BlockSpec(memory_space=pltpu.HBM)] + [vmem] * len(blocks),
        out_specs=vmem,
        out_shape=jax.ShapeDtypeStruct((sources, ch_local, LAGS), jnp.float32),
        scratch_shapes=[
            pltpu.VMEM((devices, rows, WIDTH), jnp.bfloat16),
            pltpu.VMEM((LAG_TILES * WIDTH, 128), jnp.bfloat16),
            pltpu.VMEM((segments, sources, WIDTH), jnp.float32),
            pltpu.VMEM((segments, 16, WIDTH), jnp.float32),
            pltpu.VMEM((ch_local * sources, WIDTH), jnp.bfloat16),
            pltpu.SemaphoreType.DMA,
        ],
        compiler_params=pltpu.CompilerParams(vmem_limit_bytes=40 * 2**20),
        name="correlate",
    )(place, weights, source_ids.reshape(sources, 1), table, *blocks)


def per_device(records, valid_flags, source_ids):
    segments, channels, span = records.shape
    devices = lax.axis_size("chan")
    members = devices // SHARES
    samples = span * devices
    place = lax.axis_index("chan")
    weights = valid_flags.astype(jnp.float32)

    def exchange(block, bits):
        return lax.ppermute(block, "chan", [(i, i ^ bits) for i in range(devices)])

    share = (place // members).reshape(1)
    groups = [list(range(members)), list(range(members, devices))]
    grouped = records.reshape(members, segments * channels // members, span)
    regrouped = lax.all_to_all(
        grouped, "chan", split_axis=0, concat_axis=0, axis_index_groups=groups, tiled=True
    )
    table = tables(samples)
    parts = []
    for first, last in ((0, FIRST_TILES), (FIRST_TILES, WIDTH // 128)):
        own, other = transform(share, regrouped, table, first, last)
        parts += [own, exchange(other, members)]
    white = whiten(weights.reshape(1, -1), parts)

    far = devices // 8
    lines = [[8 * k + d for k in range(far)] for d in range(8)]
    planes = [[8 * k + 2 * d + c for d in range(4)] for k in range(far) for c in range(2)]
    line = lax.all_gather(white, "chan", axis_index_groups=lines)
    plane = lax.all_gather(line, "chan", axis_index_groups=planes)
    blocks = [plane, exchange(plane, 1)]
    return correlate(
        place.reshape(1),
        weights,
        source_ids,
        table,
        blocks,
        segments,
        channels,
        SHARES,
    )


def solution(mesh):
    return jax.shard_map(
        per_device,
        mesh=mesh,
        in_specs=(P("group", None, "chan"), P("group", "chan"), P("group")),
        out_specs=P("group", "chan", None),
        check_vma=False,
    )
```

```python
import functools
import math

import jax
import jax.numpy as jnp
import ml_dtypes
import numpy as np
from jax import lax
from jax.experimental import pallas as pl
from jax.experimental.pallas import tpu as pltpu
from jax.sharding import PartitionSpec as P

BAND = 600
SOURCES = 64
HALF_LAG = 500

lowest_bin = 8
floor_share = 0.05
epsilon = 1e-06

PART = 640
WIDTH = 2 * PART
LAGS = 2 * HALF_LAG + 1
LAG_TILES = -(-LAGS // 128)
SHARES = 4
COLUMN_TILES = WIDTH // 128
FIRST_TILES = 6
FLAG_TILE = BAND // 128 * 128
FLAG_LANE = BAND - FLAG_TILE


def angles(phase, samples):
    step = np.float32(2.0 * math.pi / samples)
    return (phase.astype(np.float32) * step).astype(np.float64)


def cos_sin(samples):
    angle = angles(np.arange(samples), samples)
    return np.cos(angle).astype(np.float32), (-np.sin(angle)).astype(np.float32)


def lane_tiles(table):
    tiled = table.reshape(*table.shape[:-1], -1, 128)
    return np.ascontiguousarray(np.moveaxis(tiled, -2, -3))


@functools.lru_cache(maxsize=None)
def tables(samples, span):
    bins = lowest_bin + np.arange(BAND)
    cosine, sine = cos_sin(samples)
    phase = np.arange(samples)[:, None] * bins[None, :] % samples
    forward = np.zeros((samples, WIDTH), ml_dtypes.bfloat16)
    forward[:, :BAND] = cosine.astype(ml_dtypes.bfloat16)[phase]
    forward[:, PART : PART + BAND] = sine.astype(ml_dtypes.bfloat16)[phase]
    return lane_tiles(forward.reshape(-1, span, WIDTH)).reshape(-1, 128)


@functools.lru_cache(maxsize=None)
def inverse_table(samples):
    bins = lowest_bin + np.arange(BAND)
    cosine, sine = cos_sin(samples)
    factor = np.float32(1.0 / math.sqrt(BAND))
    phase = bins[:, None] * (np.arange(LAGS) - HALF_LAG)[None, :] % samples
    inverse = np.zeros((WIDTH, LAG_TILES * 128), ml_dtypes.bfloat16)
    inverse[:BAND, :LAGS] = (cosine * factor).astype(ml_dtypes.bfloat16)[phase]
    inverse[PART : PART + BAND, :LAGS] = (sine * factor).astype(ml_dtypes.bfloat16)[phase]
    return lane_tiles(inverse).reshape(-1, 128)


def chunk_device(chunk, members, segments):
    per_segment = members // segments
    segment, part = divmod(chunk, per_segment)
    return segment // 2 * 2 * per_segment + 2 * part + segment % 2


def transform_kernel(first, senders, share_ref, records_ref, table_ref, *rest):
    outs, (tiles_ref, sems) = rest[:-2], rest[-2:]
    members, rows, span = records_ref.shape
    lines = tiles_ref.shape[1]
    columns = lines // span
    copies = []
    for index, sender in enumerate(senders):
        start = ((share_ref[0] * members + sender) * COLUMN_TILES + first) * span
        source = table_ref.at[pl.ds(pl.multiple_of(start, span), lines)]
        copies.append(pltpu.make_async_copy(source, tiles_ref.at[index], sems.at[index]))
        copies[-1].start()
    total = jnp.zeros((rows, columns * 128), jnp.float32)
    for index in range(members):
        copies[index].wait()
        tiles = [tiles_ref[index, tile * span : (tile + 1) * span] for tile in range(columns)]
        total += jnp.dot(
            records_ref[index], jnp.concatenate(tiles, axis=1), preferred_element_type=jnp.float32
        )
    kept = rows // len(outs)
    for step, out in enumerate(outs):
        chosen = total[:kept]
        for owner in range(1, len(outs)):
            mine = (share_ref[0] ^ step) == owner
            chosen = jnp.where(mine, total[owner * kept : (owner + 1) * kept], chosen)
        out[...] = chosen


def transform(share, records, table, senders, first, last):
    members, rows, span = records.shape
    columns = last - first
    vmem = pl.BlockSpec(memory_space=pltpu.VMEM)
    shape = jax.ShapeDtypeStruct((rows // SHARES, columns * 128), jnp.float32)
    return pl.pallas_call(
        functools.partial(transform_kernel, first, senders),
        in_specs=[
            pl.BlockSpec(memory_space=pltpu.SMEM),
            vmem,
            pl.BlockSpec(memory_space=pltpu.HBM),
        ],
        out_specs=[vmem] * SHARES,
        out_shape=[shape] * SHARES,
        scratch_shapes=[
            pltpu.VMEM((members, columns * span, 128), jnp.bfloat16),
            pltpu.SemaphoreType.DMA((members,)),
        ],
        compiler_params=pltpu.CompilerParams(vmem_limit_bytes=32 * 2**20),
        cost_estimate=pl.CostEstimate(
            flops=2 * rows * members * span * columns * 128,
            bytes_accessed=2 * members * span * columns * 128,
            transcendentals=0,
        ),
        name="transform",
    )(share, records, table)


def whiten_kernel(flags_ref, *rest):
    parts, white_ref = rest[:-1], rest[-1]
    sums = []
    for first in range(0, len(parts), SHARES):
        sums.append(parts[first][...])
        for part in parts[first + 1 : first + SHARES]:
            sums[-1] += part[...]
    total = jnp.concatenate(sums, axis=1)
    real_part, imag_part = total[:, :PART], total[:, PART:]
    power = real_part * real_part + imag_part * imag_part
    level = jnp.sum(power, axis=1, keepdims=True) * (1.0 / BAND)
    factor = lax.rsqrt(power + floor_share * level + epsilon)
    white_ref[:, :PART] = (real_part * factor).astype(jnp.bfloat16)
    white_ref[:, PART:] = (imag_part * factor).astype(jnp.bfloat16)
    rows = total.shape[0]
    lane = lax.broadcasted_iota(jnp.int32, (rows, 128), 1)
    held = (lane >= FLAG_LANE) & (lane < FLAG_LANE + flags_ref.shape[1])
    tile = (real_part * factor)[:, FLAG_TILE : FLAG_TILE + 128]
    flags = jnp.concatenate(
        [
            jnp.zeros((1, FLAG_LANE), jnp.float32),
            flags_ref[...],
            jnp.zeros((1, 128 - FLAG_LANE - flags_ref.shape[1]), jnp.float32),
        ],
        axis=1,
    )
    white_ref[:, FLAG_TILE : FLAG_TILE + 128] = jnp.where(held, flags, tile).astype(jnp.bfloat16)


def whiten(flags, parts):
    return pl.pallas_call(
        whiten_kernel,
        out_shape=jax.ShapeDtypeStruct((parts[0].shape[0], WIDTH), jnp.bfloat16),
        compiler_params=pltpu.CompilerParams(vmem_limit_bytes=16 * 2**20),
        name="whiten",
    )(flags, *parts)


def correlate_kernel(shape, core, place_ref, flags_ref, ids_ref, *rest):
    segments, channels, devices, blocks = shape
    blocks, rest = rest[:blocks], rest[blocks:]
    if core:
        before_ref, table_ref, out_ref = rest[:3]
        held_ref, panel_ref, receivers_ref, inverse_ref, stacked_ref, sem = rest[3:]
        fetch = pltpu.make_async_copy(table_ref, inverse_ref, sem)
        fetch.start()
    else:
        out_ref, held_ref, panel_ref, receivers_ref = rest
    rows = held_ref.shape[1]
    members = devices // SHARES
    parts = members // segments
    ch_local = channels // devices
    ch_chip = 2 * ch_local
    place = place_ref[0]
    parity = place % 2 ^ core
    ids = ids_ref[...]
    sources = ids.shape[0]

    def position(device):
        member = device % members
        return (member // 2) * SHARES + device // members

    for index, block in enumerate(blocks):
        for line in range(block.shape[0]):
            device = place ^ (line * 8 + index * 2 + core)
            held_ref[position(device)] = block[line]

    tails = held_ref[:, :, FLAG_TILE : FLAG_TILE + 128].reshape(held_ref.shape[0] * rows, 128)
    column = lax.broadcasted_iota(jnp.int32, (sources, tails.shape[0]), 1)
    choice = (column == position(ids // ch_chip * 2 + parity) * rows).astype(jnp.bfloat16)
    tail = jnp.dot(choice, tails, preferred_element_type=jnp.float32)
    lane = lax.broadcasted_iota(jnp.int32, (sources, 128), 1)

    channel = lax.broadcasted_iota(jnp.int32, (sources, channels), 1)
    pick_sources = (channel == ids).astype(jnp.bfloat16)
    line = lax.broadcasted_iota(jnp.int32, (16, channels), 0)
    channel = lax.broadcasted_iota(jnp.int32, (16, channels), 1)
    pick_own = ((channel == place * ch_local + line) & (line < ch_local)).astype(jnp.bfloat16)
    pick = jnp.concatenate([pick_sources, pick_own], axis=0)

    counts = [jnp.zeros((sources, 1), jnp.float32) for _ in range(ch_local)]
    per_segment = channels // rows
    for g in range(segments // 2):
        segment = held_ref[g * per_segment : (g + 1) * per_segment].reshape(channels, WIDTH)
        picked = jnp.dot(pick, segment, preferred_element_type=jnp.float32)
        mine = lane == FLAG_LANE + g * ch_chip + ids % ch_chip
        weight = jnp.sum(jnp.where(mine, tail, 0.0), axis=1, keepdims=True)
        panel_ref[g] = picked[:sources] * weight
        receivers_ref[g] = picked[sources:]
        for c in range(ch_local):
            counts[c] += weight * flags_ref[2 * g + parity, c]

    shares = [None] * ch_local
    for start in [FLAG_TILE] + [start for start in range(0, PART, 128) if start != FLAG_TILE]:
        re = slice(start, start + 128)
        im = slice(PART + start, PART + start + 128)
        for c in range(ch_local):
            real_sum = jnp.zeros((sources, 128), jnp.float32)
            imag_sum = jnp.zeros((sources, 128), jnp.float32)
            for g in range(segments // 2):
                flag = flags_ref[2 * g + parity, c]
                rec_real = receivers_ref[g, c : c + 1, re] * flag
                rec_imag = receivers_ref[g, c : c + 1, im] * flag
                src_real, src_imag = panel_ref[g, :, re], panel_ref[g, :, im]
                real_sum += src_real * rec_real + src_imag * rec_imag
                imag_sum += src_imag * rec_real - src_real * rec_imag
            if start == FLAG_TILE:
                real_sum = jnp.where(lane == FLAG_LANE, counts[c], real_sum)
            if not core:
                out_ref[c, :, re] = real_sum
                out_ref[c, :, im] = imag_sum
                continue
            real_sum += before_ref[c, :, re]
            imag_sum += before_ref[c, :, im]
            if start == FLAG_TILE:
                total = real_sum[:, FLAG_LANE : FLAG_LANE + 1]
                shares[c] = 1.0 / jnp.maximum(total, 1.0)
            lines = pl.ds(c, sources, stride=ch_local)
            stacked_ref[start // 128, lines, :] = real_sum * shares[c]
            stacked_ref[(PART + start) // 128, lines, :] = imag_sum * shares[c]
    if core:
        fetch.wait()
        tiles = [inverse_ref[tile * WIDTH : (tile + 1) * WIDTH] for tile in range(LAG_TILES)]
        lags = jnp.dot(
            jnp.concatenate([stacked_ref[i] for i in range(COLUMN_TILES)], axis=1).astype(
                jnp.bfloat16
            ),
            jnp.concatenate(tiles, axis=1),
            preferred_element_type=jnp.float32,
        )
        out_ref[...] = lags.reshape(sources, ch_local, LAG_TILES * 128)[:, :, :LAGS]


def correlate(core, place, weights, ids, blocks, shape, before=None, table=None):
    segments, channels, devices = shape
    rows = blocks[0].shape[1]
    ch_local = channels // devices
    sources = ids.shape[0]
    smem = pl.BlockSpec(memory_space=pltpu.SMEM)
    vmem = pl.BlockSpec(memory_space=pltpu.VMEM)
    in_specs = [smem, smem, vmem] + [vmem] * len(blocks)
    scratch = [
        pltpu.VMEM((devices // 2, rows, WIDTH), jnp.bfloat16),
        pltpu.VMEM((segments // 2, sources, WIDTH), jnp.float32),
        pltpu.VMEM((segments // 2, 16, WIDTH), jnp.float32),
    ]
    if core:
        in_specs += [vmem, pl.BlockSpec(memory_space=pltpu.HBM)]
        scratch += [
            pltpu.VMEM(table.shape, jnp.bfloat16),
            pltpu.VMEM((COLUMN_TILES, sources * ch_local, 128), jnp.float32),
            pltpu.SemaphoreType.DMA,
        ]
    out = (sources, ch_local, LAGS) if core else (ch_local, sources, WIDTH)
    return pl.pallas_call(
        functools.partial(correlate_kernel, (*shape, len(blocks)), core),
        in_specs=in_specs,
        out_specs=vmem,
        out_shape=jax.ShapeDtypeStruct(out, jnp.float32),
        scratch_shapes=scratch,
        compiler_params=pltpu.CompilerParams(vmem_limit_bytes=32 * 2**20),
        cost_estimate=pl.CostEstimate(
            flops=sources * channels * WIDTH * segments,
            bytes_accessed=2 * (segments // 2) * channels * WIDTH,
            transcendentals=0,
        ),
        name="correlate",
    )(place, weights, ids, *blocks, *([before, table] if core else []))


def per_device(records, valid_flags, source_ids):
    segments, channels, span = records.shape
    devices = lax.axis_size("chan")
    members = devices // SHARES
    samples = span * devices
    place = lax.axis_index("chan")
    weights = valid_flags.astype(jnp.float32)

    def exchange(block, bits):
        return lax.ppermute(block, "chan", [(i, i ^ bits) for i in range(devices)])

    parity = place % 2
    partner = exchange(weights, 1)
    chip = jnp.where(
        parity == 0,
        jnp.concatenate([weights, partner], axis=1),
        jnp.concatenate([partner, weights], axis=1),
    )
    chip = chip.reshape(segments // 2, 2, -1)
    flags = lax.dynamic_index_in_dim(chip, parity, 1, keepdims=False).reshape(1, -1)

    share = (place // members).reshape(1)
    senders = [chunk_device(chunk, members, segments) for chunk in range(members)]
    groups = [[first + sender for sender in senders] for first in range(0, devices, members)]
    grouped = records.reshape(members, segments * channels // members, span)
    regrouped = lax.all_to_all(
        grouped, "chan", split_axis=0, concat_axis=0, axis_index_groups=groups, tiled=True
    )
    parts = []
    for first, last in ((0, FIRST_TILES), (FIRST_TILES, COLUMN_TILES)):
        sums = transform(share, regrouped, tables(samples, span), senders, first, last)
        parts += [sums[0]] + [exchange(sums[k], k * members) for k in range(1, SHARES)]
    white = whiten(flags, parts)

    far = devices // 8
    line = jnp.stack([white] + [exchange(white, 8 * k) for k in range(1, far)])
    plane = [line] + [exchange(line, 2 * k) for k in range(1, 4)]
    swapped = [exchange(block, 1) for block in plane]
    ids = source_ids.reshape(-1, 1)
    common = place.reshape(1), weights, ids
    shape = segments, channels, devices
    before = correlate(0, *common, plane, shape)
    inverse = inverse_table(samples)
    return correlate(1, *common, swapped, shape, before, inverse)


def solution(mesh):
    return jax.shard_map(
        per_device,
        mesh=mesh,
        in_specs=(P("group", None, "chan"), P("group", "chan"), P("group")),
        out_specs=P("group", "chan", None),
        check_vma=False,
    )
```

```python
import functools
import math

import jax
import jax.numpy as jnp
import ml_dtypes
import numpy as np
from jax import lax
from jax.experimental import pallas as pl
from jax.experimental.pallas import tpu as pltpu
from jax.sharding import PartitionSpec as P

BAND = 600
SOURCES = 64
HALF_LAG = 500

lowest_bin = 8
floor_share = 0.05
epsilon = 1e-06

PART = 640
WIDTH = 2 * PART
LAGS = 2 * HALF_LAG + 1
LAG_TILES = -(-LAGS // 128)
SHARES = 2
COLUMN_TILES = WIDTH // 128
FIRST_TILES = 6
FLAG_TILE = BAND // 128 * 128
FLAG_LANE = BAND - FLAG_TILE


def angles(phase, samples):
    step = np.float32(2.0 * math.pi / samples)
    return (phase.astype(np.float32) * step).astype(np.float64)


def cos_sin(samples):
    angle = angles(np.arange(samples), samples)
    return np.cos(angle).astype(np.float32), (-np.sin(angle)).astype(np.float32)


def lane_tiles(table):
    tiled = table.reshape(*table.shape[:-1], -1, 128)
    return np.ascontiguousarray(np.moveaxis(tiled, -2, -3))


@functools.lru_cache(maxsize=None)
def tables(samples, span):
    bins = lowest_bin + np.arange(BAND)
    cosine, sine = cos_sin(samples)
    phase = np.arange(samples)[:, None] * bins[None, :] % samples
    forward = np.zeros((samples, WIDTH), ml_dtypes.bfloat16)
    forward[:, :BAND] = cosine.astype(ml_dtypes.bfloat16)[phase]
    forward[:, PART : PART + BAND] = sine.astype(ml_dtypes.bfloat16)[phase]
    return lane_tiles(forward.reshape(-1, span, WIDTH)).reshape(-1, 128)


@functools.lru_cache(maxsize=None)
def inverse_table(samples):
    bins = lowest_bin + np.arange(BAND)
    cosine, sine = cos_sin(samples)
    factor = np.float32(1.0 / math.sqrt(BAND))
    phase = bins[:, None] * (np.arange(LAGS) - HALF_LAG)[None, :] % samples
    inverse = np.zeros((WIDTH, LAG_TILES * 128), ml_dtypes.bfloat16)
    inverse[:BAND, :LAGS] = (cosine * factor).astype(ml_dtypes.bfloat16)[phase]
    inverse[PART : PART + BAND, :LAGS] = (sine * factor).astype(ml_dtypes.bfloat16)[phase]
    return lane_tiles(inverse).reshape(-1, 128)


def balanced_steps(chips):
    pairs = [step for low in range(1, chips // 2) for step in (low, low ^ (chips - 1))]
    return pairs + [chips - 1]


def transform_kernel(first, place_ref, table_ref, *rest):
    records, rest = rest[: -SHARES - 2], rest[-SHARES - 2 :]
    outs, (tiles_ref, sems) = rest[:-2], rest[-2:]
    _, rows, span = records[0].shape
    members, lines, _ = tiles_ref.shape
    columns = lines // span
    copies = []
    for index in range(members):
        start = ((place_ref[0] ^ index) * COLUMN_TILES + first) * span
        source = table_ref.at[pl.ds(pl.multiple_of(start, span), lines)]
        copies.append(pltpu.make_async_copy(source, tiles_ref.at[index], sems.at[index]))
        copies[-1].start()
    total = jnp.zeros((rows, columns * 128), jnp.float32)
    for index in range(members):
        copies[index].wait()
        tiles = [tiles_ref[index, tile * span : (tile + 1) * span] for tile in range(columns)]
        total += jnp.dot(
            records[index // 2][index % 2],
            jnp.concatenate(tiles, axis=1),
            preferred_element_type=jnp.float32,
        )
    kept = rows // len(outs)
    for step, out in enumerate(outs):
        chosen = total[:kept]
        for owner in range(1, len(outs)):
            mine = (place_ref[0] // members ^ step) == owner
            chosen = jnp.where(mine, total[owner * kept : (owner + 1) * kept], chosen)
        out[...] = chosen


def transform(place, table, records, first, last):
    _, rows, span = records[0].shape
    members = 2 * len(records)
    columns = last - first
    vmem = pl.BlockSpec(memory_space=pltpu.VMEM)
    shape = jax.ShapeDtypeStruct((rows // SHARES, columns * 128), jnp.float32)
    return pl.pallas_call(
        functools.partial(transform_kernel, first),
        in_specs=[
            pl.BlockSpec(memory_space=pltpu.SMEM),
            pl.BlockSpec(memory_space=pltpu.HBM),
        ]
        + [vmem] * len(records),
        out_specs=[vmem] * SHARES,
        out_shape=[shape] * SHARES,
        scratch_shapes=[
            pltpu.VMEM((members, columns * span, 128), jnp.bfloat16),
            pltpu.SemaphoreType.DMA((members,)),
        ],
        compiler_params=pltpu.CompilerParams(vmem_limit_bytes=32 * 2**20),
        cost_estimate=pl.CostEstimate(
            flops=2 * rows * members * span * columns * 128,
            bytes_accessed=2 * members * span * columns * 128,
            transcendentals=0,
        ),
        name="transform",
    )(place, table, *records)


def whiten_kernel(flags_ref, *rest):
    parts, white_ref = rest[:-1], rest[-1]
    sums = []
    for first in range(0, len(parts), SHARES):
        sums.append(parts[first][...])
        for part in parts[first + 1 : first + SHARES]:
            sums[-1] += part[...]
    total = jnp.concatenate(sums, axis=1)
    real_part, imag_part = total[:, :PART], total[:, PART:]
    power = real_part * real_part + imag_part * imag_part
    level = jnp.sum(power, axis=1, keepdims=True) * (1.0 / BAND)
    factor = lax.rsqrt(power + floor_share * level + epsilon)
    white_ref[:, :PART] = (real_part * factor).astype(jnp.bfloat16)
    white_ref[:, PART:] = (imag_part * factor).astype(jnp.bfloat16)
    rows = total.shape[0]
    lane = lax.broadcasted_iota(jnp.int32, (rows, 128), 1)
    held = (lane >= FLAG_LANE) & (lane < FLAG_LANE + flags_ref.shape[1])
    tile = (real_part * factor)[:, FLAG_TILE : FLAG_TILE + 128]
    flags = jnp.concatenate(
        [
            jnp.zeros((1, FLAG_LANE), jnp.float32),
            flags_ref[...],
            jnp.zeros((1, 128 - FLAG_LANE - flags_ref.shape[1]), jnp.float32),
        ],
        axis=1,
    )
    white_ref[:, FLAG_TILE : FLAG_TILE + 128] = jnp.where(held, flags, tile).astype(jnp.bfloat16)


def whiten(flags, parts):
    return pl.pallas_call(
        whiten_kernel,
        out_shape=jax.ShapeDtypeStruct((parts[0].shape[0], WIDTH), jnp.bfloat16),
        compiler_params=pltpu.CompilerParams(vmem_limit_bytes=16 * 2**20),
        name="whiten",
    )(flags, *parts)


def correlate_kernel(shape, core, place_ref, flags_ref, ids_ref, *rest):
    segments, channels, devices, blocks = shape
    blocks, rest = rest[:blocks], rest[blocks:]
    if core:
        before_ref, table_ref, out_ref = rest[:3]
        held_ref, panel_ref, receivers_ref, inverse_ref, stacked_ref, sem = rest[3:]
        fetch = pltpu.make_async_copy(table_ref, inverse_ref, sem)
        fetch.start()
    else:
        out_ref, held_ref, panel_ref, receivers_ref = rest
    rows = held_ref.shape[1]
    members = devices // SHARES
    parts = members // segments
    ch_local = channels // devices
    ch_chip = 2 * ch_local
    place = place_ref[0]
    parity = place % 2 ^ core
    ids = ids_ref[...]
    sources = ids.shape[0]

    def position(device):
        member = device % members
        return (member // 2) * SHARES + device // members

    for index, block in enumerate(blocks):
        for line in range(block.shape[0]):
            device = place ^ (line * 8 + index * 2 + core)
            held_ref[position(device)] = block[line]

    tails = held_ref[:, :, FLAG_TILE : FLAG_TILE + 128].reshape(held_ref.shape[0] * rows, 128)
    column = lax.broadcasted_iota(jnp.int32, (sources, tails.shape[0]), 1)
    choice = (column == position(ids // ch_chip * 2 + parity) * rows).astype(jnp.bfloat16)
    tail = jnp.dot(choice, tails, preferred_element_type=jnp.float32)
    lane = lax.broadcasted_iota(jnp.int32, (sources, 128), 1)

    channel = lax.broadcasted_iota(jnp.int32, (sources, channels), 1)
    pick_sources = (channel == ids).astype(jnp.bfloat16)
    line = lax.broadcasted_iota(jnp.int32, (16, channels), 0)
    channel = lax.broadcasted_iota(jnp.int32, (16, channels), 1)
    pick_own = ((channel == place * ch_local + line) & (line < ch_local)).astype(jnp.bfloat16)
    pick = jnp.concatenate([pick_sources, pick_own], axis=0)

    counts = [jnp.zeros((sources, 1), jnp.float32) for _ in range(ch_local)]
    per_segment = channels // rows
    for g in range(segments // 2):
        segment = held_ref[g * per_segment : (g + 1) * per_segment].reshape(channels, WIDTH)
        picked = jnp.dot(pick, segment, preferred_element_type=jnp.float32)
        mine = lane == FLAG_LANE + g * ch_chip + ids % ch_chip
        weight = jnp.sum(jnp.where(mine, tail, 0.0), axis=1, keepdims=True)
        panel_ref[g] = picked[:sources] * weight
        receivers_ref[g] = picked[sources:]
        for c in range(ch_local):
            counts[c] += weight * flags_ref[2 * g + parity, c]

    shares = [None] * ch_local
    for start in [FLAG_TILE] + [start for start in range(0, PART, 128) if start != FLAG_TILE]:
        re = slice(start, start + 128)
        im = slice(PART + start, PART + start + 128)
        for c in range(ch_local):
            real_sum = jnp.zeros((sources, 128), jnp.float32)
            imag_sum = jnp.zeros((sources, 128), jnp.float32)
            for g in range(segments // 2):
                flag = flags_ref[2 * g + parity, c]
                rec_real = receivers_ref[g, c : c + 1, re] * flag
                rec_imag = receivers_ref[g, c : c + 1, im] * flag
                src_real, src_imag = panel_ref[g, :, re], panel_ref[g, :, im]
                real_sum += src_real * rec_real + src_imag * rec_imag
                imag_sum += src_imag * rec_real - src_real * rec_imag
            if start == FLAG_TILE:
                real_sum = jnp.where(lane == FLAG_LANE, counts[c], real_sum)
            if not core:
                out_ref[c, :, re] = real_sum
                out_ref[c, :, im] = imag_sum
                continue
            real_sum += before_ref[c, :, re]
            imag_sum += before_ref[c, :, im]
            if start == FLAG_TILE:
                total = real_sum[:, FLAG_LANE : FLAG_LANE + 1]
                shares[c] = 1.0 / jnp.maximum(total, 1.0)
            lines = pl.ds(c, sources, stride=ch_local)
            stacked_ref[start // 128, lines, :] = real_sum * shares[c]
            stacked_ref[(PART + start) // 128, lines, :] = imag_sum * shares[c]
    if core:
        fetch.wait()
        tiles = [inverse_ref[tile * WIDTH : (tile + 1) * WIDTH] for tile in range(LAG_TILES)]
        lags = jnp.dot(
            jnp.concatenate([stacked_ref[i] for i in range(COLUMN_TILES)], axis=1).astype(
                jnp.bfloat16
            ),
            jnp.concatenate(tiles, axis=1),
            preferred_element_type=jnp.float32,
        )
        out_ref[...] = lags.reshape(sources, ch_local, LAG_TILES * 128)[:, :, :LAGS]


def correlate(core, place, weights, ids, blocks, shape, before=None, table=None):
    segments, channels, devices = shape
    rows = blocks[0].shape[1]
    ch_local = channels // devices
    sources = ids.shape[0]
    smem = pl.BlockSpec(memory_space=pltpu.SMEM)
    vmem = pl.BlockSpec(memory_space=pltpu.VMEM)
    in_specs = [smem, smem, vmem] + [vmem] * len(blocks)
    scratch = [
        pltpu.VMEM((devices // 2, rows, WIDTH), jnp.bfloat16),
        pltpu.VMEM((segments // 2, sources, WIDTH), jnp.float32),
        pltpu.VMEM((segments // 2, 16, WIDTH), jnp.float32),
    ]
    if core:
        in_specs += [vmem, pl.BlockSpec(memory_space=pltpu.HBM)]
        scratch += [
            pltpu.VMEM(table.shape, jnp.bfloat16),
            pltpu.VMEM((COLUMN_TILES, sources * ch_local, 128), jnp.float32),
            pltpu.SemaphoreType.DMA,
        ]
    out = (sources, ch_local, LAGS) if core else (ch_local, sources, WIDTH)
    return pl.pallas_call(
        functools.partial(correlate_kernel, (*shape, len(blocks)), core),
        in_specs=in_specs,
        out_specs=vmem,
        out_shape=jax.ShapeDtypeStruct(out, jnp.float32),
        scratch_shapes=scratch,
        compiler_params=pltpu.CompilerParams(vmem_limit_bytes=32 * 2**20),
        cost_estimate=pl.CostEstimate(
            flops=sources * channels * WIDTH * segments,
            bytes_accessed=2 * (segments // 2) * channels * WIDTH,
            transcendentals=0,
        ),
        name="correlate",
    )(place, weights, ids, *blocks, *([before, table] if core else []))


def per_device(records, valid_flags, source_ids):
    segments, channels, span = records.shape
    devices = lax.axis_size("chan")
    members = devices // SHARES
    samples = span * devices
    place = lax.axis_index("chan")
    weights = valid_flags.astype(jnp.float32)

    def exchange(block, bits):
        return lax.ppermute(block, "chan", [(i, i ^ bits) for i in range(devices)])

    parity = place % 2
    partner = exchange(weights, 1)
    chip = jnp.where(
        parity == 0,
        jnp.concatenate([weights, partner], axis=1),
        jnp.concatenate([partner, weights], axis=1),
    )
    chip = chip.reshape(segments // 2, 2, -1)
    flags = lax.dynamic_index_in_dim(chip, parity, 1, keepdims=False).reshape(1, -1)

    chips = members // 2
    grouped = records.reshape(segments // 2, 2, -1, span)
    kept, handed = (
        lax.dynamic_index_in_dim(grouped, side, 1, keepdims=False).reshape(chips, -1, span)
        for side in (parity, 1 - parity)
    )
    pair = kept, exchange(handed, 1)
    chip_place = place % members // 2
    arrived = {}
    for step in [0] + balanced_steps(chips):
        block = jnp.stack([lax.dynamic_index_in_dim(p, chip_place ^ step, 0, False) for p in pair])
        arrived[step] = exchange(block, 2 * step) if step else block
    blocks = [arrived[step] for step in range(chips)]
    me = place.reshape(1)
    parts = []
    for first, last in ((0, FIRST_TILES), (FIRST_TILES, COLUMN_TILES)):
        sums = transform(me, tables(samples, span), blocks, first, last)
        parts += [sums[0]] + [exchange(sums[k], k * members) for k in range(1, SHARES)]
    white = whiten(flags, parts)

    far = devices // 8
    line = jnp.stack([white] + [exchange(white, 8 * k) for k in range(1, far)])
    plane = [line] + [exchange(line, 2 * k) for k in range(1, 4)]
    swapped = [exchange(block, 1) for block in plane]
    ids = source_ids.reshape(-1, 1)
    common = me, weights, ids
    shape = segments, channels, devices
    before = correlate(0, *common, plane, shape)
    inverse = inverse_table(samples)
    return correlate(1, *common, swapped, shape, before, inverse)


def solution(mesh):
    return jax.shard_map(
        per_device,
        mesh=mesh,
        in_specs=(P("group", None, "chan"), P("group", "chan"), P("group")),
        out_specs=P("group", "chan", None),
        check_vma=False,
    )
```

```python
import functools
import math

import jax
import jax.numpy as jnp
import ml_dtypes
import numpy as np
from jax import lax
from jax.experimental import pallas as pl
from jax.experimental.pallas import tpu as pltpu
from jax.sharding import PartitionSpec as P

BAND = 600
SOURCES = 64
HALF_LAG = 500

lowest_bin = 8
floor_share = 0.05
epsilon = 1e-06

PART = 640
WIDTH = 2 * PART
LAGS = 2 * HALF_LAG + 1
LAG_TILES = -(-LAGS // 128)
SHARES = 2
COLUMN_TILES = WIDTH // 128
FIRST_TILES = 6
FLAG_TILE = BAND // 128 * 128
FLAG_LANE = BAND - FLAG_TILE


def angles(phase, samples):
    step = np.float32(2.0 * math.pi / samples)
    return (phase.astype(np.float32) * step).astype(np.float64)


def cos_sin(samples):
    angle = angles(np.arange(samples), samples)
    return np.cos(angle).astype(np.float32), (-np.sin(angle)).astype(np.float32)


def lane_tiles(table):
    tiled = table.reshape(*table.shape[:-1], -1, 128)
    return np.ascontiguousarray(np.moveaxis(tiled, -2, -3))


@functools.lru_cache(maxsize=None)
def tables(samples, span):
    bins = lowest_bin + np.arange(BAND)
    cosine, sine = cos_sin(samples)
    phase = np.arange(samples)[:, None] * bins[None, :] % samples
    forward = np.zeros((samples, WIDTH), ml_dtypes.bfloat16)
    forward[:, :BAND] = cosine.astype(ml_dtypes.bfloat16)[phase]
    forward[:, PART : PART + BAND] = sine.astype(ml_dtypes.bfloat16)[phase]
    return lane_tiles(forward.reshape(-1, span, WIDTH)).reshape(-1, 128)


@functools.lru_cache(maxsize=None)
def inverse_table(samples):
    bins = lowest_bin + np.arange(BAND)
    cosine, sine = cos_sin(samples)
    factor = np.float32(1.0 / math.sqrt(BAND))
    phase = bins[:, None] * (np.arange(LAGS) - HALF_LAG)[None, :] % samples
    inverse = np.zeros((WIDTH, LAG_TILES * 128), ml_dtypes.bfloat16)
    inverse[:BAND, :LAGS] = (cosine * factor).astype(ml_dtypes.bfloat16)[phase]
    inverse[PART : PART + BAND, :LAGS] = (sine * factor).astype(ml_dtypes.bfloat16)[phase]
    return lane_tiles(inverse).reshape(-1, 128)


def balanced_steps(chips):
    steps = [chips - 1]
    for low in range(1, chips // 2):
        steps += [low, low ^ (chips - 1)]
    return steps


def transform_kernel(steps, first, started, place_ref, table_ref, *rest):
    records, rest = rest[: len(steps)], rest[len(steps) :]
    if started:
        before_ref, rest = rest[0], rest[1:]
    outs, (tiles_ref, sems) = rest[:-2], rest[-2:]
    _, rows, span = records[0].shape
    blocks, lines, _ = tiles_ref.shape
    columns = lines // span
    copies = []
    for index in range(blocks):
        sender = place_ref[0] ^ (2 * steps[index // 2] + index % 2)
        start = (sender * COLUMN_TILES + first) * span
        source = table_ref.at[pl.ds(pl.multiple_of(start, span), lines)]
        copies.append(pltpu.make_async_copy(source, tiles_ref.at[index], sems.at[index]))
        copies[-1].start()
    if started:
        total = before_ref[:, first * 128 : (first + columns) * 128]
    else:
        total = jnp.zeros((rows, columns * 128), jnp.float32)
    for index in range(blocks):
        copies[index].wait()
        tiles = [tiles_ref[index, tile * span : (tile + 1) * span] for tile in range(columns)]
        total += jnp.dot(
            records[index // 2][index % 2],
            jnp.concatenate(tiles, axis=1),
            preferred_element_type=jnp.float32,
        )
    if len(outs) == 1:
        outs[0][...] = total
    else:
        kept = rows // 2
        mine = place_ref[0] < table_ref.shape[0] // (2 * COLUMN_TILES * span)
        outs[0][...] = jnp.where(mine, total[:kept], total[kept:])
        outs[1][...] = jnp.where(mine, total[kept:], total[:kept])


def transform(place, table, arrived, steps, first, last, before=None):
    records = [arrived[step] for step in steps]
    _, rows, span = records[0].shape
    columns = last - first
    blocks = 2 * len(steps)
    vmem = pl.BlockSpec(memory_space=pltpu.VMEM)
    started = before is not None
    outs = 2 if started else 1
    return pl.pallas_call(
        functools.partial(transform_kernel, steps, first, started),
        in_specs=[
            pl.BlockSpec(memory_space=pltpu.SMEM),
            pl.BlockSpec(memory_space=pltpu.HBM),
        ]
        + [vmem] * (len(records) + started),
        out_specs=[vmem] * outs,
        out_shape=[jax.ShapeDtypeStruct((rows // outs, columns * 128), jnp.float32)] * outs,
        scratch_shapes=[
            pltpu.VMEM((blocks, columns * span, 128), jnp.bfloat16),
            pltpu.SemaphoreType.DMA((blocks,)),
        ],
        compiler_params=pltpu.CompilerParams(vmem_limit_bytes=24 * 2**20),
        cost_estimate=pl.CostEstimate(
            flops=2 * rows * blocks * span * columns * 128,
            bytes_accessed=2 * blocks * span * columns * 128,
            transcendentals=0,
        ),
        name="transform",
    )(place, table, *records, *([before] if started else []))


def whiten_kernel(flags_ref, *rest):
    parts, white_ref = rest[:-1], rest[-1]
    sums = []
    for first in range(0, len(parts), SHARES):
        sums.append(parts[first][...])
        for part in parts[first + 1 : first + SHARES]:
            sums[-1] += part[...]
    total = jnp.concatenate(sums, axis=1)
    real_part, imag_part = total[:, :PART], total[:, PART:]
    power = real_part * real_part + imag_part * imag_part
    level = jnp.sum(power, axis=1, keepdims=True) * (1.0 / BAND)
    factor = lax.rsqrt(power + floor_share * level + epsilon)
    white_ref[:, :PART] = (real_part * factor).astype(jnp.bfloat16)
    white_ref[:, PART:] = (imag_part * factor).astype(jnp.bfloat16)
    rows = total.shape[0]
    lane = lax.broadcasted_iota(jnp.int32, (rows, 128), 1)
    held = (lane >= FLAG_LANE) & (lane < FLAG_LANE + flags_ref.shape[1])
    tile = (real_part * factor)[:, FLAG_TILE : FLAG_TILE + 128]
    flags = jnp.concatenate(
        [
            jnp.zeros((1, FLAG_LANE), jnp.float32),
            flags_ref[...],
            jnp.zeros((1, 128 - FLAG_LANE - flags_ref.shape[1]), jnp.float32),
        ],
        axis=1,
    )
    white_ref[:, FLAG_TILE : FLAG_TILE + 128] = jnp.where(held, flags, tile).astype(jnp.bfloat16)


def whiten(flags, parts):
    return pl.pallas_call(
        whiten_kernel,
        out_shape=jax.ShapeDtypeStruct((parts[0].shape[0], WIDTH), jnp.bfloat16),
        compiler_params=pltpu.CompilerParams(vmem_limit_bytes=16 * 2**20),
        name="whiten",
    )(flags, *parts)


def correlate_kernel(shape, core, place_ref, flags_ref, ids_ref, *rest):
    segments, channels, devices, blocks = shape
    blocks, rest = rest[:blocks], rest[blocks:]
    if core:
        before_ref, table_ref, out_ref = rest[:3]
        held_ref, panel_ref, receivers_ref, inverse_ref, stacked_ref, sem = rest[3:]
        fetch = pltpu.make_async_copy(table_ref, inverse_ref, sem)
        fetch.start()
    else:
        out_ref, held_ref, panel_ref, receivers_ref = rest
    rows = held_ref.shape[1]
    members = devices // SHARES
    parts = members // segments
    ch_local = channels // devices
    ch_chip = 2 * ch_local
    place = place_ref[0]
    parity = place % 2 ^ core
    ids = ids_ref[...]
    sources = ids.shape[0]

    def position(device):
        member = device % members
        return (member // 2) * SHARES + device // members

    for index, block in enumerate(blocks):
        for line in range(block.shape[0]):
            device = place ^ (line * 8 + index * 2 + core)
            held_ref[position(device)] = block[line]

    tails = held_ref[:, :, FLAG_TILE : FLAG_TILE + 128].reshape(held_ref.shape[0] * rows, 128)
    column = lax.broadcasted_iota(jnp.int32, (sources, tails.shape[0]), 1)
    choice = (column == position(ids // ch_chip * 2 + parity) * rows).astype(jnp.bfloat16)
    tail = jnp.dot(choice, tails, preferred_element_type=jnp.float32)
    lane = lax.broadcasted_iota(jnp.int32, (sources, 128), 1)

    channel = lax.broadcasted_iota(jnp.int32, (sources, channels), 1)
    pick_sources = (channel == ids).astype(jnp.bfloat16)
    line = lax.broadcasted_iota(jnp.int32, (16, channels), 0)
    channel = lax.broadcasted_iota(jnp.int32, (16, channels), 1)
    pick_own = ((channel == place * ch_local + line) & (line < ch_local)).astype(jnp.bfloat16)
    pick = jnp.concatenate([pick_sources, pick_own], axis=0)

    counts = [jnp.zeros((sources, 1), jnp.float32) for _ in range(ch_local)]
    per_segment = channels // rows
    for g in range(segments // 2):
        segment = held_ref[g * per_segment : (g + 1) * per_segment].reshape(channels, WIDTH)
        picked = jnp.dot(pick, segment, preferred_element_type=jnp.float32)
        mine = lane == FLAG_LANE + g * ch_chip + ids % ch_chip
        weight = jnp.sum(jnp.where(mine, tail, 0.0), axis=1, keepdims=True)
        panel_ref[g] = picked[:sources] * weight
        receivers_ref[g] = picked[sources:]
        for c in range(ch_local):
            counts[c] += weight * flags_ref[2 * g + parity, c]

    shares = [None] * ch_local
    for start in [FLAG_TILE] + [start for start in range(0, PART, 128) if start != FLAG_TILE]:
        re = slice(start, start + 128)
        im = slice(PART + start, PART + start + 128)
        for c in range(ch_local):
            real_sum = jnp.zeros((sources, 128), jnp.float32)
            imag_sum = jnp.zeros((sources, 128), jnp.float32)
            for g in range(segments // 2):
                flag = flags_ref[2 * g + parity, c]
                rec_real = receivers_ref[g, c : c + 1, re] * flag
                rec_imag = receivers_ref[g, c : c + 1, im] * flag
                src_real, src_imag = panel_ref[g, :, re], panel_ref[g, :, im]
                real_sum += src_real * rec_real + src_imag * rec_imag
                imag_sum += src_imag * rec_real - src_real * rec_imag
            if start == FLAG_TILE:
                real_sum = jnp.where(lane == FLAG_LANE, counts[c], real_sum)
            if not core:
                out_ref[c, :, re] = real_sum
                out_ref[c, :, im] = imag_sum
                continue
            real_sum += before_ref[c, :, re]
            imag_sum += before_ref[c, :, im]
            if start == FLAG_TILE:
                total = real_sum[:, FLAG_LANE : FLAG_LANE + 1]
                shares[c] = 1.0 / jnp.maximum(total, 1.0)
            lines = pl.ds(c, sources, stride=ch_local)
            stacked_ref[start // 128, lines, :] = real_sum * shares[c]
            stacked_ref[(PART + start) // 128, lines, :] = imag_sum * shares[c]
    if core:
        fetch.wait()
        tiles = [inverse_ref[tile * WIDTH : (tile + 1) * WIDTH] for tile in range(LAG_TILES)]
        lags = jnp.dot(
            jnp.concatenate([stacked_ref[i] for i in range(COLUMN_TILES)], axis=1).astype(
                jnp.bfloat16
            ),
            jnp.concatenate(tiles, axis=1),
            preferred_element_type=jnp.float32,
        )
        out_ref[...] = lags.reshape(sources, ch_local, LAG_TILES * 128)[:, :, :LAGS]


def correlate(core, place, weights, ids, blocks, shape, before=None, table=None):
    segments, channels, devices = shape
    rows = blocks[0].shape[1]
    ch_local = channels // devices
    sources = ids.shape[0]
    smem = pl.BlockSpec(memory_space=pltpu.SMEM)
    vmem = pl.BlockSpec(memory_space=pltpu.VMEM)
    in_specs = [smem, smem, vmem] + [vmem] * len(blocks)
    scratch = [
        pltpu.VMEM((devices // 2, rows, WIDTH), jnp.bfloat16),
        pltpu.VMEM((segments // 2, sources, WIDTH), jnp.float32),
        pltpu.VMEM((segments // 2, 16, WIDTH), jnp.float32),
    ]
    if core:
        in_specs += [vmem, pl.BlockSpec(memory_space=pltpu.HBM)]
        scratch += [
            pltpu.VMEM(table.shape, jnp.bfloat16),
            pltpu.VMEM((COLUMN_TILES, sources * ch_local, 128), jnp.float32),
            pltpu.SemaphoreType.DMA,
        ]
    out = (sources, ch_local, LAGS) if core else (ch_local, sources, WIDTH)
    return pl.pallas_call(
        functools.partial(correlate_kernel, (*shape, len(blocks)), core),
        in_specs=in_specs,
        out_specs=vmem,
        out_shape=jax.ShapeDtypeStruct(out, jnp.float32),
        scratch_shapes=scratch,
        compiler_params=pltpu.CompilerParams(vmem_limit_bytes=32 * 2**20),
        cost_estimate=pl.CostEstimate(
            flops=sources * channels * WIDTH * segments,
            bytes_accessed=2 * (segments // 2) * channels * WIDTH,
            transcendentals=0,
        ),
        name="correlate",
    )(place, weights, ids, *blocks, *([before, table] if core else []))


def per_device(records, valid_flags, source_ids):
    segments, channels, span = records.shape
    devices = lax.axis_size("chan")
    members = devices // SHARES
    samples = span * devices
    place = lax.axis_index("chan")
    weights = valid_flags.astype(jnp.float32)

    def exchange(block, bits):
        return lax.ppermute(block, "chan", [(i, i ^ bits) for i in range(devices)])

    parity = place % 2
    partner = exchange(weights, 1)
    chip = jnp.where(
        parity == 0,
        jnp.concatenate([weights, partner], axis=1),
        jnp.concatenate([partner, weights], axis=1),
    )
    chip = chip.reshape(segments // 2, 2, -1)
    flags = lax.dynamic_index_in_dim(chip, parity, 1, keepdims=False).reshape(1, -1)

    chips = members // 2
    grouped = records.reshape(segments // 2, 2, -1, span)
    kept, handed = (
        lax.dynamic_index_in_dim(grouped, side, 1, keepdims=False).reshape(chips, -1, span)
        for side in (parity, 1 - parity)
    )
    pair = kept, exchange(handed, 1)
    chip_place = place % members // 2
    steps = [0] + balanced_steps(chips)
    arrived = {}
    for step in steps:
        block = jnp.stack([lax.dynamic_index_in_dim(p, chip_place ^ step, 0, False) for p in pair])
        arrived[step] = exchange(block, 2 * step) if step else block
    me = place.reshape(1)
    table = tables(samples, span)
    early, late = steps[: chips // 2], steps[chips // 2 :]
    before = transform(me, table, arrived, early, 0, COLUMN_TILES)[0]
    parts = []
    for first, last in ((0, FIRST_TILES), (FIRST_TILES, COLUMN_TILES)):
        own, other = transform(me, table, arrived, late, first, last, before)
        parts += [own, exchange(other, members)]
    white = whiten(flags, parts)

    far = devices // 8
    line = jnp.stack([white] + [exchange(white, 8 * k) for k in range(1, far)])
    plane = [line] + [exchange(line, 2 * k) for k in range(1, 4)]
    swapped = [exchange(block, 1) for block in plane]
    ids = source_ids.reshape(-1, 1)
    common = me, weights, ids
    shape = segments, channels, devices
    before = correlate(0, *common, plane, shape)
    inverse = inverse_table(samples)
    return correlate(1, *common, swapped, shape, before, inverse)


def solution(mesh):
    return jax.shard_map(
        per_device,
        mesh=mesh,
        in_specs=(P("group", None, "chan"), P("group", "chan"), P("group")),
        out_specs=P("group", "chan", None),
        check_vma=False,
    )
```

```python
import functools
import math

import jax
import jax.numpy as jnp
import ml_dtypes
import numpy as np
from jax import lax
from jax.experimental import pallas as pl
from jax.experimental.pallas import tpu as pltpu
from jax.sharding import PartitionSpec as P

BAND = 600
SOURCES = 64
HALF_LAG = 500

lowest_bin = 8
floor_share = 0.05
epsilon = 1e-06

PART = 640
WIDTH = 2 * PART
LAGS = 2 * HALF_LAG + 1
LAG_TILES = -(-LAGS // 128)
SHARES = 2
COLUMN_TILES = WIDTH // 128
FIRST_TILES = 6
FLAG_TILE = BAND // 128 * 128
FLAG_LANE = BAND - FLAG_TILE


def angles(phase, samples):
    step = np.float32(2.0 * math.pi / samples)
    return (phase.astype(np.float32) * step).astype(np.float64)


def cos_sin(samples):
    angle = angles(np.arange(samples), samples)
    return np.cos(angle).astype(np.float32), (-np.sin(angle)).astype(np.float32)


def lane_tiles(table):
    tiled = table.reshape(*table.shape[:-1], -1, 128)
    return np.ascontiguousarray(np.moveaxis(tiled, -2, -3))


@functools.lru_cache(maxsize=None)
def tables(samples, span):
    bins = lowest_bin + np.arange(BAND)
    cosine, sine = cos_sin(samples)
    phase = np.arange(samples)[:, None] * bins[None, :] % samples
    forward = np.zeros((samples, WIDTH), ml_dtypes.bfloat16)
    forward[:, :BAND] = cosine.astype(ml_dtypes.bfloat16)[phase]
    forward[:, PART : PART + BAND] = sine.astype(ml_dtypes.bfloat16)[phase]
    return lane_tiles(forward.reshape(-1, span, WIDTH)).reshape(-1, 128)


@functools.lru_cache(maxsize=None)
def inverse_table(samples):
    bins = lowest_bin + np.arange(BAND)
    cosine, sine = cos_sin(samples)
    factor = np.float32(1.0 / math.sqrt(BAND))
    phase = bins[:, None] * (np.arange(LAGS) - HALF_LAG)[None, :] % samples
    inverse = np.zeros((WIDTH, LAG_TILES * 128), ml_dtypes.bfloat16)
    inverse[:BAND, :LAGS] = (cosine * factor).astype(ml_dtypes.bfloat16)[phase]
    inverse[PART : PART + BAND, :LAGS] = (sine * factor).astype(ml_dtypes.bfloat16)[phase]
    return lane_tiles(inverse).reshape(-1, 128)


def balanced_steps(chips):
    steps = [chips - 1]
    for low in range(1, chips // 2):
        steps += [low, low ^ (chips - 1)]
    return steps


def transform_kernel(steps, first, started, place_ref, table_ref, *rest):
    records, rest = rest[: len(steps)], rest[len(steps) :]
    if started:
        before_ref, rest = rest[0], rest[1:]
    outs, (tiles_ref, sems) = rest[:-2], rest[-2:]
    _, rows, span = records[0].shape
    blocks, lines, _ = tiles_ref.shape
    columns = lines // span
    copies = []
    for index in range(blocks):
        sender = place_ref[0] ^ (2 * steps[index // 2] + index % 2)
        start = (sender * COLUMN_TILES + first) * span
        source = table_ref.at[pl.ds(pl.multiple_of(start, span), lines)]
        copies.append(pltpu.make_async_copy(source, tiles_ref.at[index], sems.at[index]))
        copies[-1].start()
    if started:
        total = before_ref[:, first * 128 : (first + columns) * 128]
    else:
        total = jnp.zeros((rows, columns * 128), jnp.float32)
    for index in range(blocks):
        copies[index].wait()
        tiles = [tiles_ref[index, tile * span : (tile + 1) * span] for tile in range(columns)]
        total += jnp.dot(
            records[index // 2][index % 2],
            jnp.concatenate(tiles, axis=1),
            preferred_element_type=jnp.float32,
        )
    if len(outs) == 1:
        outs[0][...] = total
    else:
        kept = rows // 2
        mine = place_ref[0] < table_ref.shape[0] // (2 * COLUMN_TILES * span)
        outs[0][...] = jnp.where(mine, total[:kept], total[kept:])
        outs[1][...] = jnp.where(mine, total[kept:], total[:kept])


def transform(place, table, arrived, steps, first, last, before=None):
    records = [arrived[step] for step in steps]
    _, rows, span = records[0].shape
    columns = last - first
    blocks = 2 * len(steps)
    vmem = pl.BlockSpec(memory_space=pltpu.VMEM)
    started = before is not None
    outs = 2 if started else 1
    return pl.pallas_call(
        functools.partial(transform_kernel, steps, first, started),
        in_specs=[
            pl.BlockSpec(memory_space=pltpu.SMEM),
            pl.BlockSpec(memory_space=pltpu.HBM),
        ]
        + [vmem] * (len(records) + started),
        out_specs=[vmem] * outs,
        out_shape=[jax.ShapeDtypeStruct((rows // outs, columns * 128), jnp.float32)] * outs,
        scratch_shapes=[
            pltpu.VMEM((blocks, columns * span, 128), jnp.bfloat16),
            pltpu.SemaphoreType.DMA((blocks,)),
        ],
        compiler_params=pltpu.CompilerParams(vmem_limit_bytes=24 * 2**20),
        cost_estimate=pl.CostEstimate(
            flops=2 * rows * blocks * span * columns * 128,
            bytes_accessed=2 * blocks * span * columns * 128,
            transcendentals=0,
        ),
        name="transform",
    )(place, table, *records, *([before] if started else []))


def whiten_kernel(flags_ref, *rest):
    parts, white_ref = rest[:-1], rest[-1]
    sums = []
    for first in range(0, len(parts), SHARES):
        sums.append(parts[first][...])
        for part in parts[first + 1 : first + SHARES]:
            sums[-1] += part[...]
    total = jnp.concatenate(sums, axis=1)
    real_part, imag_part = total[:, :PART], total[:, PART:]
    power = real_part * real_part + imag_part * imag_part
    level = jnp.sum(power, axis=1, keepdims=True) * (1.0 / BAND)
    factor = lax.rsqrt(power + floor_share * level + epsilon)
    white_ref[:, :PART] = (real_part * factor).astype(jnp.bfloat16)
    white_ref[:, PART:] = (imag_part * factor).astype(jnp.bfloat16)
    rows = total.shape[0]
    lane = lax.broadcasted_iota(jnp.int32, (rows, 128), 1)
    held = (lane >= FLAG_LANE) & (lane < FLAG_LANE + flags_ref.shape[1])
    tile = (real_part * factor)[:, FLAG_TILE : FLAG_TILE + 128]
    flags = jnp.concatenate(
        [
            jnp.zeros((1, FLAG_LANE), jnp.float32),
            flags_ref[...],
            jnp.zeros((1, 128 - FLAG_LANE - flags_ref.shape[1]), jnp.float32),
        ],
        axis=1,
    )
    white_ref[:, FLAG_TILE : FLAG_TILE + 128] = jnp.where(held, flags, tile).astype(jnp.bfloat16)


def whiten(flags, parts):
    return pl.pallas_call(
        whiten_kernel,
        out_shape=jax.ShapeDtypeStruct((parts[0].shape[0], WIDTH), jnp.bfloat16),
        compiler_params=pltpu.CompilerParams(vmem_limit_bytes=16 * 2**20),
        name="whiten",
    )(flags, *parts)


def correlate_kernel(shape, core, steps, place_ref, flags_ref, ids_ref, *rest):
    segments, channels, devices = shape
    blocks, rest = rest[: len(steps)], rest[len(steps) :]
    if core:
        before_ref, table_ref, out_ref = rest[:3]
        held_ref, panel_ref, receivers_ref, inverse_ref, stacked_ref, sem = rest[3:]
        fetch = pltpu.make_async_copy(table_ref, inverse_ref, sem)
        fetch.start()
    else:
        out_ref, held_ref, panel_ref, receivers_ref = rest
    rows = held_ref.shape[1]
    members = devices // SHARES
    parts = members // segments
    ch_local = channels // devices
    ch_chip = 2 * ch_local
    place = place_ref[0]
    parity = place % 2 ^ core
    ids = ids_ref[...]
    sources = ids.shape[0]

    def position(device):
        member = device % members
        return (member // 2) * SHARES + device // members

    for step, block in zip(steps, blocks):
        far = block.shape[0]
        for line in range(far):
            device = place ^ ((line + far // 2) % far * 8 + step + core)
            held_ref[position(device)] = block[line]

    tails = held_ref[:, :, FLAG_TILE : FLAG_TILE + 128].reshape(held_ref.shape[0] * rows, 128)
    column = lax.broadcasted_iota(jnp.int32, (sources, tails.shape[0]), 1)
    choice = (column == position(ids // ch_chip * 2 + parity) * rows).astype(jnp.bfloat16)
    tail = jnp.dot(choice, tails, preferred_element_type=jnp.float32)
    lane = lax.broadcasted_iota(jnp.int32, (sources, 128), 1)

    channel = lax.broadcasted_iota(jnp.int32, (sources, channels), 1)
    pick_sources = (channel == ids).astype(jnp.bfloat16)
    line = lax.broadcasted_iota(jnp.int32, (16, channels), 0)
    channel = lax.broadcasted_iota(jnp.int32, (16, channels), 1)
    pick_own = ((channel == place * ch_local + line) & (line < ch_local)).astype(jnp.bfloat16)
    pick = jnp.concatenate([pick_sources, pick_own], axis=0)

    counts = [jnp.zeros((sources, 1), jnp.float32) for _ in range(ch_local)]
    per_segment = channels // rows
    for g in range(segments // 2):
        segment = held_ref[g * per_segment : (g + 1) * per_segment].reshape(channels, WIDTH)
        picked = jnp.dot(pick, segment, preferred_element_type=jnp.float32)
        mine = lane == FLAG_LANE + g * ch_chip + ids % ch_chip
        weight = jnp.sum(jnp.where(mine, tail, 0.0), axis=1, keepdims=True)
        panel_ref[g] = picked[:sources] * weight
        receivers_ref[g] = picked[sources:]
        for c in range(ch_local):
            counts[c] += weight * flags_ref[2 * g + parity, c]

    shares = [None] * ch_local
    for start in [FLAG_TILE] + [start for start in range(0, PART, 128) if start != FLAG_TILE]:
        re = slice(start, start + 128)
        im = slice(PART + start, PART + start + 128)
        for c in range(ch_local):
            real_sum = jnp.zeros((sources, 128), jnp.float32)
            imag_sum = jnp.zeros((sources, 128), jnp.float32)
            for g in range(segments // 2):
                flag = flags_ref[2 * g + parity, c]
                rec_real = receivers_ref[g, c : c + 1, re] * flag
                rec_imag = receivers_ref[g, c : c + 1, im] * flag
                src_real, src_imag = panel_ref[g, :, re], panel_ref[g, :, im]
                real_sum += src_real * rec_real + src_imag * rec_imag
                imag_sum += src_imag * rec_real - src_real * rec_imag
            if start == FLAG_TILE:
                real_sum = jnp.where(lane == FLAG_LANE, counts[c], real_sum)
            if not core:
                out_ref[c, :, re] = real_sum
                out_ref[c, :, im] = imag_sum
                continue
            real_sum += before_ref[c, :, re]
            imag_sum += before_ref[c, :, im]
            if start == FLAG_TILE:
                total = real_sum[:, FLAG_LANE : FLAG_LANE + 1]
                shares[c] = 1.0 / jnp.maximum(total, 1.0)
            lines = pl.ds(c, sources, stride=ch_local)
            stacked_ref[start // 128, lines, :] = real_sum * shares[c]
            stacked_ref[(PART + start) // 128, lines, :] = imag_sum * shares[c]
    if core:
        fetch.wait()
        tiles = [inverse_ref[tile * WIDTH : (tile + 1) * WIDTH] for tile in range(LAG_TILES)]
        lags = jnp.dot(
            jnp.concatenate([stacked_ref[i] for i in range(COLUMN_TILES)], axis=1).astype(
                jnp.bfloat16
            ),
            jnp.concatenate(tiles, axis=1),
            preferred_element_type=jnp.float32,
        )
        out_ref[...] = lags.reshape(sources, ch_local, LAG_TILES * 128)[:, :, :LAGS]


def correlate(core, place, weights, ids, steps, blocks, shape, before=None, table=None):
    segments, channels, devices = shape
    rows = blocks[0].shape[1]
    ch_local = channels // devices
    sources = ids.shape[0]
    smem = pl.BlockSpec(memory_space=pltpu.SMEM)
    vmem = pl.BlockSpec(memory_space=pltpu.VMEM)
    in_specs = [smem, smem, vmem] + [vmem] * len(blocks)
    scratch = [
        pltpu.VMEM((devices // 2, rows, WIDTH), jnp.bfloat16),
        pltpu.VMEM((segments // 2, sources, WIDTH), jnp.float32),
        pltpu.VMEM((segments // 2, 16, WIDTH), jnp.float32),
    ]
    if core:
        in_specs += [vmem, pl.BlockSpec(memory_space=pltpu.HBM)]
        scratch += [
            pltpu.VMEM(table.shape, jnp.bfloat16),
            pltpu.VMEM((COLUMN_TILES, sources * ch_local, 128), jnp.float32),
            pltpu.SemaphoreType.DMA,
        ]
    out = (sources, ch_local, LAGS) if core else (ch_local, sources, WIDTH)
    return pl.pallas_call(
        functools.partial(correlate_kernel, shape, core, steps),
        in_specs=in_specs,
        out_specs=vmem,
        out_shape=jax.ShapeDtypeStruct(out, jnp.float32),
        scratch_shapes=scratch,
        compiler_params=pltpu.CompilerParams(vmem_limit_bytes=16 * 2**20),
        cost_estimate=pl.CostEstimate(
            flops=sources * channels * WIDTH * segments,
            bytes_accessed=2 * (segments // 2) * channels * WIDTH,
            transcendentals=0,
        ),
        name="correlate",
    )(place, weights, ids, *blocks, *([before, table] if core else []))


def per_device(records, valid_flags, source_ids):
    segments, channels, span = records.shape
    devices = lax.axis_size("chan")
    members = devices // SHARES
    samples = span * devices
    place = lax.axis_index("chan")
    weights = valid_flags.astype(jnp.float32)

    def exchange(block, bits):
        return lax.ppermute(block, "chan", [(i, i ^ bits) for i in range(devices)])

    parity = place % 2
    partner = exchange(weights, 1)
    chip = jnp.where(
        parity == 0,
        jnp.concatenate([weights, partner], axis=1),
        jnp.concatenate([partner, weights], axis=1),
    )
    chip = chip.reshape(segments // 2, 2, -1)
    flags = lax.dynamic_index_in_dim(chip, parity, 1, keepdims=False).reshape(1, -1)

    chips = members // 2
    grouped = records.reshape(segments // 2, 2, -1, span)
    kept, handed = (
        lax.dynamic_index_in_dim(grouped, side, 1, keepdims=False).reshape(chips, -1, span)
        for side in (parity, 1 - parity)
    )
    pair = kept, exchange(handed, 1)
    chip_place = place % members // 2
    steps = [0] + balanced_steps(chips)
    arrived = {}
    for step in steps:
        block = jnp.stack([lax.dynamic_index_in_dim(p, chip_place ^ step, 0, False) for p in pair])
        arrived[step] = exchange(block, 2 * step) if step else block
    me = place.reshape(1)
    table = tables(samples, span)
    early, late = steps[: chips // 2], steps[chips // 2 :]
    before = transform(me, table, arrived, early, 0, COLUMN_TILES)[0]
    parts = []
    for first, last in ((0, FIRST_TILES), (FIRST_TILES, COLUMN_TILES)):
        own, other = transform(me, table, arrived, late, first, last, before)
        parts += [own, exchange(other, members)]
    white = whiten(flags, parts)

    far = devices // 8
    line = [white] + [exchange(white, 8 * k) for k in range(1, far)]
    halves = [jnp.stack(line[far // 2 :]), jnp.stack(line[: far // 2])]
    steps = [2 * near for near in range(4)]
    blocks = [
        jnp.concatenate([exchange(half, step) if step else half for half in halves])
        for step in steps
    ]
    swapped = [exchange(block, 1) for block in blocks]
    ids = source_ids.reshape(-1, 1)
    common = me, weights, ids
    shape = segments, channels, devices
    before = correlate(0, *common, steps, blocks, shape)
    return correlate(1, *common, steps, swapped, shape, before, inverse_table(samples))


def solution(mesh):
    return jax.shard_map(
        per_device,
        mesh=mesh,
        in_specs=(P("group", None, "chan"), P("group", "chan"), P("group")),
        out_specs=P("group", "chan", None),
        check_vma=False,
    )
```

```python
import functools
import math

import jax
import jax.numpy as jnp
import ml_dtypes
import numpy as np
from jax import lax
from jax.experimental import pallas as pl
from jax.experimental.pallas import tpu as pltpu
from jax.sharding import PartitionSpec as P

BAND = 600
SOURCES = 64
HALF_LAG = 500

lowest_bin = 8
floor_share = 0.05
epsilon = 1e-06

PART = 640
WIDTH = 2 * PART
LAGS = 2 * HALF_LAG + 1
LAG_TILES = -(-LAGS // 128)
SHARES = 2
COLUMN_TILES = WIDTH // 128
FIRST_TILES = 6
FLAG_TILE = BAND // 128 * 128
FLAG_LANE = BAND - FLAG_TILE


def angles(phase, samples):
    step = np.float32(2.0 * math.pi / samples)
    return (phase.astype(np.float32) * step).astype(np.float64)


def cos_sin(samples):
    angle = angles(np.arange(samples), samples)
    return np.cos(angle).astype(np.float32), (-np.sin(angle)).astype(np.float32)


def lane_tiles(table):
    tiled = table.reshape(*table.shape[:-1], -1, 128)
    return np.ascontiguousarray(np.moveaxis(tiled, -2, -3))


@functools.lru_cache(maxsize=None)
def tables(samples, span):
    bins = lowest_bin + np.arange(BAND)
    cosine, sine = cos_sin(samples)
    phase = np.arange(samples)[:, None] * bins[None, :] % samples
    forward = np.zeros((samples, WIDTH), ml_dtypes.bfloat16)
    forward[:, :BAND] = cosine.astype(ml_dtypes.bfloat16)[phase]
    forward[:, PART : PART + BAND] = sine.astype(ml_dtypes.bfloat16)[phase]
    return lane_tiles(forward.reshape(-1, span, WIDTH)).reshape(-1, 128)


@functools.lru_cache(maxsize=None)
def inverse_table(samples):
    bins = lowest_bin + np.arange(BAND)
    cosine, sine = cos_sin(samples)
    factor = np.float32(1.0 / math.sqrt(BAND))
    phase = bins[:, None] * (np.arange(LAGS) - HALF_LAG)[None, :] % samples
    inverse = np.zeros((WIDTH, LAG_TILES * 128), ml_dtypes.bfloat16)
    inverse[:BAND, :LAGS] = (cosine * factor).astype(ml_dtypes.bfloat16)[phase]
    inverse[PART : PART + BAND, :LAGS] = (sine * factor).astype(ml_dtypes.bfloat16)[phase]
    return lane_tiles(inverse).reshape(-1, 128)


def balanced_steps(chips):
    steps = [chips - 1]
    for low in range(1, chips // 2):
        steps += [low, low ^ (chips - 1)]
    return steps


def transform_kernel(steps, first, started, place_ref, table_ref, *rest):
    records, rest = rest[: len(steps)], rest[len(steps) :]
    if started:
        before_ref, rest = rest[0], rest[1:]
    outs, (tiles_ref, sems) = rest[:-2], rest[-2:]
    _, rows, span = records[0].shape
    blocks, lines, _ = tiles_ref.shape
    columns = lines // span
    copies = []
    for index in range(blocks):
        sender = place_ref[0] ^ (2 * steps[index // 2] + index % 2)
        start = (sender * COLUMN_TILES + first) * span
        source = table_ref.at[pl.ds(pl.multiple_of(start, span), lines)]
        copies.append(pltpu.make_async_copy(source, tiles_ref.at[index], sems.at[index]))
        copies[-1].start()
    if started:
        total = before_ref[:, first * 128 : (first + columns) * 128]
    else:
        total = jnp.zeros((rows, columns * 128), jnp.float32)
    for index in range(blocks):
        copies[index].wait()
        tiles = [tiles_ref[index, tile * span : (tile + 1) * span] for tile in range(columns)]
        total += jnp.dot(
            records[index // 2][index % 2],
            jnp.concatenate(tiles, axis=1),
            preferred_element_type=jnp.float32,
        )
    if len(outs) == 1:
        outs[0][...] = total
    else:
        kept = rows // 2
        mine = place_ref[0] < table_ref.shape[0] // (2 * COLUMN_TILES * span)
        outs[0][...] = jnp.where(mine, total[:kept], total[kept:])
        outs[1][...] = jnp.where(mine, total[kept:], total[:kept])


def transform(place, table, arrived, steps, first, last, before=None):
    records = [arrived[step] for step in steps]
    _, rows, span = records[0].shape
    columns = last - first
    blocks = 2 * len(steps)
    vmem = pl.BlockSpec(memory_space=pltpu.VMEM)
    started = before is not None
    outs = 2 if started else 1
    return pl.pallas_call(
        functools.partial(transform_kernel, steps, first, started),
        in_specs=[
            pl.BlockSpec(memory_space=pltpu.SMEM),
            pl.BlockSpec(memory_space=pltpu.HBM),
        ]
        + [vmem] * (len(records) + started),
        out_specs=[vmem] * outs,
        out_shape=[jax.ShapeDtypeStruct((rows // outs, columns * 128), jnp.float32)] * outs,
        scratch_shapes=[
            pltpu.VMEM((blocks, columns * span, 128), jnp.bfloat16),
            pltpu.SemaphoreType.DMA((blocks,)),
        ],
        compiler_params=pltpu.CompilerParams(vmem_limit_bytes=24 * 2**20),
        cost_estimate=pl.CostEstimate(
            flops=2 * rows * blocks * span * columns * 128,
            bytes_accessed=2 * blocks * span * columns * 128,
            transcendentals=0,
        ),
        name="transform",
    )(place, table, *records, *([before] if started else []))


def whiten_kernel(flags_ref, *rest):
    parts, white_ref = rest[:-1], rest[-1]
    sums = []
    for first in range(0, len(parts), SHARES):
        sums.append(parts[first][...])
        for part in parts[first + 1 : first + SHARES]:
            sums[-1] += part[...]
    total = jnp.concatenate(sums, axis=1)
    real_part, imag_part = total[:, :PART], total[:, PART:]
    power = real_part * real_part + imag_part * imag_part
    level = jnp.sum(power, axis=1, keepdims=True) * (1.0 / BAND)
    factor = lax.rsqrt(power + floor_share * level + epsilon)
    white_ref[:, :PART] = (real_part * factor).astype(jnp.bfloat16)
    white_ref[:, PART:] = (imag_part * factor).astype(jnp.bfloat16)
    rows = total.shape[0]
    lane = lax.broadcasted_iota(jnp.int32, (rows, 128), 1)
    held = (lane >= FLAG_LANE) & (lane < FLAG_LANE + flags_ref.shape[1])
    tile = (real_part * factor)[:, FLAG_TILE : FLAG_TILE + 128]
    flags = jnp.concatenate(
        [
            jnp.zeros((1, FLAG_LANE), jnp.float32),
            flags_ref[...],
            jnp.zeros((1, 128 - FLAG_LANE - flags_ref.shape[1]), jnp.float32),
        ],
        axis=1,
    )
    white_ref[:, FLAG_TILE : FLAG_TILE + 128] = jnp.where(held, flags, tile).astype(jnp.bfloat16)


def whiten(flags, parts):
    return pl.pallas_call(
        whiten_kernel,
        out_shape=jax.ShapeDtypeStruct((parts[0].shape[0], WIDTH), jnp.bfloat16),
        compiler_params=pltpu.CompilerParams(vmem_limit_bytes=16 * 2**20),
        name="whiten",
    )(flags, *parts)


def join_kernel(first_ref, second_ref, out_ref):
    half = first_ref.shape[0]
    out_ref[:half] = first_ref[...]
    out_ref[half:] = second_ref[...]


def join(first, second):
    half, rows, columns = first.shape
    return pl.pallas_call(
        join_kernel,
        out_shape=jax.ShapeDtypeStruct((2 * half, rows, columns), first.dtype),
        compiler_params=pltpu.CompilerParams(vmem_limit_bytes=16 * 2**20),
        name="join",
    )(first, second)


def correlate_kernel(shape, core, steps, place_ref, flags_ref, ids_ref, *rest):
    segments, channels, devices = shape
    blocks, rest = rest[: len(steps)], rest[len(steps) :]
    if core:
        before_ref, table_ref, out_ref = rest[:3]
        held_ref, panel_ref, receivers_ref, inverse_ref, stacked_ref, sem = rest[3:]
        fetch = pltpu.make_async_copy(table_ref, inverse_ref, sem)
        fetch.start()
    else:
        out_ref, held_ref, panel_ref, receivers_ref = rest
    rows = held_ref.shape[1]
    members = devices // SHARES
    parts = members // segments
    ch_local = channels // devices
    ch_chip = 2 * ch_local
    place = place_ref[0]
    parity = place % 2 ^ core
    ids = ids_ref[...]
    sources = ids.shape[0]

    def position(device):
        member = device % members
        return (member // 2) * SHARES + device // members

    for step, block in zip(steps, blocks):
        far = block.shape[0]
        for line in range(far):
            device = place ^ ((line + far // 2) % far * 8 + step + core)
            held_ref[position(device)] = block[line]

    tails = held_ref[:, :, FLAG_TILE : FLAG_TILE + 128].reshape(held_ref.shape[0] * rows, 128)
    column = lax.broadcasted_iota(jnp.int32, (sources, tails.shape[0]), 1)
    choice = (column == position(ids // ch_chip * 2 + parity) * rows).astype(jnp.bfloat16)
    tail = jnp.dot(choice, tails, preferred_element_type=jnp.float32)
    lane = lax.broadcasted_iota(jnp.int32, (sources, 128), 1)

    channel = lax.broadcasted_iota(jnp.int32, (sources, channels), 1)
    pick_sources = (channel == ids).astype(jnp.bfloat16)
    line = lax.broadcasted_iota(jnp.int32, (16, channels), 0)
    channel = lax.broadcasted_iota(jnp.int32, (16, channels), 1)
    pick_own = ((channel == place * ch_local + line) & (line < ch_local)).astype(jnp.bfloat16)
    pick = jnp.concatenate([pick_sources, pick_own], axis=0)

    counts = [jnp.zeros((sources, 1), jnp.float32) for _ in range(ch_local)]
    per_segment = channels // rows
    for g in range(segments // 2):
        segment = held_ref[g * per_segment : (g + 1) * per_segment].reshape(channels, WIDTH)
        picked = jnp.dot(pick, segment, preferred_element_type=jnp.float32)
        mine = lane == FLAG_LANE + g * ch_chip + ids % ch_chip
        weight = jnp.sum(jnp.where(mine, tail, 0.0), axis=1, keepdims=True)
        panel_ref[g] = picked[:sources] * weight
        receivers_ref[g] = picked[sources:]
        for c in range(ch_local):
            counts[c] += weight * flags_ref[2 * g + parity, c]

    shares = [None] * ch_local
    for start in [FLAG_TILE] + [start for start in range(0, PART, 128) if start != FLAG_TILE]:
        re = slice(start, start + 128)
        im = slice(PART + start, PART + start + 128)
        for c in range(ch_local):
            real_sum = jnp.zeros((sources, 128), jnp.float32)
            imag_sum = jnp.zeros((sources, 128), jnp.float32)
            for g in range(segments // 2):
                flag = flags_ref[2 * g + parity, c]
                rec_real = receivers_ref[g, c : c + 1, re] * flag
                rec_imag = receivers_ref[g, c : c + 1, im] * flag
                src_real, src_imag = panel_ref[g, :, re], panel_ref[g, :, im]
                real_sum += src_real * rec_real + src_imag * rec_imag
                imag_sum += src_imag * rec_real - src_real * rec_imag
            if start == FLAG_TILE:
                real_sum = jnp.where(lane == FLAG_LANE, counts[c], real_sum)
            if not core:
                out_ref[c, :, re] = real_sum
                out_ref[c, :, im] = imag_sum
                continue
            real_sum += before_ref[c, :, re]
            imag_sum += before_ref[c, :, im]
            if start == FLAG_TILE:
                total = real_sum[:, FLAG_LANE : FLAG_LANE + 1]
                shares[c] = 1.0 / jnp.maximum(total, 1.0)
            lines = pl.ds(c, sources, stride=ch_local)
            stacked_ref[start // 128, lines, :] = real_sum * shares[c]
            stacked_ref[(PART + start) // 128, lines, :] = imag_sum * shares[c]
    if core:
        fetch.wait()
        tiles = [inverse_ref[tile * WIDTH : (tile + 1) * WIDTH] for tile in range(LAG_TILES)]
        lags = jnp.dot(
            jnp.concatenate([stacked_ref[i] for i in range(COLUMN_TILES)], axis=1).astype(
                jnp.bfloat16
            ),
            jnp.concatenate(tiles, axis=1),
            preferred_element_type=jnp.float32,
        )
        out_ref[...] = lags.reshape(sources, ch_local, LAG_TILES * 128)[:, :, :LAGS]


def correlate(core, place, weights, ids, steps, blocks, shape, before=None, table=None):
    segments, channels, devices = shape
    rows = blocks[0].shape[1]
    ch_local = channels // devices
    sources = ids.shape[0]
    smem = pl.BlockSpec(memory_space=pltpu.SMEM)
    vmem = pl.BlockSpec(memory_space=pltpu.VMEM)
    in_specs = [smem, smem, vmem] + [vmem] * len(blocks)
    scratch = [
        pltpu.VMEM((devices // 2, rows, WIDTH), jnp.bfloat16),
        pltpu.VMEM((segments // 2, sources, WIDTH), jnp.float32),
        pltpu.VMEM((segments // 2, 16, WIDTH), jnp.float32),
    ]
    if core:
        in_specs += [vmem, pl.BlockSpec(memory_space=pltpu.HBM)]
        scratch += [
            pltpu.VMEM(table.shape, jnp.bfloat16),
            pltpu.VMEM((COLUMN_TILES, sources * ch_local, 128), jnp.float32),
            pltpu.SemaphoreType.DMA,
        ]
    out = (sources, ch_local, LAGS) if core else (ch_local, sources, WIDTH)
    return pl.pallas_call(
        functools.partial(correlate_kernel, shape, core, steps),
        in_specs=in_specs,
        out_specs=vmem,
        out_shape=jax.ShapeDtypeStruct(out, jnp.float32),
        scratch_shapes=scratch,
        compiler_params=pltpu.CompilerParams(vmem_limit_bytes=16 * 2**20),
        cost_estimate=pl.CostEstimate(
            flops=sources * channels * WIDTH * segments,
            bytes_accessed=2 * (segments // 2) * channels * WIDTH,
            transcendentals=0,
        ),
        name="correlate",
    )(place, weights, ids, *blocks, *([before, table] if core else []))


def per_device(records, valid_flags, source_ids):
    segments, channels, span = records.shape
    devices = lax.axis_size("chan")
    members = devices // SHARES
    samples = span * devices
    place = lax.axis_index("chan")
    weights = valid_flags.astype(jnp.float32)

    def exchange(block, bits):
        return lax.ppermute(block, "chan", [(i, i ^ bits) for i in range(devices)])

    parity = place % 2
    partner = exchange(weights, 1)
    chip = jnp.where(
        parity == 0,
        jnp.concatenate([weights, partner], axis=1),
        jnp.concatenate([partner, weights], axis=1),
    )
    chip = chip.reshape(segments // 2, 2, -1)
    flags = lax.dynamic_index_in_dim(chip, parity, 1, keepdims=False).reshape(1, -1)

    chips = members // 2
    grouped = records.reshape(segments // 2, 2, -1, span)
    kept, handed = (
        lax.dynamic_index_in_dim(grouped, side, 1, keepdims=False).reshape(chips, -1, span)
        for side in (parity, 1 - parity)
    )
    pair = kept, exchange(handed, 1)
    chip_place = place % members // 2
    steps = [0] + balanced_steps(chips)
    arrived = {}
    for step in steps:
        block = jnp.stack([lax.dynamic_index_in_dim(p, chip_place ^ step, 0, False) for p in pair])
        arrived[step] = exchange(block, 2 * step) if step else block
    me = place.reshape(1)
    table = tables(samples, span)
    early, late = steps[: chips // 2], steps[chips // 2 :]
    before = transform(me, table, arrived, early, 0, COLUMN_TILES)[0]
    parts = []
    for first, last in ((0, FIRST_TILES), (FIRST_TILES, COLUMN_TILES)):
        own, other = transform(me, table, arrived, late, first, last, before)
        parts += [own, exchange(other, members)]
    white = whiten(flags, parts)

    far = devices // 8
    line = [white] + [exchange(white, 8 * k) for k in range(1, far)]
    halves = [jnp.stack(line[far // 2 :]), jnp.stack(line[: far // 2])]
    steps = [2 * near for near in range(4)]
    blocks = []
    for step in steps:
        came = [exchange(half, step) if step else half for half in halves]
        blocks.append(join(*came))
    swapped = [exchange(block, 1) for block in blocks]
    ids = source_ids.reshape(-1, 1)
    common = me, weights, ids
    shape = segments, channels, devices
    before = correlate(0, *common, steps, blocks, shape)
    return correlate(1, *common, steps, swapped, shape, before, inverse_table(samples))


def solution(mesh):
    return jax.shard_map(
        per_device,
        mesh=mesh,
        in_specs=(P("group", None, "chan"), P("group", "chan"), P("group")),
        out_specs=P("group", "chan", None),
        check_vma=False,
    )
```

```python
import functools
import math

import jax
import jax.numpy as jnp
import ml_dtypes
import numpy as np
from jax import lax
from jax.experimental import pallas as pl
from jax.experimental.pallas import tpu as pltpu
from jax.sharding import PartitionSpec as P

BAND = 600
SOURCES = 64
HALF_LAG = 500

lowest_bin = 8
floor_share = 0.05
epsilon = 1e-06

PART = 640
WIDTH = 2 * PART
LAGS = 2 * HALF_LAG + 1
LAG_TILES = -(-LAGS // 128)
SHARES = 2
COLUMN_TILES = WIDTH // 128
FIRST_TILES = 6
FLAG_TILE = BAND // 128 * 128
FLAG_LANE = BAND - FLAG_TILE


def angles(phase, samples):
    step = np.float32(2.0 * math.pi / samples)
    return (phase.astype(np.float32) * step).astype(np.float64)


def cos_sin(samples):
    angle = angles(np.arange(samples), samples)
    return np.cos(angle).astype(np.float32), (-np.sin(angle)).astype(np.float32)


def lane_tiles(table):
    tiled = table.reshape(*table.shape[:-1], -1, 128)
    return np.ascontiguousarray(np.moveaxis(tiled, -2, -3))


@functools.lru_cache(maxsize=None)
def tables(samples, span):
    bins = lowest_bin + np.arange(BAND)
    cosine, sine = cos_sin(samples)
    phase = np.arange(samples)[:, None] * bins[None, :] % samples
    forward = np.zeros((samples, WIDTH), ml_dtypes.bfloat16)
    forward[:, :BAND] = cosine.astype(ml_dtypes.bfloat16)[phase]
    forward[:, PART : PART + BAND] = sine.astype(ml_dtypes.bfloat16)[phase]
    return lane_tiles(forward.reshape(-1, span, WIDTH)).reshape(-1, 128)


@functools.lru_cache(maxsize=None)
def inverse_table(samples):
    bins = lowest_bin + np.arange(BAND)
    cosine, sine = cos_sin(samples)
    factor = np.float32(1.0 / math.sqrt(BAND))
    phase = bins[:, None] * (np.arange(LAGS) - HALF_LAG)[None, :] % samples
    inverse = np.zeros((WIDTH, LAG_TILES * 128), ml_dtypes.bfloat16)
    inverse[:BAND, :LAGS] = (cosine * factor).astype(ml_dtypes.bfloat16)[phase]
    inverse[PART : PART + BAND, :LAGS] = (sine * factor).astype(ml_dtypes.bfloat16)[phase]
    return lane_tiles(inverse).reshape(-1, 128)


def balanced_steps(chips):
    steps = [chips - 1]
    for low in range(1, chips // 2):
        steps += [low, low ^ (chips - 1)]
    return steps


def transform_kernel(steps, first, started, place_ref, table_ref, *rest):
    records, rest = rest[: len(steps)], rest[len(steps) :]
    if started:
        before_ref, rest = rest[0], rest[1:]
    outs, (tiles_ref, sems) = rest[:-2], rest[-2:]
    _, rows, span = records[0].shape
    blocks, lines, _ = tiles_ref.shape
    columns = lines // span
    copies = []
    for index in range(blocks):
        sender = place_ref[0] ^ (2 * steps[index // 2] + index % 2)
        start = (sender * COLUMN_TILES + first) * span
        source = table_ref.at[pl.ds(pl.multiple_of(start, span), lines)]
        copies.append(pltpu.make_async_copy(source, tiles_ref.at[index], sems.at[index]))
        copies[-1].start()
    if started:
        total = before_ref[:, first * 128 : (first + columns) * 128]
    else:
        total = jnp.zeros((rows, columns * 128), jnp.float32)
    for index in range(blocks):
        copies[index].wait()
        tiles = [tiles_ref[index, tile * span : (tile + 1) * span] for tile in range(columns)]
        total += jnp.dot(
            records[index // 2][index % 2],
            jnp.concatenate(tiles, axis=1),
            preferred_element_type=jnp.float32,
        )
    if len(outs) == 1:
        outs[0][...] = total
    else:
        kept = rows // 2
        mine = place_ref[0] < table_ref.shape[0] // (2 * COLUMN_TILES * span)
        outs[0][...] = jnp.where(mine, total[:kept], total[kept:])
        outs[1][...] = jnp.where(mine, total[kept:], total[:kept])


def transform(place, table, arrived, steps, first, last, before=None):
    records = [arrived[step] for step in steps]
    _, rows, span = records[0].shape
    columns = last - first
    blocks = 2 * len(steps)
    vmem = pl.BlockSpec(memory_space=pltpu.VMEM)
    started = before is not None
    outs = 2 if started else 1
    return pl.pallas_call(
        functools.partial(transform_kernel, steps, first, started),
        in_specs=[
            pl.BlockSpec(memory_space=pltpu.SMEM),
            pl.BlockSpec(memory_space=pltpu.HBM),
        ]
        + [vmem] * (len(records) + started),
        out_specs=[vmem] * outs,
        out_shape=[jax.ShapeDtypeStruct((rows // outs, columns * 128), jnp.float32)] * outs,
        scratch_shapes=[
            pltpu.VMEM((blocks, columns * span, 128), jnp.bfloat16),
            pltpu.SemaphoreType.DMA((blocks,)),
        ],
        compiler_params=pltpu.CompilerParams(vmem_limit_bytes=24 * 2**20),
        cost_estimate=pl.CostEstimate(
            flops=2 * rows * blocks * span * columns * 128,
            bytes_accessed=2 * blocks * span * columns * 128,
            transcendentals=0,
        ),
        name="transform",
    )(place, table, *records, *([before] if started else []))


def whiten_kernel(flags_ref, *rest):
    parts, white_ref = rest[:-1], rest[-1]
    sums = []
    for first in range(0, len(parts), SHARES):
        sums.append(parts[first][...])
        for part in parts[first + 1 : first + SHARES]:
            sums[-1] += part[...]
    total = jnp.concatenate(sums, axis=1)
    real_part, imag_part = total[:, :PART], total[:, PART:]
    power = real_part * real_part + imag_part * imag_part
    level = jnp.sum(power, axis=1, keepdims=True) * (1.0 / BAND)
    factor = lax.rsqrt(power + floor_share * level + epsilon)
    white_ref[:, :PART] = (real_part * factor).astype(jnp.bfloat16)
    white_ref[:, PART:] = (imag_part * factor).astype(jnp.bfloat16)
    rows = total.shape[0]
    lane = lax.broadcasted_iota(jnp.int32, (rows, 128), 1)
    held = (lane >= FLAG_LANE) & (lane < FLAG_LANE + flags_ref.shape[1])
    tile = (real_part * factor)[:, FLAG_TILE : FLAG_TILE + 128]
    flags = jnp.concatenate(
        [
            jnp.zeros((1, FLAG_LANE), jnp.float32),
            flags_ref[...],
            jnp.zeros((1, 128 - FLAG_LANE - flags_ref.shape[1]), jnp.float32),
        ],
        axis=1,
    )
    white_ref[:, FLAG_TILE : FLAG_TILE + 128] = jnp.where(held, flags, tile).astype(jnp.bfloat16)


def whiten(flags, parts):
    return pl.pallas_call(
        whiten_kernel,
        out_shape=jax.ShapeDtypeStruct((parts[0].shape[0], WIDTH), jnp.bfloat16),
        compiler_params=pltpu.CompilerParams(vmem_limit_bytes=16 * 2**20),
        name="whiten",
    )(flags, *parts)


def correlate_kernel(shape, core, steps, place_ref, flags_ref, ids_ref, *rest):
    segments, channels, devices = shape
    blocks, rest = rest[: len(steps)], rest[len(steps) :]
    if core:
        before_ref, table_ref, out_ref = rest[:3]
        panel_ref, receivers_ref, inverse_ref, stacked_ref, sem = rest[3:]
        fetch = pltpu.make_async_copy(table_ref, inverse_ref, sem)
        fetch.start()
    else:
        out_ref, panel_ref, receivers_ref = rest
    far, rows, _ = blocks[0].shape
    members = devices // SHARES
    parts = members // segments
    ch_local = channels // devices
    ch_chip = 2 * ch_local
    place = place_ref[0]
    centre = place ^ core
    parity = centre % 2
    ids = ids_ref[...]
    sources = ids.shape[0]

    distances = [(line + far // 2) % far * 8 + step for step in steps for line in range(far)]
    places = [(index, line) for index in range(len(steps)) for line in range(far)]

    heads = [
        blocks[index][line, :16, FLAG_TILE : FLAG_TILE + 128] for index, line in places
    ]
    tails = jnp.concatenate(heads, axis=0)
    distance = (ids // ch_chip * 2 + parity) ^ centre
    slot = distance % 8 // 2 * far + (distance // 8 + far // 2) % far
    column = lax.broadcasted_iota(jnp.int32, (sources, tails.shape[0]), 1)
    choice = (column == slot * 16).astype(jnp.bfloat16)
    tail = jnp.dot(choice, tails, preferred_element_type=jnp.float32)
    lane = lax.broadcasted_iota(jnp.int32, (sources, 128), 1)

    line = lax.broadcasted_iota(jnp.int32, (16, 1), 0)
    own = jnp.where(line < ch_local, place * ch_local + line, -1)
    wanted = jnp.concatenate([ids, own], axis=0)
    column = lax.broadcasted_iota(jnp.int32, (1, channels), 1)

    counts = [jnp.zeros((sources, 1), jnp.float32) for _ in range(ch_local)]
    numbers = []
    for g in range(segments // 2):
        chosen = [n for n, d in enumerate(distances) if d % members // 2 // parts == g]
        channel = column % rows
        for order, n in enumerate(chosen):
            device = centre ^ distances[n]
            base = device % members // 2 % parts * (SHARES * rows) + device // members * rows
            channel = jnp.where(column // rows == order, channel + base, channel)
        pick = (channel == wanted).astype(jnp.bfloat16)
        segment = jnp.concatenate([blocks[places[n][0]][places[n][1]] for n in chosen], axis=0)
        picked = jnp.dot(pick, segment, preferred_element_type=jnp.float32)
        number = (centre ^ distances[chosen[0]]) % members // 2 // parts
        numbers.append(2 * number + parity)
        mine = lane == FLAG_LANE + number * ch_chip + ids % ch_chip
        weight = jnp.sum(jnp.where(mine, tail, 0.0), axis=1, keepdims=True)
        panel_ref[g] = picked[:sources] * weight
        receivers_ref[g] = picked[sources:]
        for c in range(ch_local):
            counts[c] += weight * flags_ref[numbers[g], c]

    shares = [None] * ch_local
    for start in [FLAG_TILE] + [start for start in range(0, PART, 128) if start != FLAG_TILE]:
        re = slice(start, start + 128)
        im = slice(PART + start, PART + start + 128)
        for c in range(ch_local):
            real_sum = jnp.zeros((sources, 128), jnp.float32)
            imag_sum = jnp.zeros((sources, 128), jnp.float32)
            for g in range(segments // 2):
                flag = flags_ref[numbers[g], c]
                rec_real = receivers_ref[g, c : c + 1, re] * flag
                rec_imag = receivers_ref[g, c : c + 1, im] * flag
                src_real, src_imag = panel_ref[g, :, re], panel_ref[g, :, im]
                real_sum += src_real * rec_real + src_imag * rec_imag
                imag_sum += src_imag * rec_real - src_real * rec_imag
            if start == FLAG_TILE:
                real_sum = jnp.where(lane == FLAG_LANE, counts[c], real_sum)
            if not core:
                out_ref[c, :, re] = real_sum
                out_ref[c, :, im] = imag_sum
                continue
            real_sum += before_ref[c, :, re]
            imag_sum += before_ref[c, :, im]
            if start == FLAG_TILE:
                total = real_sum[:, FLAG_LANE : FLAG_LANE + 1]
                shares[c] = 1.0 / jnp.maximum(total, 1.0)
            lines = pl.ds(c, sources, stride=ch_local)
            stacked_ref[start // 128, lines, :] = real_sum * shares[c]
            stacked_ref[(PART + start) // 128, lines, :] = imag_sum * shares[c]
    if core:
        fetch.wait()
        tiles = [inverse_ref[tile * WIDTH : (tile + 1) * WIDTH] for tile in range(LAG_TILES)]
        lags = jnp.dot(
            jnp.concatenate([stacked_ref[i] for i in range(COLUMN_TILES)], axis=1).astype(
                jnp.bfloat16
            ),
            jnp.concatenate(tiles, axis=1),
            preferred_element_type=jnp.float32,
        )
        out_ref[...] = lags.reshape(sources, ch_local, LAG_TILES * 128)[:, :, :LAGS]


def correlate(core, place, weights, ids, steps, blocks, shape, before=None, table=None):
    segments, channels, devices = shape
    ch_local = channels // devices
    sources = ids.shape[0]
    smem = pl.BlockSpec(memory_space=pltpu.SMEM)
    vmem = pl.BlockSpec(memory_space=pltpu.VMEM)
    in_specs = [smem, smem, vmem] + [vmem] * len(blocks)
    scratch = [
        pltpu.VMEM((segments // 2, sources, WIDTH), jnp.float32),
        pltpu.VMEM((segments // 2, 16, WIDTH), jnp.float32),
    ]
    if core:
        in_specs += [vmem, pl.BlockSpec(memory_space=pltpu.HBM)]
        scratch += [
            pltpu.VMEM(table.shape, jnp.bfloat16),
            pltpu.VMEM((COLUMN_TILES, sources * ch_local, 128), jnp.float32),
            pltpu.SemaphoreType.DMA,
        ]
    out = (sources, ch_local, LAGS) if core else (ch_local, sources, WIDTH)
    return pl.pallas_call(
        functools.partial(correlate_kernel, shape, core, steps),
        in_specs=in_specs,
        out_specs=vmem,
        out_shape=jax.ShapeDtypeStruct(out, jnp.float32),
        scratch_shapes=scratch,
        compiler_params=pltpu.CompilerParams(vmem_limit_bytes=16 * 2**20),
        cost_estimate=pl.CostEstimate(
            flops=sources * channels * WIDTH * segments,
            bytes_accessed=2 * (segments // 2) * channels * WIDTH,
            transcendentals=0,
        ),
        name="correlate",
    )(place, weights, ids, *blocks, *([before, table] if core else []))


def per_device(records, valid_flags, source_ids):
    segments, channels, span = records.shape
    devices = lax.axis_size("chan")
    members = devices // SHARES
    samples = span * devices
    place = lax.axis_index("chan")
    weights = valid_flags.astype(jnp.float32)

    def exchange(block, bits):
        return lax.ppermute(block, "chan", [(i, i ^ bits) for i in range(devices)])

    parity = place % 2
    partner = exchange(weights, 1)
    chip = jnp.where(
        parity == 0,
        jnp.concatenate([weights, partner], axis=1),
        jnp.concatenate([partner, weights], axis=1),
    )
    chip = chip.reshape(segments // 2, 2, -1)
    flags = lax.dynamic_index_in_dim(chip, parity, 1, keepdims=False).reshape(1, -1)

    chips = members // 2
    grouped = records.reshape(segments // 2, 2, -1, span)
    kept, handed = (
        lax.dynamic_index_in_dim(grouped, side, 1, keepdims=False).reshape(chips, -1, span)
        for side in (parity, 1 - parity)
    )
    pair = kept, exchange(handed, 1)
    chip_place = place % members // 2
    steps = [0] + balanced_steps(chips)
    arrived = {}
    for step in steps:
        block = jnp.stack([lax.dynamic_index_in_dim(p, chip_place ^ step, 0, False) for p in pair])
        arrived[step] = exchange(block, 2 * step) if step else block
    me = place.reshape(1)
    table = tables(samples, span)
    early, late = steps[: chips // 2], steps[chips // 2 :]
    before = transform(me, table, arrived, early, 0, COLUMN_TILES)[0]
    parts = []
    for first, last in ((0, FIRST_TILES), (FIRST_TILES, COLUMN_TILES)):
        own, other = transform(me, table, arrived, late, first, last, before)
        parts += [own, exchange(other, members)]
    white = whiten(flags, parts)

    far = devices // 8
    line = [white] + [exchange(white, 8 * k) for k in range(1, far)]
    halves = [jnp.stack(line[far // 2 :]), jnp.stack(line[: far // 2])]
    steps = [2 * near for near in range(4)]
    blocks = [
        jnp.concatenate([exchange(half, step) if step else half for half in halves])
        for step in steps
    ]
    swapped = [exchange(block, 1) for block in blocks]
    ids = source_ids.reshape(-1, 1)
    common = me, weights, ids
    shape = segments, channels, devices
    before = correlate(0, *common, steps, blocks, shape)
    return correlate(1, *common, steps, swapped, shape, before, inverse_table(samples))


def solution(mesh):
    return jax.shard_map(
        per_device,
        mesh=mesh,
        in_specs=(P("group", None, "chan"), P("group", "chan"), P("group")),
        out_specs=P("group", "chan", None),
        check_vma=False,
    )
```

```python
import functools
import math

import jax
import jax.numpy as jnp
import ml_dtypes
import numpy as np
from jax import lax
from jax.experimental import pallas as pl
from jax.experimental.pallas import tpu as pltpu
from jax.sharding import PartitionSpec as P

BAND = 600
SOURCES = 64
HALF_LAG = 500

lowest_bin = 8
floor_share = 0.05
epsilon = 1e-06

PART = 640
WIDTH = 2 * PART
LAGS = 2 * HALF_LAG + 1
LAG_TILES = -(-LAGS // 128)
SHARES = 2
COLUMN_TILES = WIDTH // 128
FIRST_TILES = 6
FLAG_TILE = BAND // 128 * 128
FLAG_LANE = BAND - FLAG_TILE


def angles(phase, samples):
    step = np.float32(2.0 * math.pi / samples)
    return (phase.astype(np.float32) * step).astype(np.float64)


def cos_sin(samples):
    angle = angles(np.arange(samples), samples)
    return np.cos(angle).astype(np.float32), (-np.sin(angle)).astype(np.float32)


def lane_tiles(table):
    tiled = table.reshape(*table.shape[:-1], -1, 128)
    return np.ascontiguousarray(np.moveaxis(tiled, -2, -3))


@functools.lru_cache(maxsize=None)
def tables(samples, span):
    bins = lowest_bin + np.arange(BAND)
    cosine, sine = cos_sin(samples)
    phase = np.arange(samples)[:, None] * bins[None, :] % samples
    forward = np.zeros((samples, WIDTH), ml_dtypes.bfloat16)
    forward[:, :BAND] = cosine.astype(ml_dtypes.bfloat16)[phase]
    forward[:, PART : PART + BAND] = sine.astype(ml_dtypes.bfloat16)[phase]
    return lane_tiles(forward.reshape(-1, span, WIDTH)).reshape(-1, 128)


@functools.lru_cache(maxsize=None)
def inverse_table(samples):
    bins = lowest_bin + np.arange(BAND)
    cosine, sine = cos_sin(samples)
    factor = np.float32(1.0 / math.sqrt(BAND))
    phase = bins[:, None] * (np.arange(LAGS) - HALF_LAG)[None, :] % samples
    inverse = np.zeros((WIDTH, LAG_TILES * 128), ml_dtypes.bfloat16)
    inverse[:BAND, :LAGS] = (cosine * factor).astype(ml_dtypes.bfloat16)[phase]
    inverse[PART : PART + BAND, :LAGS] = (sine * factor).astype(ml_dtypes.bfloat16)[phase]
    return lane_tiles(inverse).reshape(-1, 128)


def balanced_steps(chips):
    steps = [chips - 1]
    for low in range(1, chips // 2):
        steps += [low, low ^ (chips - 1)]
    return steps


def transform_kernel(steps, first, started, place_ref, table_ref, *rest):
    records, rest = rest[: len(steps)], rest[len(steps) :]
    if started:
        before_ref, rest = rest[0], rest[1:]
    outs, (tiles_ref, sems) = rest[:-2], rest[-2:]
    _, rows, span = records[0].shape
    blocks, lines, _ = tiles_ref.shape
    columns = lines // span
    copies = []
    for index in range(blocks):
        sender = place_ref[0] ^ (2 * steps[index // 2] + index % 2)
        start = (sender * COLUMN_TILES + first) * span
        source = table_ref.at[pl.ds(pl.multiple_of(start, span), lines)]
        copies.append(pltpu.make_async_copy(source, tiles_ref.at[index], sems.at[index]))
        copies[-1].start()
    if started:
        total = before_ref[:, first * 128 : (first + columns) * 128]
    else:
        total = jnp.zeros((rows, columns * 128), jnp.float32)
    for index in range(blocks):
        copies[index].wait()
        tiles = [tiles_ref[index, tile * span : (tile + 1) * span] for tile in range(columns)]
        total += jnp.dot(
            records[index // 2][index % 2],
            jnp.concatenate(tiles, axis=1),
            preferred_element_type=jnp.float32,
        )
    if len(outs) == 1:
        outs[0][...] = total
    else:
        kept = rows // 2
        mine = place_ref[0] < table_ref.shape[0] // (2 * COLUMN_TILES * span)
        outs[0][...] = jnp.where(mine, total[:kept], total[kept:])
        outs[1][...] = jnp.where(mine, total[kept:], total[:kept])


def transform(place, table, arrived, steps, first, last, before=None):
    records = [arrived[step] for step in steps]
    _, rows, span = records[0].shape
    columns = last - first
    blocks = 2 * len(steps)
    vmem = pl.BlockSpec(memory_space=pltpu.VMEM)
    started = before is not None
    outs = 2 if started else 1
    return pl.pallas_call(
        functools.partial(transform_kernel, steps, first, started),
        in_specs=[
            pl.BlockSpec(memory_space=pltpu.SMEM),
            pl.BlockSpec(memory_space=pltpu.HBM),
        ]
        + [vmem] * (len(records) + started),
        out_specs=[vmem] * outs,
        out_shape=[jax.ShapeDtypeStruct((rows // outs, columns * 128), jnp.float32)] * outs,
        scratch_shapes=[
            pltpu.VMEM((blocks, columns * span, 128), jnp.bfloat16),
            pltpu.SemaphoreType.DMA((blocks,)),
        ],
        compiler_params=pltpu.CompilerParams(vmem_limit_bytes=24 * 2**20),
        cost_estimate=pl.CostEstimate(
            flops=2 * rows * blocks * span * columns * 128,
            bytes_accessed=2 * blocks * span * columns * 128,
            transcendentals=0,
        ),
        name="transform",
    )(place, table, *records, *([before] if started else []))


def whiten_kernel(flags_ref, *rest):
    parts, white_ref = rest[:-1], rest[-1]
    sums = []
    for first in range(0, len(parts), SHARES):
        sums.append(parts[first][...])
        for part in parts[first + 1 : first + SHARES]:
            sums[-1] += part[...]
    total = jnp.concatenate(sums, axis=1)
    real_part, imag_part = total[:, :PART], total[:, PART:]
    power = real_part * real_part + imag_part * imag_part
    level = jnp.sum(power, axis=1, keepdims=True) * (1.0 / BAND)
    factor = lax.rsqrt(power + floor_share * level + epsilon)
    white_ref[:, :PART] = (real_part * factor).astype(jnp.bfloat16)
    white_ref[:, PART:] = (imag_part * factor).astype(jnp.bfloat16)
    rows = total.shape[0]
    lane = lax.broadcasted_iota(jnp.int32, (rows, 128), 1)
    held = (lane >= FLAG_LANE) & (lane < FLAG_LANE + flags_ref.shape[1])
    tile = (real_part * factor)[:, FLAG_TILE : FLAG_TILE + 128]
    flags = jnp.concatenate(
        [
            jnp.zeros((1, FLAG_LANE), jnp.float32),
            flags_ref[...],
            jnp.zeros((1, 128 - FLAG_LANE - flags_ref.shape[1]), jnp.float32),
        ],
        axis=1,
    )
    white_ref[:, FLAG_TILE : FLAG_TILE + 128] = jnp.where(held, flags, tile).astype(jnp.bfloat16)


def whiten(flags, parts):
    return pl.pallas_call(
        whiten_kernel,
        out_shape=jax.ShapeDtypeStruct((parts[0].shape[0], WIDTH), jnp.bfloat16),
        compiler_params=pltpu.CompilerParams(vmem_limit_bytes=16 * 2**20),
        name="whiten",
    )(flags, *parts)


def correlate_kernel(shape, core, layout, place_ref, flags_ref, ids_ref, *rest):
    segments, channels, devices = shape
    blocks, rest = rest[: len(layout)], rest[len(layout) :]
    if core:
        before_ref, table_ref, out_ref = rest[:3]
        panel_ref, receivers_ref, inverse_ref, stacked_ref, sem = rest[3:]
        fetch = pltpu.make_async_copy(table_ref, inverse_ref, sem)
        fetch.start()
    else:
        out_ref, panel_ref, receivers_ref = rest
    rows = blocks[0].shape[1]
    members = devices // SHARES
    parts = members // segments
    ch_local = channels // devices
    ch_chip = 2 * ch_local
    place = place_ref[0]
    centre = place ^ core
    parity = centre % 2
    ids = ids_ref[...]
    sources = ids.shape[0]

    distances = [distance for ways in layout for distance in ways]
    places = [(index, line) for index, ways in enumerate(layout) for line in range(len(ways))]

    heads = [
        blocks[index][line, :16, FLAG_TILE : FLAG_TILE + 128] for index, line in places
    ]
    tails = jnp.concatenate(heads, axis=0)
    distance = (ids // ch_chip * 2 + parity) ^ centre
    slot = jnp.zeros_like(distance)
    for n, known in enumerate(distances):
        slot = jnp.where(distance == known, n, slot)
    column = lax.broadcasted_iota(jnp.int32, (sources, tails.shape[0]), 1)
    choice = (column == slot * 16).astype(jnp.bfloat16)
    tail = jnp.dot(choice, tails, preferred_element_type=jnp.float32)
    lane = lax.broadcasted_iota(jnp.int32, (sources, 128), 1)

    line = lax.broadcasted_iota(jnp.int32, (16, 1), 0)
    own = jnp.where(line < ch_local, place * ch_local + line, -1)
    wanted = jnp.concatenate([ids, own], axis=0)
    column = lax.broadcasted_iota(jnp.int32, (1, channels), 1)

    counts = [jnp.zeros((sources, 1), jnp.float32) for _ in range(ch_local)]
    numbers = []
    for g in range(segments // 2):
        chosen = [n for n, d in enumerate(distances) if d % members // 2 // parts == g]
        channel = column % rows
        for order, n in enumerate(chosen):
            device = centre ^ distances[n]
            base = device % members // 2 % parts * (SHARES * rows) + device // members * rows
            channel = jnp.where(column // rows == order, channel + base, channel)
        pick = (channel == wanted).astype(jnp.bfloat16)
        segment = jnp.concatenate([blocks[places[n][0]][places[n][1]] for n in chosen], axis=0)
        picked = jnp.dot(pick, segment, preferred_element_type=jnp.float32)
        number = (centre ^ distances[chosen[0]]) % members // 2 // parts
        numbers.append(2 * number + parity)
        mine = lane == FLAG_LANE + number * ch_chip + ids % ch_chip
        weight = jnp.sum(jnp.where(mine, tail, 0.0), axis=1, keepdims=True)
        panel_ref[g] = picked[:sources] * weight
        receivers_ref[g] = picked[sources:]
        for c in range(ch_local):
            counts[c] += weight * flags_ref[numbers[g], c]

    shares = [None] * ch_local
    for start in [FLAG_TILE] + [start for start in range(0, PART, 128) if start != FLAG_TILE]:
        re = slice(start, start + 128)
        im = slice(PART + start, PART + start + 128)
        for c in range(ch_local):
            real_sum = jnp.zeros((sources, 128), jnp.float32)
            imag_sum = jnp.zeros((sources, 128), jnp.float32)
            for g in range(segments // 2):
                flag = flags_ref[numbers[g], c]
                rec_real = receivers_ref[g, c : c + 1, re] * flag
                rec_imag = receivers_ref[g, c : c + 1, im] * flag
                src_real, src_imag = panel_ref[g, :, re], panel_ref[g, :, im]
                real_sum += src_real * rec_real + src_imag * rec_imag
                imag_sum += src_imag * rec_real - src_real * rec_imag
            if start == FLAG_TILE:
                real_sum = jnp.where(lane == FLAG_LANE, counts[c], real_sum)
            if not core:
                out_ref[c, :, re] = real_sum
                out_ref[c, :, im] = imag_sum
                continue
            real_sum += before_ref[c, :, re]
            imag_sum += before_ref[c, :, im]
            if start == FLAG_TILE:
                total = real_sum[:, FLAG_LANE : FLAG_LANE + 1]
                shares[c] = 1.0 / jnp.maximum(total, 1.0)
            lines = pl.ds(c, sources, stride=ch_local)
            stacked_ref[start // 128, lines, :] = real_sum * shares[c]
            stacked_ref[(PART + start) // 128, lines, :] = imag_sum * shares[c]
    if core:
        fetch.wait()
        tiles = [inverse_ref[tile * WIDTH : (tile + 1) * WIDTH] for tile in range(LAG_TILES)]
        lags = jnp.dot(
            jnp.concatenate([stacked_ref[i] for i in range(COLUMN_TILES)], axis=1).astype(
                jnp.bfloat16
            ),
            jnp.concatenate(tiles, axis=1),
            preferred_element_type=jnp.float32,
        )
        out_ref[...] = lags.reshape(sources, ch_local, LAG_TILES * 128)[:, :, :LAGS]


def correlate(core, place, weights, ids, layout, blocks, shape, before=None, table=None):
    segments, channels, devices = shape
    ch_local = channels // devices
    sources = ids.shape[0]
    smem = pl.BlockSpec(memory_space=pltpu.SMEM)
    vmem = pl.BlockSpec(memory_space=pltpu.VMEM)
    in_specs = [smem, smem, vmem] + [vmem] * len(blocks)
    scratch = [
        pltpu.VMEM((segments // 2, sources, WIDTH), jnp.float32),
        pltpu.VMEM((segments // 2, 16, WIDTH), jnp.float32),
    ]
    if core:
        in_specs += [vmem, pl.BlockSpec(memory_space=pltpu.HBM)]
        scratch += [
            pltpu.VMEM(table.shape, jnp.bfloat16),
            pltpu.VMEM((COLUMN_TILES, sources * ch_local, 128), jnp.float32),
            pltpu.SemaphoreType.DMA,
        ]
    out = (sources, ch_local, LAGS) if core else (ch_local, sources, WIDTH)
    return pl.pallas_call(
        functools.partial(correlate_kernel, shape, core, layout),
        in_specs=in_specs,
        out_specs=vmem,
        out_shape=jax.ShapeDtypeStruct(out, jnp.float32),
        scratch_shapes=scratch,
        compiler_params=pltpu.CompilerParams(vmem_limit_bytes=16 * 2**20),
        cost_estimate=pl.CostEstimate(
            flops=sources * channels * WIDTH * segments,
            bytes_accessed=2 * (segments // 2) * channels * WIDTH,
            transcendentals=0,
        ),
        name="correlate",
    )(place, weights, ids, *blocks, *([before, table] if core else []))


def per_device(records, valid_flags, source_ids):
    segments, channels, span = records.shape
    devices = lax.axis_size("chan")
    members = devices // SHARES
    samples = span * devices
    place = lax.axis_index("chan")
    weights = valid_flags.astype(jnp.float32)

    def exchange(block, bits):
        return lax.ppermute(block, "chan", [(i, i ^ bits) for i in range(devices)])

    parity = place % 2
    partner = exchange(weights, 1)
    chip = jnp.where(
        parity == 0,
        jnp.concatenate([weights, partner], axis=1),
        jnp.concatenate([partner, weights], axis=1),
    )
    chip = chip.reshape(segments // 2, 2, -1)
    flags = lax.dynamic_index_in_dim(chip, parity, 1, keepdims=False).reshape(1, -1)

    chips = members // 2
    grouped = records.reshape(segments // 2, 2, -1, span)
    kept, handed = (
        lax.dynamic_index_in_dim(grouped, side, 1, keepdims=False).reshape(chips, -1, span)
        for side in (parity, 1 - parity)
    )
    pair = kept, exchange(handed, 1)
    chip_place = place % members // 2
    steps = [0] + balanced_steps(chips)
    arrived = {}
    for step in steps:
        block = jnp.stack([lax.dynamic_index_in_dim(p, chip_place ^ step, 0, False) for p in pair])
        arrived[step] = exchange(block, 2 * step) if step else block
    me = place.reshape(1)
    table = tables(samples, span)
    early, late = steps[: chips // 2], steps[chips // 2 :]
    before = transform(me, table, arrived, early, 0, COLUMN_TILES)[0]
    parts = []
    for first, last in ((0, FIRST_TILES), (FIRST_TILES, COLUMN_TILES)):
        own, other = transform(me, table, arrived, late, first, last, before)
        parts += [own, exchange(other, members)]
    white = whiten(flags, parts)

    far = devices // 8
    line = [white] + [exchange(white, 8 * k) for k in range(1, far)]
    halves = [(first, jnp.stack(line[first : first + far // 2])) for first in (far // 2, 0)]
    layout, blocks = [], []
    for near in range(0, 8, 2):
        came = [exchange(half, near) if near else half for _, half in halves]
        ways = [[8 * (first + k) + near for k in range(far // 2)] for first, _ in halves]
        if near != 2:
            came, ways = [jnp.concatenate(came)], [ways[0] + ways[1]]
        blocks += came
        layout += ways
    swapped = [exchange(block, 1) for block in blocks]
    ids = source_ids.reshape(-1, 1)
    common = me, weights, ids
    shape = segments, channels, devices
    before = correlate(0, *common, layout, blocks, shape)
    return correlate(1, *common, layout, swapped, shape, before, inverse_table(samples))


def solution(mesh):
    return jax.shard_map(
        per_device,
        mesh=mesh,
        in_specs=(P("group", None, "chan"), P("group", "chan"), P("group")),
        out_specs=P("group", "chan", None),
        check_vma=False,
    )
```

```python
import functools
import math

import jax
import jax.numpy as jnp
import ml_dtypes
import numpy as np
from jax import lax
from jax.experimental import pallas as pl
from jax.experimental.pallas import tpu as pltpu
from jax.sharding import PartitionSpec as P

BAND = 600
SOURCES = 64
HALF_LAG = 500

lowest_bin = 8
floor_share = 0.05
epsilon = 1e-06

PART = 640
WIDTH = 2 * PART
LAGS = 2 * HALF_LAG + 1
LAG_TILES = -(-LAGS // 128)
SHARES = 2
COLUMN_TILES = WIDTH // 128
FIRST_TILES = 6
FLAG_TILE = BAND // 128 * 128
FLAG_LANE = BAND - FLAG_TILE


def angles(phase, samples):
    step = np.float32(2.0 * math.pi / samples)
    return (phase.astype(np.float32) * step).astype(np.float64)


def cos_sin(samples):
    angle = angles(np.arange(samples), samples)
    return np.cos(angle).astype(np.float32), (-np.sin(angle)).astype(np.float32)


def lane_tiles(table):
    tiled = table.reshape(*table.shape[:-1], -1, 128)
    return np.ascontiguousarray(np.moveaxis(tiled, -2, -3))


@functools.lru_cache(maxsize=None)
def tables(samples, span):
    bins = lowest_bin + np.arange(BAND)
    cosine, sine = cos_sin(samples)
    phase = np.arange(samples)[:, None] * bins[None, :] % samples
    forward = np.zeros((samples, WIDTH), ml_dtypes.bfloat16)
    forward[:, :BAND] = cosine.astype(ml_dtypes.bfloat16)[phase]
    forward[:, PART : PART + BAND] = sine.astype(ml_dtypes.bfloat16)[phase]
    return lane_tiles(forward.reshape(-1, span, WIDTH)).reshape(-1, 128)


@functools.lru_cache(maxsize=None)
def inverse_table(samples):
    bins = lowest_bin + np.arange(BAND)
    cosine, sine = cos_sin(samples)
    factor = np.float32(1.0 / math.sqrt(BAND))
    phase = bins[:, None] * (np.arange(LAGS) - HALF_LAG)[None, :] % samples
    inverse = np.zeros((WIDTH, LAG_TILES * 128), ml_dtypes.bfloat16)
    inverse[:BAND, :LAGS] = (cosine * factor).astype(ml_dtypes.bfloat16)[phase]
    inverse[PART : PART + BAND, :LAGS] = (sine * factor).astype(ml_dtypes.bfloat16)[phase]
    return lane_tiles(inverse).reshape(-1, 128)


def balanced_steps(chips):
    steps = [chips - 1]
    for low in range(1, chips // 2):
        steps += [low, low ^ (chips - 1)]
    return steps


def transform_kernel(steps, first, started, place_ref, table_ref, *rest):
    records, rest = rest[: len(steps)], rest[len(steps) :]
    if started:
        before_ref, rest = rest[0], rest[1:]
    outs, (tiles_ref, sems) = rest[:-2], rest[-2:]
    _, rows, span = records[0].shape
    blocks, lines, _ = tiles_ref.shape
    columns = lines // span
    copies = []
    for index in range(blocks):
        sender = place_ref[0] ^ (2 * steps[index // 2] + index % 2)
        start = (sender * COLUMN_TILES + first) * span
        source = table_ref.at[pl.ds(pl.multiple_of(start, span), lines)]
        copies.append(pltpu.make_async_copy(source, tiles_ref.at[index], sems.at[index]))
        copies[-1].start()
    if started:
        total = before_ref[:, first * 128 : (first + columns) * 128]
    else:
        total = jnp.zeros((rows, columns * 128), jnp.float32)
    for index in range(blocks):
        copies[index].wait()
        tiles = [tiles_ref[index, tile * span : (tile + 1) * span] for tile in range(columns)]
        total += jnp.dot(
            records[index // 2][index % 2],
            jnp.concatenate(tiles, axis=1),
            preferred_element_type=jnp.float32,
        )
    if len(outs) == 1:
        outs[0][...] = total
    else:
        kept = rows // 2
        mine = place_ref[0] < table_ref.shape[0] // (2 * COLUMN_TILES * span)
        outs[0][...] = jnp.where(mine, total[:kept], total[kept:])
        outs[1][...] = jnp.where(mine, total[kept:], total[:kept])


def transform(place, table, arrived, steps, first, last, before=None):
    records = [arrived[step] for step in steps]
    _, rows, span = records[0].shape
    columns = last - first
    blocks = 2 * len(steps)
    vmem = pl.BlockSpec(memory_space=pltpu.VMEM)
    started = before is not None
    outs = 2 if started else 1
    return pl.pallas_call(
        functools.partial(transform_kernel, steps, first, started),
        in_specs=[
            pl.BlockSpec(memory_space=pltpu.SMEM),
            pl.BlockSpec(memory_space=pltpu.HBM),
        ]
        + [vmem] * (len(records) + started),
        out_specs=[vmem] * outs,
        out_shape=[jax.ShapeDtypeStruct((rows // outs, columns * 128), jnp.float32)] * outs,
        scratch_shapes=[
            pltpu.VMEM((blocks, columns * span, 128), jnp.bfloat16),
            pltpu.SemaphoreType.DMA((blocks,)),
        ],
        compiler_params=pltpu.CompilerParams(vmem_limit_bytes=24 * 2**20),
        cost_estimate=pl.CostEstimate(
            flops=2 * rows * blocks * span * columns * 128,
            bytes_accessed=2 * blocks * span * columns * 128,
            transcendentals=0,
        ),
        name="transform",
    )(place, table, *records, *([before] if started else []))


def whiten_kernel(flags_ref, *rest):
    parts, white_ref = rest[:-1], rest[-1]
    sums = []
    for first in range(0, len(parts), SHARES):
        sums.append(parts[first][...])
        for part in parts[first + 1 : first + SHARES]:
            sums[-1] += part[...]
    total = jnp.concatenate(sums, axis=1)
    real_part, imag_part = total[:, :PART], total[:, PART:]
    power = real_part * real_part + imag_part * imag_part
    level = jnp.sum(power, axis=1, keepdims=True) * (1.0 / BAND)
    factor = lax.rsqrt(power + floor_share * level + epsilon)
    white_ref[:, :PART] = (real_part * factor).astype(jnp.bfloat16)
    white_ref[:, PART:] = (imag_part * factor).astype(jnp.bfloat16)
    rows = total.shape[0]
    lane = lax.broadcasted_iota(jnp.int32, (rows, 128), 1)
    held = (lane >= FLAG_LANE) & (lane < FLAG_LANE + flags_ref.shape[1])
    tile = (real_part * factor)[:, FLAG_TILE : FLAG_TILE + 128]
    flags = jnp.concatenate(
        [
            jnp.zeros((1, FLAG_LANE), jnp.float32),
            flags_ref[...],
            jnp.zeros((1, 128 - FLAG_LANE - flags_ref.shape[1]), jnp.float32),
        ],
        axis=1,
    )
    white_ref[:, FLAG_TILE : FLAG_TILE + 128] = jnp.where(held, flags, tile).astype(jnp.bfloat16)


def whiten(flags, parts):
    return pl.pallas_call(
        whiten_kernel,
        out_shape=jax.ShapeDtypeStruct((parts[0].shape[0], WIDTH), jnp.bfloat16),
        compiler_params=pltpu.CompilerParams(vmem_limit_bytes=16 * 2**20),
        name="whiten",
    )(flags, *parts)


def correlate_kernel(shape, core, layout, place_ref, flags_ref, ids_ref, *rest):
    segments, channels, devices = shape
    blocks, rest = rest[: len(layout)], rest[len(layout) :]
    if core:
        before_ref, table_ref, out_ref = rest[:3]
        panel_ref, receivers_ref, inverse_ref, stacked_ref, sem = rest[3:]
        fetch = pltpu.make_async_copy(table_ref, inverse_ref, sem)
        fetch.start()
    else:
        out_ref, panel_ref, receivers_ref = rest
    rows = blocks[0].shape[1]
    members = devices // SHARES
    parts = members // segments
    ch_local = channels // devices
    ch_chip = 2 * ch_local
    place = place_ref[0]
    centre = place ^ core
    parity = centre % 2
    ids = ids_ref[...]
    sources = ids.shape[0]

    distances = [distance for ways in layout for distance in ways]
    places = [(index, line) for index, ways in enumerate(layout) for line in range(len(ways))]

    heads = [
        blocks[index][line, :16, FLAG_TILE : FLAG_TILE + 128] for index, line in places
    ]
    tails = jnp.concatenate(heads, axis=0)
    distance = (ids // ch_chip * 2 + parity) ^ centre
    slot = jnp.zeros_like(distance)
    for n, known in enumerate(distances):
        slot = jnp.where(distance == known, n, slot)
    column = lax.broadcasted_iota(jnp.int32, (sources, tails.shape[0]), 1)
    choice = (column == slot * 16).astype(jnp.bfloat16)
    tail = jnp.dot(choice, tails, preferred_element_type=jnp.float32)
    lane = lax.broadcasted_iota(jnp.int32, (sources, 128), 1)

    line = lax.broadcasted_iota(jnp.int32, (16, 1), 0)
    own = jnp.where(line < ch_local, place * ch_local + line, -1)
    wanted = jnp.concatenate([ids, own], axis=0)
    column = lax.broadcasted_iota(jnp.int32, (1, channels), 1)

    counts = [jnp.zeros((sources, 1), jnp.float32) for _ in range(ch_local)]
    numbers = []
    for g in range(segments // 2):
        chosen = [n for n, d in enumerate(distances) if d % members // 2 // parts == g]
        channel = column % rows
        for order, n in enumerate(chosen):
            device = centre ^ distances[n]
            base = device % members // 2 % parts * (SHARES * rows) + device // members * rows
            channel = jnp.where(column // rows == order, channel + base, channel)
        pick = (channel == wanted).astype(jnp.bfloat16)
        segment = jnp.concatenate([blocks[places[n][0]][places[n][1]] for n in chosen], axis=0)
        picked = jnp.dot(pick, segment, preferred_element_type=jnp.float32)
        number = (centre ^ distances[chosen[0]]) % members // 2 // parts
        numbers.append(2 * number + parity)
        mine = lane == FLAG_LANE + number * ch_chip + ids % ch_chip
        weight = jnp.sum(jnp.where(mine, tail, 0.0), axis=1, keepdims=True)
        panel_ref[g] = picked[:sources] * weight
        receivers_ref[g] = picked[sources:]
        for c in range(ch_local):
            counts[c] += weight * flags_ref[numbers[g], c]

    shares = [None] * ch_local
    for start in [FLAG_TILE] + [start for start in range(0, PART, 128) if start != FLAG_TILE]:
        re = slice(start, start + 128)
        im = slice(PART + start, PART + start + 128)
        for c in range(ch_local):
            real_sum = jnp.zeros((sources, 128), jnp.float32)
            imag_sum = jnp.zeros((sources, 128), jnp.float32)
            for g in range(segments // 2):
                flag = flags_ref[numbers[g], c]
                rec_real = receivers_ref[g, c : c + 1, re] * flag
                rec_imag = receivers_ref[g, c : c + 1, im] * flag
                src_real, src_imag = panel_ref[g, :, re], panel_ref[g, :, im]
                real_sum += src_real * rec_real + src_imag * rec_imag
                imag_sum += src_imag * rec_real - src_real * rec_imag
            if start == FLAG_TILE:
                real_sum = jnp.where(lane == FLAG_LANE, counts[c], real_sum)
            if not core:
                out_ref[c, :, re] = real_sum
                out_ref[c, :, im] = imag_sum
                continue
            real_sum += before_ref[c, :, re]
            imag_sum += before_ref[c, :, im]
            if start == FLAG_TILE:
                total = real_sum[:, FLAG_LANE : FLAG_LANE + 1]
                shares[c] = 1.0 / jnp.maximum(total, 1.0)
            lines = pl.ds(c, sources, stride=ch_local)
            stacked_ref[start // 128, lines, :] = real_sum * shares[c]
            stacked_ref[(PART + start) // 128, lines, :] = imag_sum * shares[c]
    if core:
        fetch.wait()
        tiles = [inverse_ref[tile * WIDTH : (tile + 1) * WIDTH] for tile in range(LAG_TILES)]
        lags = jnp.dot(
            jnp.concatenate([stacked_ref[i] for i in range(COLUMN_TILES)], axis=1).astype(
                jnp.bfloat16
            ),
            jnp.concatenate(tiles, axis=1),
            preferred_element_type=jnp.float32,
        )
        out_ref[...] = lags.reshape(sources, ch_local, LAG_TILES * 128)[:, :, :LAGS]


def correlate(core, place, weights, ids, layout, blocks, shape, before=None, table=None):
    segments, channels, devices = shape
    ch_local = channels // devices
    sources = ids.shape[0]
    smem = pl.BlockSpec(memory_space=pltpu.SMEM)
    vmem = pl.BlockSpec(memory_space=pltpu.VMEM)
    in_specs = [smem, smem, vmem] + [vmem] * len(blocks)
    scratch = [
        pltpu.VMEM((segments // 2, sources, WIDTH), jnp.float32),
        pltpu.VMEM((segments // 2, 16, WIDTH), jnp.float32),
    ]
    if core:
        in_specs += [vmem, pl.BlockSpec(memory_space=pltpu.HBM)]
        scratch += [
            pltpu.VMEM(table.shape, jnp.bfloat16),
            pltpu.VMEM((COLUMN_TILES, sources * ch_local, 128), jnp.float32),
            pltpu.SemaphoreType.DMA,
        ]
    out = (sources, ch_local, LAGS) if core else (ch_local, sources, WIDTH)
    return pl.pallas_call(
        functools.partial(correlate_kernel, shape, core, layout),
        in_specs=in_specs,
        out_specs=vmem,
        out_shape=jax.ShapeDtypeStruct(out, jnp.float32),
        scratch_shapes=scratch,
        compiler_params=pltpu.CompilerParams(vmem_limit_bytes=16 * 2**20),
        cost_estimate=pl.CostEstimate(
            flops=sources * channels * WIDTH * segments,
            bytes_accessed=2 * (segments // 2) * channels * WIDTH,
            transcendentals=0,
        ),
        name="correlate",
    )(place, weights, ids, *blocks, *([before, table] if core else []))


def per_device(records, valid_flags, source_ids):
    segments, channels, span = records.shape
    devices = lax.axis_size("chan")
    members = devices // SHARES
    samples = span * devices
    place = lax.axis_index("chan")
    weights = valid_flags.astype(jnp.float32)

    def exchange(block, bits):
        return lax.ppermute(block, "chan", [(i, i ^ bits) for i in range(devices)])

    parity = place % 2
    partner = exchange(weights, 1)
    chip = jnp.where(
        parity == 0,
        jnp.concatenate([weights, partner], axis=1),
        jnp.concatenate([partner, weights], axis=1),
    )
    chip = chip.reshape(segments // 2, 2, -1)
    flags = lax.dynamic_index_in_dim(chip, parity, 1, keepdims=False).reshape(1, -1)

    chips = members // 2
    grouped = records.reshape(segments // 2, 2, -1, span)
    kept, handed = (
        lax.dynamic_index_in_dim(grouped, side, 1, keepdims=False).reshape(chips, -1, span)
        for side in (parity, 1 - parity)
    )
    pair = kept, exchange(handed, 1)
    chip_place = place % members // 2
    steps = [0] + balanced_steps(chips)
    arrived = {}
    for step in steps:
        block = jnp.stack([lax.dynamic_index_in_dim(p, chip_place ^ step, 0, False) for p in pair])
        arrived[step] = exchange(block, 2 * step) if step else block
    me = place.reshape(1)
    table = tables(samples, span)
    early, late = steps[: chips // 2], steps[chips // 2 :]
    before = transform(me, table, arrived, early, 0, COLUMN_TILES)[0]
    parts = []
    for first, last in ((0, FIRST_TILES), (FIRST_TILES, COLUMN_TILES)):
        own, other = transform(me, table, arrived, late, first, last, before)
        parts += [own, exchange(other, members)]
    white = whiten(flags, parts)

    far = devices // 8
    line = [white] + [exchange(white, 8 * k) for k in range(1, far)]
    halves = [(first, jnp.stack(line[first : first + far // 2])) for first in (far // 2, 0)]
    layout, blocks = [], []
    for near in range(0, 8, 2):
        came = [exchange(half, near) if near else half for _, half in halves]
        ways = [[8 * (first + k) + near for k in range(far // 2)] for first, _ in halves]
        if near != 2:
            if near == 6:
                came, ways = came[::-1], ways[::-1]
            came, ways = [jnp.concatenate(came)], [ways[0] + ways[1]]
        blocks += came
        layout += ways
    swapped = [exchange(block, 1) for block in blocks]
    ids = source_ids.reshape(-1, 1)
    common = me, weights, ids
    shape = segments, channels, devices
    before = correlate(0, *common, layout, blocks, shape)
    return correlate(1, *common, layout, swapped, shape, before, inverse_table(samples))


def solution(mesh):
    return jax.shard_map(
        per_device,
        mesh=mesh,
        in_specs=(P("group", None, "chan"), P("group", "chan"), P("group")),
        out_specs=P("group", "chan", None),
        check_vma=False,
    )
```
